256 devices in a mesh: cap: 8 (over y, core), grp: 8 (over z), sub: 4 (over x).
Axes of the slice: x: 4, y: 4, z: 8, core: 2. Of those that a mesh axis runs over, the one named last changes fastest.
Arguments:
- right_side: float32 [3, 32, 64, 512], P(None, 'cap', 'grp', 'sub'), may hold values from -6 to 6
- viscosity: float32 [32, 64, 512], P('cap', 'grp', 'sub'), may hold values from 1 to 1000000
- coarse_basis: float32 [8, 8, 512, 512], P('cap', 'grp', 'sub'), may hold values from -0.5 to 0.5
- coarse_factor: float32 [8, 4, 1536, 1536], P('cap', 'sub', 'grp'), as said below
Outputs:
- velocity: float32 [3, 32, 64, 512], P(None, 'cap', 'grp', 'sub')
- pressure: float32 [32, 64, 512], P('cap', 'grp', 'sub')
The draws below stay inside these ranges and needn't reach their ends.
Inputs may be any that keep to these rules, and one draw needn't show every extreme that they name: Each block coarse_factor[a, s] is symmetric and positive definite.
All inputs are finite; a program needn't handle non-finite values.
Results may differ from the reference program's by a relative error of at most 0.0003.
Values sent between devices are 32-bit elements; how exact they have to be, the bound alone decides.
No kernel may reach another device: no remote copies, remote signals or barrier semaphores. Data moves between devices by JAX's collectives and lax.ppermute only.
A program may use at most 64 MiB of HBM per device.

```python
import math
import jax
import jax.numpy as jnp
from jax import lax

CX = 4
CY = 8
CZ = 128
KC = 1536
KB = 512
KRYLOV = 5
NEWTON = 2
CAP_BLOCKS = 8
GROUPS = 8
RADIAL_BLOCKS = 4
NX = 32
NY = 64
NZ = 512
N_CAP = 8
N_GRP = 8
N_SUB = 4


def draw_coarse_factor(key, part):
    key = jax.random.fold_in(key, 7)
    first_key, second_key = jax.random.split(key)
    shape = (CAP_BLOCKS, RADIAL_BLOCKS, KC, KC)
    diag_part = jax.random.uniform(first_key, (CAP_BLOCKS, RADIAL_BLOCKS, KC), jnp.float32, 1.0, 1.5)
    spread_part = jax.random.uniform(second_key, shape, jnp.float32, -1.0, 1.0) * (0.3 / KC ** 0.5)
    symmetric = spread_part + jnp.swapaxes(spread_part, -1, -2)
    identity = jnp.eye(KC, dtype=jnp.float32)
    return symmetric * (1.0 - identity) + identity * diag_part[..., None]


def block_levels(own_key, dims, cuts, low, top_value):
    factor_of = 1.0
    for dim, shards_of in cuts:
        steps = jax.random.uniform(jax.random.fold_in(jax.random.fold_in(own_key, 6), dim), (shards_of,), jnp.float32, low / len(cuts), top_value / len(cuts))
        factor_of = factor_of * jnp.repeat(jnp.exp(steps), dims[dim] // shards_of).reshape((-1,) + (1,) * (len(dims) - 1 - dim))
    return factor_of


def centred(stream_key, extent, scale, limit, shards=(), kind=jnp.bfloat16):
    values = scale * jax.random.normal(stream_key, extent, jnp.float32)
    if shards:
        values = values * block_levels(stream_key, extent, shards, -0.22, 0.18)
    return jnp.clip(values, -limit, limit).astype(kind)


def setup_inputs(seed: int = 0) -> dict:
    streams_of = jax.random.split(jax.random.key(seed), 5)
    return {
        "right_side": centred(streams_of[0], (3, NX, NY, NZ), 1.0, 6.0, ((1, 8), (2, 8), (3, 4)), jnp.float32),
        "viscosity": jnp.clip(jnp.exp(math.log(1000000) - 13.815511 * jax.random.uniform(streams_of[1], (NX, NY, NZ), jnp.float32) ** block_levels(streams_of[1], (NX, NY, NZ), ((0, 8), (1, 8), (2, 4)), -0.2, 0.2)), 1.0, 1000000),
        "coarse_basis": centred(streams_of[2], (CAP_BLOCKS, GROUPS, NZ, KB), CZ ** -0.5, 0.5, ((0, 8), (1, 8), (2, 4)), jnp.float32),
        "coarse_factor": draw_coarse_factor(jax.random.fold_in(streams_of[4], 71), 0),
    }


exact_mode = lax.Precision.HIGHEST


def stencil_faces(padded):
    centre = padded[1:-1, 1:-1, 1:-1]
    faces = (0.5 * (centre + padded[2:, 1:-1, 1:-1]), 0.5 * (centre + padded[:-2, 1:-1, 1:-1]),
             0.5 * (centre + padded[1:-1, 2:, 1:-1]), 0.5 * (centre + padded[1:-1, :-2, 1:-1]),
             0.5 * (centre + padded[1:-1, 1:-1, 2:]), 0.5 * (centre + padded[1:-1, 1:-1, :-2]))
    diagonal = 1.0 + faces[0] + faces[1] + faces[2] + faces[3] + faces[4] + faces[5]
    return faces, diagonal


def apply_stencil(padded_field, field, faces, diagonal):
    beside = faces[0] * padded_field[:, 2:, 1:-1, 1:-1] + faces[1] * padded_field[:, :-2, 1:-1, 1:-1]
    beside = beside + faces[2] * padded_field[:, 1:-1, 2:, 1:-1] + faces[3] * padded_field[:, 1:-1, :-2, 1:-1]
    beside = beside + faces[4] * padded_field[:, 1:-1, 1:-1, 2:] + faces[5] * padded_field[:, 1:-1, 1:-1, :-2]
    return diagonal * field - beside


def divergence_of(padded_field):
    result = 0.5 * (padded_field[0, 2:, 1:-1, 1:-1] - padded_field[0, :-2, 1:-1, 1:-1])
    result = result + 0.5 * (padded_field[1, 1:-1, 2:, 1:-1] - padded_field[1, 1:-1, :-2, 1:-1])
    return result + 0.5 * (padded_field[2, 1:-1, 1:-1, 2:] - padded_field[2, 1:-1, 1:-1, :-2])


def pad_field(field):
    return jnp.pad(field, ((0, 0), (1, 1), (1, 1), (1, 1)))


def reference(right_side, viscosity, coarse_basis, coarse_factor):
    basis_blocks = coarse_basis.reshape(N_CAP, N_GRP, N_SUB, CZ, KB)

    def precondition(residual, diagonal):
        blocks = residual.reshape(3, N_CAP, CX, N_GRP, CY, N_SUB, CZ)
        profile = jnp.mean(blocks, axis=(2, 4))
        local = jnp.einsum('pagsz,agszk->asgpk', profile, basis_blocks, precision=exact_mode)
        merged = jnp.sum(local, axis=2).reshape(N_CAP, N_SUB, KC)
        solved = jnp.einsum('asij,asj->asi', coarse_factor, merged, precision=exact_mode)
        solved = solved.reshape(N_CAP, N_SUB, 3, KB)
        spread = jnp.einsum('agszk,aspk->pagsz', basis_blocks, solved, precision=exact_mode)
        spread = jnp.broadcast_to(spread[:, :, None, :, None, :, :], (3, N_CAP, CX, N_GRP, CY, N_SUB, CZ))
        return residual / diagonal + spread.reshape(residual.shape)

    velocity = jnp.zeros_like(right_side)
    viscous = viscosity
    for newton_step in range(NEWTON):
        if newton_step > 0:
            viscous = viscosity / (1.0 + 25.0 * jnp.sum(velocity * velocity, axis=0))
        faces, diagonal = stencil_faces(jnp.pad(viscous, 1))

        def operate(field):
            return apply_stencil(pad_field(field), field, faces, diagonal)

        residual = right_side - operate(velocity)
        precond = precondition(residual, diagonal)
        norm_now = jnp.sum(residual * precond)
        direction = precond
        for krylov_step in range(KRYLOV):
            image = operate(direction)
            alpha = norm_now / jnp.sum(direction * image)
            velocity = velocity + alpha * direction
            residual = residual - alpha * image
            if krylov_step + 1 < KRYLOV:
                precond = precondition(residual, diagonal)
                fresh = jnp.sum(residual * precond)
                direction = precond + (fresh / norm_now) * direction
                norm_now = fresh
    pressure = -(viscous / (1.0 + viscous)) * divergence_of(pad_field(velocity))
    return velocity, pressure
```

```python
import functools

import jax
import jax.numpy as jnp
from jax import lax
from jax.experimental import pallas as pl
from jax.experimental.pallas import tpu as pltpu
from jax.sharding import PartitionSpec as P

S = 5
SLABS = 12
ROWS = 64
LANES = 128
GROUPS = 8
KB = 512
KC = 1536
SPAN = 2.6
FIELD = (SLABS, ROWS, LANES)
FACE = (3, ROWS, LANES)
EDGE = (ROWS, LANES)
GRAM = (24, LANES)
COEF = (8, 4, ROWS, LANES)
f32 = jnp.float32


def gram_row(i, j):
    i, j = min(i, j), max(i, j)
    return sum(min(t, S - 1) + 1 for t in range(j)) + i


def lane_ids():
    return lax.broadcasted_iota(jnp.int32, (ROWS, LANES), 1)


def row_ids():
    return lax.broadcasted_iota(jnp.int32, (ROWS, LANES), 0)


def along_z(w, halo, i, lanes):
    ends = pltpu.roll(halo, LANES - 1 - 2 * i, 1)
    after = pltpu.roll(jnp.where(lanes == 0, ends, w), LANES - 1, 1)
    before = pltpu.roll(jnp.where(lanes == LANES - 1, ends, w), 1, 1)
    return after, before


def flag(place, i):
    return jnp.full((ROWS, LANES), place[i], jnp.int32) == 1


def faces_of(place, near, far):
    odd, inner = flag(place, 0), flag(place, 1)
    far = jnp.where(inner, far, 0.0)
    return jnp.where(odd, near, far), jnp.where(odd, far, near)


def merge_edges(place, near, far):
    from_near = (lane_ids() + place[2]) % 2 == 1
    return jnp.where(from_near, near, jnp.where(flag(place, 3), far, 0.0))


def edge_of(get, count, lanes):
    edge = jnp.zeros((ROWS, LANES), f32)
    for i in range(count):
        moved = pltpu.roll(get(i), 2 * i + 1, 1)
        edge = jnp.where((lanes == 2 * i) | (lanes == 2 * i + 1), moved, edge)
    return edge


def store_coefs(coef, vis, low, high, halo):
    lanes, rows = lane_ids(), row_ids()
    for x in range(4):
        v = vis(x)
        up = vis(x + 1) if x < 3 else high
        down = vis(x - 1) if x else low
        yp = jnp.where(rows == ROWS - 1, 0.0, pltpu.roll(v, ROWS - 1, 0))
        ym = jnp.where(rows == 0, 0.0, pltpu.roll(v, 1, 0))
        zp, zm = along_z(v, halo, x, lanes)
        faces = [0.5 * (v + n) for n in (up, down, yp, ym, zp, zm)]
        diagonal = 1.0 + faces[0] + faces[1] + faces[2] + faces[3] + faces[4] + faces[5]
        faces[2] = jnp.where(rows == ROWS - 1, 0.0, faces[2])
        faces[3] = jnp.where(rows == 0, 0.0, faces[3])
        coef[0, x] = diagonal
        for f in range(6):
            coef[1 + f, x] = faces[f]
        coef[7, x] = 1.0 / diagonal


def stencil(coef, field, sides, halo, write):
    lanes = lane_ids()
    beyond = [sides(c) for c in range(3)]
    for x in range(4):
        for c in range(3):
            s = 4 * c + x
            w = field[s]
            up = field[s + 1] if x < 3 else beyond[c][1]
            down = field[s - 1] if x else beyond[c][0]
            yp, ym = pltpu.roll(w, ROWS - 1, 0), pltpu.roll(w, 1, 0)
            zp, zm = along_z(w, halo, s, lanes)
            beside = coef[1, x] * up + coef[2, x] * down
            beside = beside + coef[3, x] * yp + coef[4, x] * ym
            beside = beside + coef[5, x] * zp + coef[6, x] * zm
            write(c, x, coef[0, x] * w - beside)


def dot_rows(a, b):
    total = jnp.zeros((8, LANES), f32)
    for s in range(SLABS):
        total = total + jnp.sum((a[s] * b[s]).reshape(8, 8, LANES), axis=0)
    return jnp.sum(total, axis=0, keepdims=True)


def merge(u, gt, prof, mb):
    for c in range(3):
        total = u[4 * c] + u[4 * c + 1] + u[4 * c + 2] + u[4 * c + 3]
        prof[8 * c : 8 * c + 8] = jnp.sum(total.reshape(8, 8, LANES), axis=1) * (1.0 / 32.0)

    @pl.loop(0, KB // 32)
    def _(step):
        at = pl.multiple_of(step * 32, 32)
        for c in range(3):
            total = jnp.zeros((32, LANES), f32)
            for g in range(GROUPS):
                total = total + gt[g, pl.ds(at, 32), :] * prof[8 * c + g : 8 * c + g + 1, :]
            total = jnp.sum(total, axis=1, keepdims=True)
            mb[pl.ds(c * KB + at, 32), :] = jnp.broadcast_to(total, (32, LANES))


def solve(factor, mb, sb):
    def rows_of(step, totals):
        totals = list(totals)
        for part in range(4):
            at = pl.multiple_of(step * 32 + part * 8, 8)
            m = mb[pl.ds(at, 8), :]
            for q in range(KC // LANES):
                totals[q] = totals[q] + factor[pl.ds(at, 8), LANES * q : LANES * (q + 1)] * m
        return tuple(totals)

    zero = jnp.zeros((8, LANES), f32)
    totals = lax.fori_loop(0, KC // 32, rows_of, (zero,) * (KC // LANES))
    for q in range(KC // LANES):
        row = jnp.sum(totals[q], axis=0, keepdims=True)
        sb[LANES * q : LANES * (q + 1), :] = jnp.broadcast_to(row, (LANES, LANES)).T


def spread_over(gt, sb, spread):
    def spread_of(step, totals):
        totals = list(totals)
        for part in range(2):
            at = pl.multiple_of(step * 16 + part * 8, 8)
            solved = [sb[pl.ds(c * KB + at, 8), :] for c in range(3)]
            for g in range(GROUPS):
                b = gt[g, pl.ds(at, 8), :]
                for c in range(3):
                    totals[8 * c + g] = totals[8 * c + g] + b * solved[c]
        return tuple(totals)

    zero = jnp.zeros((8, LANES), f32)
    totals = lax.fori_loop(0, KB // 16, spread_of, (zero,) * 24)
    for r in range(24):
        spread[r : r + 1, :] = jnp.sum(totals[r], axis=0, keepdims=True)


def coarse(u, gt, factor, prof, mb, sb, spread):
    merge(u, gt, prof, mb)
    solve(factor, mb, sb)
    spread_over(gt, sb, spread)


def finish_direction(place, u, coef, spread, v, near, far, edge):
    for x in range(4):
        for c in range(3):
            s = 4 * c + x
            wide = jnp.broadcast_to(spread[8 * c : 8 * c + 8, :][:, None, :], (8, 8, LANES))
            v[s] = u[s] * coef[7, x] + wide.reshape(ROWS, LANES)
    for c in range(3):
        near[c] = v[4 * c + 3 - 3 * place[0]]
        far[c] = v[4 * c + 3 * place[0]]
    edge[...] = edge_of(lambda i: v[i], SLABS, lane_ids())


def basis_coefs(span, k):
    half = 0.5 * span
    if k == 0:
        return half, None, 1.0 / half
    return half, 0.5 * half, 2.0 / half


def start_kernel(place, fields, vnear, vfar, vedge_near, vedge_far, gt, factor_in,
                 coef, v, near, far, edge, gram, factor, prof, mb, sb, spread, arrived):
    fetch = pltpu.make_async_copy(factor_in, factor, arrived)
    fetch.start()
    low, high = faces_of(place, vnear[...], vfar[...])
    halo = merge_edges(place, vedge_near[...], vedge_far[...])
    store_coefs(coef, lambda x: fields[SLABS + x], low, high, halo)
    merge(fields, gt, prof, mb)
    fetch.wait()
    solve(factor, mb, sb)
    spread_over(gt, sb, spread)
    finish_direction(place, fields, coef, spread, v, near, far, edge)
    gram[...] = jnp.zeros(GRAM, f32)
    gram[0:1, :] = dot_rows(v, fields)


def image_kernel(place, v, near, far, edge_near, edge_far, coef, gram, image, sums):
    halo = merge_edges(place, edge_near[...], edge_far[...])

    def write(c, x, value):
        image[4 * c + x] = value

    stencil(coef, v, lambda c: faces_of(place, near[c], far[c]), halo, write)
    sums[...] = jnp.zeros((8, LANES), f32)
    sums[0:1, :] = gram[0:1, :]
    sums[1:2, :] = dot_rows(v, image)


def first_kernel(place, sums, image, u0, v0, coef, gram_in, gt, factor,
                 span, u, v, near, far, edge, gram, prof, mb, sb, spread):
    norm = jnp.sum(sums[0:1, :], axis=1, keepdims=True)
    curve = jnp.sum(sums[1:2, :], axis=1, keepdims=True)
    width = SPAN * curve / norm
    span[...] = jnp.broadcast_to(width, (8, LANES))
    shift, _, scale = basis_coefs(width, 0)
    for s in range(SLABS):
        u[s] = (image[s] - shift * u0[s]) * scale
    coarse(u, gt, factor, prof, mb, sb, spread)
    finish_direction(place, u, coef, spread, v, near, far, edge)
    gram[...] = gram_in[...]
    gram[1:2, :] = dot_rows(v0, u)
    gram[2:3, :] = dot_rows(v, u)


def next_residual(place, k, span, vk, near, far, edge_near, edge_far, coef, uk, uback, u):
    halo = merge_edges(place, edge_near[...], edge_far[...])
    shift, back, scale = basis_coefs(span[0:1, 0:1], k)

    def write(c, x, value):
        s = 4 * c + x
        value = value - shift * uk[s]
        if k:
            value = value - back * uback[s]
        u[s] = value * scale

    stencil(coef, vk, lambda c: faces_of(place, near[c], far[c]), halo, write)


def step_kernel(k, *refs):
    place, span, hnear, hfar, enear, efar, coef, gram_in, gt, factor, uk = refs[:11]
    refs = refs[11:]
    uback = None
    if k:
        uback, refs = refs[0], refs[1:]
    vs, refs = refs[: k + 1], refs[k + 1 :]
    u, v, near, far, edge, gram, prof, mb, sb, spread = refs
    next_residual(place, k, span, vs[k], hnear, hfar, enear, efar, coef, uk, uback, u)
    coarse(u, gt, factor, prof, mb, sb, spread)
    finish_direction(place, u, coef, spread, v, near, far, edge)
    gram[...] = gram_in[...]
    for i in range(k + 1):
        r = gram_row(i, k + 1)
        gram[r : r + 1, :] = dot_rows(vs[i], u)
    r = gram_row(k + 1, k + 1)
    gram[r : r + 1, :] = dot_rows(v, u)


def last_kernel(place, span, hnear, hfar, enear, efar, coef, gram_in, uk, uback,
                v0, v1, v2, v3, v4, gram, u):
    vs = (v0, v1, v2, v3, v4)
    next_residual(place, S - 1, span, v4, hnear, hfar, enear, efar, coef, uk, uback, u)
    gram[...] = gram_in[...]
    for i in range(S):
        r = gram_row(i, S)
        gram[r : r + 1, :] = dot_rows(vs[i], u)


def krylov_weights(span, sums):
    n = [[sums[gram_row(i, j) : gram_row(i, j) + 1, :] for j in range(S + 1)] for i in range(S)]
    half = 0.5 * span
    quarter = 0.5 * half

    def operate(p):
        out = [None] * (S + 1)

        def put(i, value):
            out[i] = value if out[i] is None else out[i] + value

        for j, w in enumerate(p):
            put(j, half * w)
            put(j + 1, (half if j == 0 else quarter) * w)
            if j:
                put(j - 1, quarter * w)
        return out[: len(p) + 1]

    def pair(a, b):
        total = None
        for i, ai in enumerate(a):
            part = None
            for j, bj in enumerate(b):
                term = n[i][j] * bj
                part = term if part is None else part + term
            total = ai * part if total is None else total + ai * part
        return total

    one = jnp.ones_like(span)
    r, p = [one], [one]
    x = []
    norm = n[0][0]
    for k in range(S):
        image = operate(p)
        alpha = norm / pair(p, image)
        for j, w in enumerate(p):
            if j < len(x):
                x[j] = x[j] + alpha * w
            else:
                x.append(alpha * w)
        r = [(r[j] - alpha * w) if j < len(r) else -(alpha * w) for j, w in enumerate(image)]
        if k + 1 < S:
            fresh = pair(r, r)
            beta = fresh / norm
            p = [r[j] + beta * p[j] if j < len(p) else r[j] for j in range(len(r))]
            norm = fresh
    return x


def weights_of(span, gram):
    sums = jnp.sum(gram[...], axis=1, keepdims=True)
    return krylov_weights(span[0:1, 0:1], sums)


def combine(x, parts, before=None):
    total = x[0] * parts[0]
    for j in range(1, S):
        total = total + x[j] * parts[j]
    return total if before is None else before + total


def restart_kernel(place, span, gram_in, fields, vnear, vfar, vedge_near, vedge_far, gt, factor,
                   v0, v1, v2, v3, v4, n0, n1, n2, n3, n4, f0, f1, f2, f3, f4,
                   en0, en1, en2, en3, en4, ef0, ef1, ef2, ef3, ef4,
                   vel, vel_low, vel_high, vel_edge, coef, u, v, near, far, edge, gram,
                   vis, prof, mb, sb, spread):
    x = weights_of(span, gram_in)
    vs = (v0, v1, v2, v3, v4)
    ns, fs = (n0, n1, n2, n3, n4), (f0, f1, f2, f3, f4)
    ens, efs = (en0, en1, en2, en3, en4), (ef0, ef1, ef2, ef3, ef4)
    for s in range(SLABS):
        vel[s] = combine(x, [t[s] for t in vs])
    for c in range(3):
        vel_low[c], vel_high[c] = faces_of(
            place, combine(x, [t[c] for t in ns]), combine(x, [t[c] for t in fs]))
    halo = merge_edges(
        place, combine(x, [t[...] for t in ens]), combine(x, [t[...] for t in efs]))
    vel_edge[...] = halo

    def thinned(viscosity, a, b, c):
        return viscosity / (1.0 + 25.0 * (a * a + b * b + c * c))

    for i in range(4):
        vis[i] = thinned(fields[SLABS + i], vel[i], vel[4 + i], vel[8 + i])
    vis_low, vis_high = faces_of(place, vnear[...], vfar[...])
    vis_low = thinned(vis_low, vel_low[0], vel_low[1], vel_low[2])
    vis_high = thinned(vis_high, vel_high[0], vel_high[1], vel_high[2])
    second = pltpu.roll(halo, LANES - 8, 1)
    third = pltpu.roll(halo, LANES - 16, 1)
    vis_halo = thinned(
        merge_edges(place, vedge_near[...], vedge_far[...]), halo, second, third)
    store_coefs(coef, lambda i: vis[i], vis_low, vis_high, vis_halo)

    def write(c, i, value):
        u[4 * c + i] = fields[4 * c + i] - value

    stencil(coef, vel, lambda c: (vel_low[c], vel_high[c]), halo, write)
    coarse(u, gt, factor, prof, mb, sb, spread)
    finish_direction(place, u, coef, spread, v, near, far, edge)
    gram[...] = jnp.zeros(GRAM, f32)
    gram[0:1, :] = dot_rows(v, u)


def end_kernel(place, span, gram_in, fields, vel_in, vel_low, vel_high, vel_edge,
               v0, v1, v2, v3, v4, n0, n1, n2, n3, n4, f0, f1, f2, f3, f4,
               en0, en1, en2, en3, en4, ef0, ef1, ef2, ef3, ef4,
               velocity, pressure, vel, press):
    lanes, rows = lane_ids(), row_ids()
    x = weights_of(span, gram_in)
    vs = (v0, v1, v2, v3, v4)
    ns, fs = (n0, n1, n2, n3, n4), (f0, f1, f2, f3, f4)
    ens, efs = (en0, en1, en2, en3, en4), (ef0, ef1, ef2, ef3, ef4)
    at = pl.multiple_of(place[4] * 8, 8)
    for s in range(SLABS):
        vel[s] = combine(x, [t[s] for t in vs], vel_in[s])
    low, high = faces_of(
        place, combine(x, [t[0] for t in ns]), combine(x, [t[0] for t in fs]))
    low, high = vel_low[0] + low, vel_high[0] + high
    halo = vel_edge[...] + merge_edges(
        place, combine(x, [t[...] for t in ens]), combine(x, [t[...] for t in efs]))
    for i in range(4):
        flow = vel_in[i] * vel_in[i] + vel_in[4 + i] * vel_in[4 + i] + vel_in[8 + i] * vel_in[8 + i]
        vis = fields[SLABS + i] / (1.0 + 25.0 * flow)
        up = vel[i + 1] if i < 3 else high
        down = vel[i - 1] if i else low
        w = vel[4 + i]
        yp = jnp.where(rows == ROWS - 1, 0.0, pltpu.roll(w, ROWS - 1, 0))
        ym = jnp.where(rows == 0, 0.0, pltpu.roll(w, 1, 0))
        zp, zm = along_z(vel[8 + i], halo, 8 + i, lanes)
        divergence = 0.5 * (up - down) + 0.5 * (yp - ym) + 0.5 * (zp - zm)
        press[i] = -(vis / (1.0 + vis)) * divergence
    for s in range(SLABS):
        velocity[s] = vel[s, pl.ds(at, 8), :]
    for i in range(4):
        pressure[i] = press[i, pl.ds(at, 8), :]


def call(kernel, outs, scratch, place, *args, far_away=None):
    vmem = pl.BlockSpec(memory_space=pltpu.VMEM)
    places = [pl.BlockSpec(memory_space=pltpu.SMEM)] + [vmem] * len(args)
    if far_away is not None:
        places[1 + far_away] = pl.BlockSpec(memory_space=pl.ANY)
    return pl.pallas_call(
        kernel,
        out_shape=[jax.ShapeDtypeStruct(o, f32) for o in outs],
        in_specs=places,
        out_specs=[vmem] * len(outs),
        scratch_shapes=[pltpu.VMEM(s, f32) if isinstance(s, tuple) else s for s in scratch],
        compiler_params=pltpu.CompilerParams(vmem_limit_bytes=20 * 2**20),
    )(place, *args)


COARSE_SCRATCH = ((24, LANES), (KC, LANES), (KC, LANES), (24, LANES))
DIRECTION = (FIELD, FACE, FACE, EDGE, GRAM)


def swap_near(value, axis):
    return lax.ppermute(value, axis, [(i, i ^ 1) for i in range(lax.axis_size(axis))])


def swap_far(value, axis):
    count = lax.axis_size(axis)
    pairs = [(i, (i + 1) % count) for i in range(1, count, 2)]
    return lax.ppermute(value, axis, pairs + [(b, a) for a, b in pairs])


def swapped(near, far, edge):
    return (
        swap_far(far, "cap"),
        swap_near(near, "cap"),
        swap_far(edge, "sub"),
        swap_near(edge, "sub"),
    )


def ordered(pieces):
    far_face, near_face, far_edge, near_edge = pieces
    return near_face, far_face, near_edge, far_edge


def summed(value):
    for axis in ("sub", "cap"):
        count = lax.axis_size(axis)
        pieces = [value] + [
            lax.ppermute(value, axis, [(i, i ^ d) for i in range(count)])
            for d in range(1, count)
        ]
        while len(pieces) > 1:
            pieces = [pieces[i] + pieces[i + 1] for i in range(0, len(pieces), 2)]
        value = pieces[0]
    return value


def body(right_side, viscosity, coarse_basis, coarse_factor):
    cap, sub = lax.axis_index("cap"), lax.axis_index("sub")
    caps, subs = lax.axis_size("cap"), lax.axis_size("sub")
    place = jnp.stack([
        cap % 2, (cap != 0) & (cap != caps - 1),
        sub % 2, (sub != 0) & (sub != subs - 1),
        lax.axis_index("grp"),
    ]).astype(jnp.int32)
    odd = cap % 2 == 1
    factor = lax.all_gather(coarse_factor[0, 0], "grp", axis=0, tiled=True)
    columns = []
    for x in range(4):
        columns += [viscosity[x, :, -1:], viscosity[x, :, :1]]
    own_edge = jnp.concatenate(columns + [jnp.zeros((8, LANES - 8), f32)], axis=1)
    first, last = viscosity[0], viscosity[3]
    halos = ordered(swapped(
        jnp.where(odd, first, last), jnp.where(odd, last, first), own_edge))
    packed = jnp.concatenate(
        [right_side.reshape(SLABS, 8, LANES), viscosity, jnp.stack(halos),
         coarse_basis[0, 0].T.reshape(KB // 8, 8, LANES)], axis=0)
    whole = lax.all_gather(packed, "grp", axis=0)
    spread_out = whole[:, :20].transpose(1, 0, 2, 3).reshape(20, ROWS, LANES)
    fields = spread_out[:16]
    vhalo = tuple(spread_out[16 + i] for i in range(4))
    gt = whole[:, 20:].reshape(GROUPS, KB, LANES)

    coef, v, near, far, edge, gram, factor = call(
        start_kernel, (COEF,) + DIRECTION + ((KC, KC),),
        COARSE_SCRATCH + (pltpu.SemaphoreType.DMA(()),),
        place, fields, *vhalo, gt, factor, far_away=6)
    u = fields
    span = None
    velocity = None
    for picard in range(2):
        us, vs, halos = [u], [v], []
        for k in range(S):
            halos.append(ordered(swapped(near, far, edge)))
            if k == 0 and picard == 0:
                image, sums = call(
                    image_kernel, (FIELD, (8, LANES)), (), place, v, *halos[0], coef, gram)
                span, u, v, near, far, edge, gram = call(
                    first_kernel, ((8, LANES), FIELD) + DIRECTION, COARSE_SCRATCH,
                    place, summed(sums), image, u, v, coef, gram, gt, factor)
            elif k + 1 < S:
                back = [us[k - 1]] if k else []
                u, v, near, far, edge, gram = call(
                    functools.partial(step_kernel, k), (FIELD,) + DIRECTION, COARSE_SCRATCH,
                    place, span, *halos[k], coef, gram, gt, factor, us[k], *back, *vs)
            else:
                (gram,) = call(
                    last_kernel, (GRAM,), (FIELD,),
                    place, span, *halos[k], coef, gram, us[k], us[k - 1], *vs)
                break
            us.append(u)
            vs.append(v)
        gram = summed(gram)
        kept = vs + [h[side] for side in range(4) for h in halos]
        if picard == 0:
            (*velocity, coef, u, v, near, far, edge, gram) = call(
                restart_kernel, (FIELD, FACE, FACE, EDGE, COEF, FIELD) + DIRECTION,
                ((4, ROWS, LANES),) + COARSE_SCRATCH,
                place, span, gram, fields, *vhalo, gt, factor, *kept)
        else:
            result, pressure = call(
                end_kernel, ((SLABS, 8, LANES), (4, 8, LANES)), (FIELD, (4, ROWS, LANES)),
                place, span, gram, fields, *velocity, *kept)
    return result.reshape(3, 4, 8, LANES), pressure


def solution(mesh):
    placed = (
        P(None, "cap", "grp", "sub"),
        P("cap", "grp", "sub"),
        P("cap", "grp", "sub", None),
        P("cap", "sub", "grp", None),
    )
    return jax.shard_map(
        body,
        mesh=mesh,
        in_specs=placed,
        out_specs=(P(None, "cap", "grp", "sub"), P("cap", "grp", "sub")),
        check_vma=False,
    )
```

```python
import functools

import jax
import jax.numpy as jnp
from jax import lax
from jax.experimental import pallas as pl
from jax.experimental.pallas import tpu as pltpu
from jax.sharding import PartitionSpec as P

S = 5
SLABS = 12
ROWS = 64
LANES = 128
GROUPS = 8
KB = 512
KC = 1536
SPAN = 2.6
FIELD = (SLABS, ROWS, LANES)
FACE = (3, ROWS, LANES)
EDGE = (ROWS, LANES)
GRAM = (24, LANES)
COEF = (8, 4, ROWS, LANES)
f32 = jnp.float32


def gram_row(i, j):
    i, j = min(i, j), max(i, j)
    return sum(min(t, S - 1) + 1 for t in range(j)) + i


def lane_ids():
    return lax.broadcasted_iota(jnp.int32, (ROWS, LANES), 1)


def row_ids():
    return lax.broadcasted_iota(jnp.int32, (ROWS, LANES), 0)


def along_z(w, halo, i, lanes):
    ends = pltpu.roll(halo, LANES - 1 - 2 * i, 1)
    after = pltpu.roll(jnp.where(lanes == 0, ends, w), LANES - 1, 1)
    before = pltpu.roll(jnp.where(lanes == LANES - 1, ends, w), 1, 1)
    return after, before


def flag(place, i):
    return jnp.full((ROWS, LANES), place[i], jnp.int32) == 1


def faces_of(place, near, far):
    odd, inner = flag(place, 0), flag(place, 1)
    far = jnp.where(inner, far, 0.0)
    return jnp.where(odd, near, far), jnp.where(odd, far, near)


def merge_edges(place, near, far):
    from_near = (lane_ids() + place[2]) % 2 == 1
    return jnp.where(from_near, near, jnp.where(flag(place, 3), far, 0.0))


def edge_of(get, count, lanes):
    edge = jnp.zeros((ROWS, LANES), f32)
    for i in range(count):
        moved = pltpu.roll(get(i), 2 * i + 1, 1)
        edge = jnp.where((lanes == 2 * i) | (lanes == 2 * i + 1), moved, edge)
    return edge


def store_coefs(coef, vis, low, high, halo):
    lanes, rows = lane_ids(), row_ids()
    for x in range(4):
        v = vis(x)
        up = vis(x + 1) if x < 3 else high
        down = vis(x - 1) if x else low
        yp = jnp.where(rows == ROWS - 1, 0.0, pltpu.roll(v, ROWS - 1, 0))
        ym = jnp.where(rows == 0, 0.0, pltpu.roll(v, 1, 0))
        zp, zm = along_z(v, halo, x, lanes)
        faces = [0.5 * (v + n) for n in (up, down, yp, ym, zp, zm)]
        diagonal = 1.0 + faces[0] + faces[1] + faces[2] + faces[3] + faces[4] + faces[5]
        faces[2] = jnp.where(rows == ROWS - 1, 0.0, faces[2])
        faces[3] = jnp.where(rows == 0, 0.0, faces[3])
        coef[0, x] = diagonal
        for f in range(6):
            coef[1 + f, x] = faces[f]
        coef[7, x] = 1.0 / diagonal


def stencil(coef, field, sides, halo, write):
    lanes = lane_ids()
    beyond = [sides(c) for c in range(3)]
    for x in range(4):
        for c in range(3):
            s = 4 * c + x
            w = field[s]
            up = field[s + 1] if x < 3 else beyond[c][1]
            down = field[s - 1] if x else beyond[c][0]
            yp, ym = pltpu.roll(w, ROWS - 1, 0), pltpu.roll(w, 1, 0)
            zp, zm = along_z(w, halo, s, lanes)
            beside = coef[1, x] * up + coef[2, x] * down
            beside = beside + coef[3, x] * yp + coef[4, x] * ym
            beside = beside + coef[5, x] * zp + coef[6, x] * zm
            write(c, x, coef[0, x] * w - beside)


def dot_rows(a, b):
    total = jnp.zeros((8, LANES), f32)
    for s in range(SLABS):
        total = total + jnp.sum((a[s] * b[s]).reshape(8, 8, LANES), axis=0)
    return jnp.sum(total, axis=0, keepdims=True)


def merge(u, gt, prof, mb):
    for c in range(3):
        total = u[4 * c] + u[4 * c + 1] + u[4 * c + 2] + u[4 * c + 3]
        prof[8 * c : 8 * c + 8] = jnp.sum(total.reshape(8, 8, LANES), axis=1) * (1.0 / 32.0)

    @pl.loop(0, KB // 32)
    def _(step):
        at = pl.multiple_of(step * 32, 32)
        for c in range(3):
            total = jnp.zeros((32, LANES), f32)
            for g in range(GROUPS):
                total = total + gt[g, pl.ds(at, 32), :] * prof[8 * c + g : 8 * c + g + 1, :]
            total = jnp.sum(total, axis=1, keepdims=True)
            mb[pl.ds(c * KB + at, 32), :] = jnp.broadcast_to(total, (32, LANES))


def solve(factor, mb, sb):
    def rows_of(step, totals):
        totals = list(totals)
        for part in range(4):
            at = pl.multiple_of(step * 32 + part * 8, 8)
            m = mb[pl.ds(at, 8), :]
            for q in range(KC // LANES):
                totals[q] = totals[q] + factor[pl.ds(at, 8), LANES * q : LANES * (q + 1)] * m
        return tuple(totals)

    zero = jnp.zeros((8, LANES), f32)
    totals = lax.fori_loop(0, KC // 32, rows_of, (zero,) * (KC // LANES))
    for q in range(KC // LANES):
        row = jnp.sum(totals[q], axis=0, keepdims=True)
        sb[LANES * q : LANES * (q + 1), :] = jnp.broadcast_to(row, (LANES, LANES)).T


def solve_own(own, mb, pay):
    def rows_of(step, totals):
        totals = list(totals)
        for part in range(8):
            at = pl.multiple_of(step * 64 + part * 8, 8)
            m = mb[pl.ds(at, 8), :]
            for q in range(2):
                r = 2 * (part % 4) + q
                totals[r] = totals[r] + own[pl.ds(at, 8), LANES * q : LANES * (q + 1)] * m
        return tuple(totals)

    zero = jnp.zeros((8, LANES), f32)
    t = lax.fori_loop(0, KC // 64, rows_of, (zero,) * 8)
    pay[0] = zero
    for q in range(2):
        total = (t[q] + t[2 + q]) + (t[4 + q] + t[6 + q])
        pay[0, q : q + 1, :] = jnp.sum(total, axis=0, keepdims=True)


def unpack(place, pays, sb):
    for d in range(GROUPS):
        at = (place[4] ^ d) * (KC // GROUPS)
        left = jnp.broadcast_to(pays[d][0, 0:1, :], (LANES, LANES)).T
        right = jnp.broadcast_to(pays[d][0, 1:2, :], (LANES, LANES)).T
        sb[pl.ds(pl.multiple_of(at, 64), LANES), :] = left
        sb[pl.ds(pl.multiple_of(at + LANES, 64), 64), :] = right[:64]


def spread_over(gt, sb, spread):
    def spread_of(step, totals):
        totals = list(totals)
        for part in range(2):
            at = pl.multiple_of(step * 16 + part * 8, 8)
            solved = [sb[pl.ds(c * KB + at, 8), :] for c in range(3)]
            for g in range(GROUPS):
                b = gt[g, pl.ds(at, 8), :]
                for c in range(3):
                    totals[8 * c + g] = totals[8 * c + g] + b * solved[c]
        return tuple(totals)

    zero = jnp.zeros((8, LANES), f32)
    totals = lax.fori_loop(0, KB // 16, spread_of, (zero,) * 24)
    for r in range(24):
        spread[r : r + 1, :] = jnp.sum(totals[r], axis=0, keepdims=True)


def coarse(u, gt, factor, prof, mb, sb, spread):
    merge(u, gt, prof, mb)
    solve(factor, mb, sb)
    spread_over(gt, sb, spread)


def finish_direction(place, u, coef, spread, v, near, far, edge):
    for x in range(4):
        for c in range(3):
            s = 4 * c + x
            wide = jnp.broadcast_to(spread[8 * c : 8 * c + 8, :][:, None, :], (8, 8, LANES))
            v[s] = u[s] * coef[7, x] + wide.reshape(ROWS, LANES)
    for c in range(3):
        near[c] = v[4 * c + 3 - 3 * place[0]]
        far[c] = v[4 * c + 3 * place[0]]
    edge[...] = edge_of(lambda i: v[i], SLABS, lane_ids())


def basis_coefs(span, k):
    half = 0.5 * span
    if k == 0:
        return half, None, 1.0 / half
    return half, 0.5 * half, 2.0 / half


def begin_kernel(place, whole, own, vhalos, fields, gt, pay, prof, mb, arrived):
    copies = []
    for g in range(GROUPS):
        copies.append(pltpu.make_async_copy(
            whole.at[g, pl.ds(0, 16)], fields.at[:, g], arrived.at[0, g]))
    for g in range(GROUPS):
        copies.append(pltpu.make_async_copy(
            whole.at[g, pl.ds(16, KB // 8)], gt.at[g], arrived.at[1, g]))
    for copy in copies:
        copy.start()
    for i in range(4):
        pay[1 + i] = vhalos[i]
    for copy in copies:
        copy.wait()
    flat = gt.reshape(GROUPS, KB, LANES)
    merge([fields[s].reshape(ROWS, LANES) for s in range(SLABS)], flat, prof, mb)
    solve_own(own, mb, pay)


def start_kernel(place, p0, p1, p2, p3, p4, p5, p6, p7, fields, gt,
                 coef, v, near, far, edge, gram, vh, sb, spread):
    pays = (p0, p1, p2, p3, p4, p5, p6, p7)
    unpack(place, pays, sb)
    for d in range(GROUPS):
        at = pl.multiple_of((place[4] ^ d) * 8, 8)
        for i in range(4):
            vh[i, pl.ds(at, 8), :] = pays[d][1 + i]
    low, high = faces_of(place, vh[0], vh[1])
    halo = merge_edges(place, vh[2], vh[3])
    store_coefs(coef, lambda x: fields[SLABS + x], low, high, halo)
    spread_over(gt, sb, spread)
    finish_direction(place, fields, coef, spread, v, near, far, edge)
    gram[...] = jnp.zeros(GRAM, f32)
    gram[0:1, :] = dot_rows(v, fields)


def image_kernel(place, v, near, far, edge_near, edge_far, coef, gram, image, sums):
    halo = merge_edges(place, edge_near[...], edge_far[...])

    def write(c, x, value):
        image[4 * c + x] = value

    stencil(coef, v, lambda c: faces_of(place, near[c], far[c]), halo, write)
    sums[...] = jnp.zeros((8, LANES), f32)
    sums[0:1, :] = gram[0:1, :]
    sums[1:2, :] = dot_rows(v, image)


def first_kernel(place, sums, image, u0, gt, own, span, u, pay, prof, mb):
    norm = jnp.sum(sums[0:1, :], axis=1, keepdims=True)
    curve = jnp.sum(sums[1:2, :], axis=1, keepdims=True)
    width = SPAN * curve / norm
    span[...] = jnp.broadcast_to(width, (8, LANES))
    shift, _, scale = basis_coefs(width, 0)
    for s in range(SLABS):
        u[s] = (image[s] - shift * u0[s]) * scale
    merge(u, gt, prof, mb)
    solve_own(own, mb, pay)


def residual_kernel(place, span, hnear, hfar, enear, efar, vk, coef, gt, own, uk, uback,
                    u, pay, prof, mb):
    next_residual(place, 1, span, vk, hnear, hfar, enear, efar, coef, uk, uback, u)
    merge(u, gt, prof, mb)
    solve_own(own, mb, pay)


def direction_kernel(place, p0, p1, p2, p3, p4, p5, p6, p7, gram_in, coef, gt, u, *refs):
    vs, (v, near, far, edge, gram, sb, spread) = refs[:-7], refs[-7:]
    unpack(place, (p0, p1, p2, p3, p4, p5, p6, p7), sb)
    spread_over(gt, sb, spread)
    finish_direction(place, u, coef, spread, v, near, far, edge)
    store_dots(gram, gram_in, vs, u, v)


def store_dots(gram, gram_in, vs, u, v=None):
    gram[...] = gram_in[...]
    for i, vi in enumerate(vs):
        r = gram_row(i, len(vs))
        gram[r : r + 1, :] = dot_rows(vi, u)
    if v is not None:
        r = gram_row(len(vs), len(vs))
        gram[r : r + 1, :] = dot_rows(v, u)


def next_residual(place, k, span, vk, near, far, edge_near, edge_far, coef, uk, uback, u):
    halo = merge_edges(place, edge_near[...], edge_far[...])
    shift, back, scale = basis_coefs(span[0:1, 0:1], k)

    def write(c, x, value):
        s = 4 * c + x
        value = value - shift * uk[s]
        if k:
            value = value - back * uback[s]
        u[s] = value * scale

    stencil(coef, vk, lambda c: faces_of(place, near[c], far[c]), halo, write)


def step_kernel(k, *refs):
    place, span, hnear, hfar, enear, efar, coef, gram_in, gt, factor, uk = refs[:11]
    refs = refs[11:]
    uback = None
    if k:
        uback, refs = refs[0], refs[1:]
    vs, refs = refs[: k + 1], refs[k + 1 :]
    u, v, near, far, edge, gram, prof, mb, sb, spread = refs
    next_residual(place, k, span, vs[k], hnear, hfar, enear, efar, coef, uk, uback, u)
    coarse(u, gt, factor, prof, mb, sb, spread)
    finish_direction(place, u, coef, spread, v, near, far, edge)
    store_dots(gram, gram_in, vs, u, v)


def last_kernel(place, span, hnear, hfar, enear, efar, coef, gram_in, uk, uback,
                v0, v1, v2, v3, v4, gram, u):
    vs = (v0, v1, v2, v3, v4)
    next_residual(place, S - 1, span, v4, hnear, hfar, enear, efar, coef, uk, uback, u)
    store_dots(gram, gram_in, vs, u)


def krylov_weights(span, sums):
    n = [[sums[gram_row(i, j) : gram_row(i, j) + 1, :] for j in range(S + 1)] for i in range(S)]
    half = 0.5 * span
    quarter = 0.5 * half

    def operate(p):
        out = [None] * (S + 1)

        def put(i, value):
            out[i] = value if out[i] is None else out[i] + value

        for j, w in enumerate(p):
            put(j, half * w)
            put(j + 1, (half if j == 0 else quarter) * w)
            if j:
                put(j - 1, quarter * w)
        return out[: len(p) + 1]

    def pair(a, b):
        total = None
        for i, ai in enumerate(a):
            part = None
            for j, bj in enumerate(b):
                term = n[i][j] * bj
                part = term if part is None else part + term
            total = ai * part if total is None else total + ai * part
        return total

    one = jnp.ones_like(span)
    r, p = [one], [one]
    x = []
    norm = n[0][0]
    for k in range(S):
        image = operate(p)
        alpha = norm / pair(p, image)
        for j, w in enumerate(p):
            if j < len(x):
                x[j] = x[j] + alpha * w
            else:
                x.append(alpha * w)
        r = [(r[j] - alpha * w) if j < len(r) else -(alpha * w) for j, w in enumerate(image)]
        if k + 1 < S:
            fresh = pair(r, r)
            beta = fresh / norm
            p = [r[j] + beta * p[j] if j < len(p) else r[j] for j in range(len(r))]
            norm = fresh
    return x


def weights_of(span, gram):
    sums = jnp.sum(gram[...], axis=1, keepdims=True)
    return krylov_weights(span[0:1, 0:1], sums)


def combine(x, parts, before=None):
    total = x[0] * parts[0]
    for j in range(1, S):
        total = total + x[j] * parts[j]
    return total if before is None else before + total


def restart_kernel(place, span, gram_in, fields, vh, gt, factor_in,
                   v0, v1, v2, v3, v4, n0, n1, n2, n3, n4, f0, f1, f2, f3, f4,
                   en0, en1, en2, en3, en4, ef0, ef1, ef2, ef3, ef4,
                   vel, vel_low, vel_high, vel_edge, coef, u, v, near, far, edge, gram, factor,
                   vis, prof, mb, sb, spread, arrived):
    fetch = pltpu.make_async_copy(factor_in, factor, arrived)
    fetch.start()
    x = weights_of(span, gram_in)
    vs = (v0, v1, v2, v3, v4)
    ns, fs = (n0, n1, n2, n3, n4), (f0, f1, f2, f3, f4)
    ens, efs = (en0, en1, en2, en3, en4), (ef0, ef1, ef2, ef3, ef4)
    for s in range(SLABS):
        vel[s] = combine(x, [t[s] for t in vs])
    for c in range(3):
        vel_low[c], vel_high[c] = faces_of(
            place, combine(x, [t[c] for t in ns]), combine(x, [t[c] for t in fs]))
    halo = merge_edges(
        place, combine(x, [t[...] for t in ens]), combine(x, [t[...] for t in efs]))
    vel_edge[...] = halo

    def thinned(viscosity, a, b, c):
        return viscosity / (1.0 + 25.0 * (a * a + b * b + c * c))

    for i in range(4):
        vis[i] = thinned(fields[SLABS + i], vel[i], vel[4 + i], vel[8 + i])
    vis_low, vis_high = faces_of(place, vh[0], vh[1])
    vis_low = thinned(vis_low, vel_low[0], vel_low[1], vel_low[2])
    vis_high = thinned(vis_high, vel_high[0], vel_high[1], vel_high[2])
    second = pltpu.roll(halo, LANES - 8, 1)
    third = pltpu.roll(halo, LANES - 16, 1)
    vis_halo = thinned(
        merge_edges(place, vh[2], vh[3]), halo, second, third)
    store_coefs(coef, lambda i: vis[i], vis_low, vis_high, vis_halo)

    def write(c, i, value):
        u[4 * c + i] = fields[4 * c + i] - value

    stencil(coef, vel, lambda c: (vel_low[c], vel_high[c]), halo, write)
    merge(u, gt, prof, mb)
    fetch.wait()
    solve(factor, mb, sb)
    spread_over(gt, sb, spread)
    finish_direction(place, u, coef, spread, v, near, far, edge)
    gram[...] = jnp.zeros(GRAM, f32)
    gram[0:1, :] = dot_rows(v, u)


def end_kernel(place, span, gram_in, fields, vel_in, vel_low, vel_high, vel_edge,
               v0, v1, v2, v3, v4, n0, n1, n2, n3, n4, f0, f1, f2, f3, f4,
               en0, en1, en2, en3, en4, ef0, ef1, ef2, ef3, ef4,
               velocity, pressure, vel, press):
    lanes, rows = lane_ids(), row_ids()
    x = weights_of(span, gram_in)
    vs = (v0, v1, v2, v3, v4)
    ns, fs = (n0, n1, n2, n3, n4), (f0, f1, f2, f3, f4)
    ens, efs = (en0, en1, en2, en3, en4), (ef0, ef1, ef2, ef3, ef4)
    at = pl.multiple_of(place[4] * 8, 8)
    for s in range(SLABS):
        vel[s] = combine(x, [t[s] for t in vs], vel_in[s])
    low, high = faces_of(
        place, combine(x, [t[0] for t in ns]), combine(x, [t[0] for t in fs]))
    low, high = vel_low[0] + low, vel_high[0] + high
    halo = vel_edge[...] + merge_edges(
        place, combine(x, [t[...] for t in ens]), combine(x, [t[...] for t in efs]))
    for i in range(4):
        flow = vel_in[i] * vel_in[i] + vel_in[4 + i] * vel_in[4 + i] + vel_in[8 + i] * vel_in[8 + i]
        vis = fields[SLABS + i] / (1.0 + 25.0 * flow)
        up = vel[i + 1] if i < 3 else high
        down = vel[i - 1] if i else low
        w = vel[4 + i]
        yp = jnp.where(rows == ROWS - 1, 0.0, pltpu.roll(w, ROWS - 1, 0))
        ym = jnp.where(rows == 0, 0.0, pltpu.roll(w, 1, 0))
        zp, zm = along_z(vel[8 + i], halo, 8 + i, lanes)
        divergence = 0.5 * (up - down) + 0.5 * (yp - ym) + 0.5 * (zp - zm)
        press[i] = -(vis / (1.0 + vis)) * divergence
    for s in range(SLABS):
        velocity[s] = vel[s, pl.ds(at, 8), :]
    for i in range(4):
        pressure[i] = press[i, pl.ds(at, 8), :]


def call(kernel, outs, scratch, place, *args, far_away=None, limit=20):
    vmem = pl.BlockSpec(memory_space=pltpu.VMEM)
    places = [pl.BlockSpec(memory_space=pltpu.SMEM)] + [vmem] * len(args)
    if far_away is not None:
        places[1 + far_away] = pl.BlockSpec(memory_space=pl.ANY)
    return pl.pallas_call(
        kernel,
        out_shape=[jax.ShapeDtypeStruct(o, f32) for o in outs],
        in_specs=places,
        out_specs=[vmem] * len(outs),
        scratch_shapes=[pltpu.VMEM(s, f32) if isinstance(s, tuple) else s for s in scratch],
        compiler_params=pltpu.CompilerParams(vmem_limit_bytes=limit * 2**20),
    )(place, *args)


MERGE = ((24, LANES), (KC, LANES))
SPREAD = ((KC, LANES), (24, LANES))
DIRECTION = (FIELD, FACE, FACE, EDGE, GRAM)


def swap_near(value, axis):
    return lax.ppermute(value, axis, [(i, i ^ 1) for i in range(lax.axis_size(axis))])


def swap_far(value, axis):
    count = lax.axis_size(axis)
    pairs = [(i, (i + 1) % count) for i in range(1, count, 2)]
    return lax.ppermute(value, axis, pairs + [(b, a) for a, b in pairs])


def swapped(near, far, edge):
    return (
        swap_far(far, "cap"),
        swap_near(near, "cap"),
        swap_far(edge, "sub"),
        swap_near(edge, "sub"),
    )


def ordered(pieces):
    far_face, near_face, far_edge, near_edge = pieces
    return near_face, far_face, near_edge, far_edge


def summed(value):
    for axis in ("sub", "cap"):
        count = lax.axis_size(axis)
        pieces = [value] + [
            lax.ppermute(value, axis, [(i, i ^ d) for i in range(count)])
            for d in range(1, count)
        ]
        while len(pieces) > 1:
            pieces = [pieces[i] + pieces[i + 1] for i in range(0, len(pieces), 2)]
        value = pieces[0]
    return value


def exchanged(pay):
    count = lax.axis_size("grp")
    return [pay] + [
        lax.ppermute(pay, "grp", [(i, i ^ d) for i in range(count)]) for d in range(1, count)
    ]


def body(right_side, viscosity, coarse_basis, coarse_factor):
    cap, sub = lax.axis_index("cap"), lax.axis_index("sub")
    caps, subs = lax.axis_size("cap"), lax.axis_size("sub")
    place = jnp.stack([
        cap % 2, (cap != 0) & (cap != caps - 1),
        sub % 2, (sub != 0) & (sub != subs - 1),
        lax.axis_index("grp"),
    ]).astype(jnp.int32)
    odd = cap % 2 == 1
    packed = jnp.concatenate(
        [right_side.reshape(SLABS, 8, LANES), viscosity,
         coarse_basis[0, 0].T.reshape(KB // 8, 8, LANES)], axis=0)
    whole = lax.all_gather(packed, "grp", axis=0)

    columns = []
    for x in range(4):
        columns += [viscosity[x, :, -1:], viscosity[x, :, :1]]
    own_edge = jnp.concatenate(columns + [jnp.zeros((8, LANES - 8), f32)], axis=1)
    first, last = viscosity[0], viscosity[3]
    vhalos = jnp.stack(ordered(swapped(
        jnp.where(odd, first, last), jnp.where(odd, last, first), own_edge)))
    vhalos, rows, _ = lax.optimization_barrier((vhalos, coarse_factor[0, 0], packed))
    factor = lax.all_gather(rows, "grp", axis=0, tiled=True)
    own = jnp.pad(coarse_factor[0, 0].T, ((0, 0), (0, 2 * LANES - KC // GROUPS)))

    fields, gt, pay = call(
        begin_kernel, ((16, 8, 8, LANES), (GROUPS, KB // 8, 8, LANES), (5, 8, LANES)),
        MERGE + (pltpu.SemaphoreType.DMA((2, GROUPS)),),
        place, whole, own, vhalos, far_away=0)
    fields = fields.reshape(16, ROWS, LANES)
    gt = gt.reshape(GROUPS, KB, LANES)
    coef, v, near, far, edge, gram, vh = call(
        start_kernel, (COEF,) + DIRECTION + ((4, ROWS, LANES),), SPREAD,
        place, *exchanged(pay), fields, gt)
    u = fields
    span = None
    velocity = None
    for picard in range(2):
        us, vs, halos = [u], [v], []
        for k in range(S):
            halos.append(ordered(swapped(near, far, edge)))
            if k + 1 == S:
                (gram,) = call(
                    last_kernel, (GRAM,), (FIELD,),
                    place, span, *halos[k], coef, gram, us[k], us[k - 1], *vs)
                break
            if picard == 0:
                if k == 0:
                    image, sums = call(
                        image_kernel, (FIELD, (8, LANES)), (), place, v, *halos[0], coef, gram)
                    span, u, pay = call(
                        first_kernel, ((8, LANES), FIELD, (1, 8, LANES)), MERGE,
                        place, summed(sums), image, us[0], gt, own)
                else:
                    u, pay = call(
                        residual_kernel, (FIELD, (1, 8, LANES)), MERGE,
                        place, span, *halos[k], vs[k], coef, gt, own, us[k], us[k - 1])
                v, near, far, edge, gram = call(
                    direction_kernel, DIRECTION, SPREAD,
                    place, *exchanged(pay), gram, coef, gt, u, *vs)
            else:
                back = [us[k - 1]] if k else []
                u, v, near, far, edge, gram = call(
                    functools.partial(step_kernel, k), (FIELD,) + DIRECTION, MERGE + SPREAD,
                    place, span, *halos[k], coef, gram, gt, factor, us[k], *back, *vs)
            us.append(u)
            vs.append(v)
        gram = summed(gram)
        kept = vs + [h[side] for side in range(4) for h in halos]
        if picard == 0:
            (*velocity, coef, u, v, near, far, edge, gram, factor) = call(
                restart_kernel,
                (FIELD, FACE, FACE, EDGE, COEF, FIELD) + DIRECTION + ((KC, KC),),
                ((4, ROWS, LANES),) + MERGE + SPREAD + (pltpu.SemaphoreType.DMA(()),),
                place, span, gram, fields, vh, gt, factor, *kept, far_away=5, limit=40)
        else:
            result, pressure = call(
                end_kernel, ((SLABS, 8, LANES), (4, 8, LANES)), (FIELD, (4, ROWS, LANES)),
                place, span, gram, fields, *velocity, *kept)
    return result.reshape(3, 4, 8, LANES), pressure


def solution(mesh):
    placed = (
        P(None, "cap", "grp", "sub"),
        P("cap", "grp", "sub"),
        P("cap", "grp", "sub", None),
        P("cap", "sub", "grp", None),
    )
    return jax.shard_map(
        body,
        mesh=mesh,
        in_specs=placed,
        out_specs=(P(None, "cap", "grp", "sub"), P("cap", "grp", "sub")),
        check_vma=False,
    )
```

```python
import functools

import jax
import jax.numpy as jnp
from jax import lax
from jax.experimental import pallas as pl
from jax.experimental.pallas import tpu as pltpu
from jax.sharding import PartitionSpec as P

S = 5
SLABS = 12
ROWS = 64
LANES = 128
GROUPS = 8
KB = 512
KC = 1536
SPAN = 2.6
FIELD = (SLABS, ROWS, LANES)
FACE = (3, ROWS, LANES)
EDGE = (ROWS, LANES)
GRAM = (24, LANES)
COEF = (8, 4, ROWS, LANES)
f32 = jnp.float32


def gram_row(i, j):
    i, j = min(i, j), max(i, j)
    return sum(min(t, S - 1) + 1 for t in range(j)) + i


def lane_ids():
    return lax.broadcasted_iota(jnp.int32, (ROWS, LANES), 1)


def row_ids():
    return lax.broadcasted_iota(jnp.int32, (ROWS, LANES), 0)


def along_z(w, halo, i, lanes):
    ends = pltpu.roll(halo, LANES - 1 - 2 * i, 1)
    after = pltpu.roll(jnp.where(lanes == 0, ends, w), LANES - 1, 1)
    before = pltpu.roll(jnp.where(lanes == LANES - 1, ends, w), 1, 1)
    return after, before


def flag(place, i):
    return jnp.full((ROWS, LANES), place[i], jnp.int32) == 1


def faces_of(place, near, far):
    odd, inner = flag(place, 0), flag(place, 1)
    far = jnp.where(inner, far, 0.0)
    return jnp.where(odd, near, far), jnp.where(odd, far, near)


def merge_edges(place, near, far):
    from_near = (lane_ids() + place[2]) % 2 == 1
    return jnp.where(from_near, near, jnp.where(flag(place, 3), far, 0.0))


def edge_of(get, count, lanes):
    edge = jnp.zeros((ROWS, LANES), f32)
    for i in range(count):
        moved = pltpu.roll(get(i), 2 * i + 1, 1)
        edge = jnp.where((lanes == 2 * i) | (lanes == 2 * i + 1), moved, edge)
    return edge


def store_coefs(coef, vis, low, high, halo):
    lanes, rows = lane_ids(), row_ids()
    for x in range(4):
        v = vis(x)
        up = vis(x + 1) if x < 3 else high
        down = vis(x - 1) if x else low
        yp = jnp.where(rows == ROWS - 1, 0.0, pltpu.roll(v, ROWS - 1, 0))
        ym = jnp.where(rows == 0, 0.0, pltpu.roll(v, 1, 0))
        zp, zm = along_z(v, halo, x, lanes)
        faces = [0.5 * (v + n) for n in (up, down, yp, ym, zp, zm)]
        diagonal = 1.0 + faces[0] + faces[1] + faces[2] + faces[3] + faces[4] + faces[5]
        faces[2] = jnp.where(rows == ROWS - 1, 0.0, faces[2])
        faces[3] = jnp.where(rows == 0, 0.0, faces[3])
        coef[0, x] = diagonal
        for f in range(6):
            coef[1 + f, x] = faces[f]
        coef[7, x] = 1.0 / diagonal


def stencil(coef, field, sides, halo, write):
    lanes = lane_ids()
    beyond = [sides(c) for c in range(3)]
    for x in range(4):
        for c in range(3):
            s = 4 * c + x
            w = field[s]
            up = field[s + 1] if x < 3 else beyond[c][1]
            down = field[s - 1] if x else beyond[c][0]
            yp, ym = pltpu.roll(w, ROWS - 1, 0), pltpu.roll(w, 1, 0)
            zp, zm = along_z(w, halo, s, lanes)
            beside = coef[1, x] * up + coef[2, x] * down
            beside = beside + coef[3, x] * yp + coef[4, x] * ym
            beside = beside + coef[5, x] * zp + coef[6, x] * zm
            write(c, x, coef[0, x] * w - beside)


def dot_rows(a, b):
    total = jnp.zeros((8, LANES), f32)
    for s in range(SLABS):
        total = total + jnp.sum((a[s] * b[s]).reshape(8, 8, LANES), axis=0)
    return jnp.sum(total, axis=0, keepdims=True)


def merge(u, gt, prof, mb):
    for c in range(3):
        total = u[4 * c] + u[4 * c + 1] + u[4 * c + 2] + u[4 * c + 3]
        prof[8 * c : 8 * c + 8] = jnp.sum(total.reshape(8, 8, LANES), axis=1) * (1.0 / 32.0)

    @pl.loop(0, KB // 32, unroll=4)
    def _(step):
        at = pl.multiple_of(step * 32, 32)
        totals = [jnp.zeros((32, LANES), f32)] * 3
        for g in range(GROUPS):
            b = gt[g, pl.ds(at, 32), :]
            for c in range(3):
                totals[c] = totals[c] + b * prof[8 * c + g : 8 * c + g + 1, :]
        for c in range(3):
            total = jnp.sum(totals[c], axis=1, keepdims=True)
            mb[pl.ds(c * KB + at, 32), :] = jnp.broadcast_to(total, (32, LANES))


def solve(factor, mb, sb):
    def rows_of(step, totals):
        totals = list(totals)
        for part in range(4):
            at = pl.multiple_of(step * 32 + part * 8, 8)
            m = mb[pl.ds(at, 8), :]
            for q in range(KC // LANES):
                totals[q] = totals[q] + factor[pl.ds(at, 8), LANES * q : LANES * (q + 1)] * m
        return tuple(totals)

    zero = jnp.zeros((8, LANES), f32)
    totals = lax.fori_loop(0, KC // 32, rows_of, (zero,) * (KC // LANES))
    for q in range(KC // LANES):
        row = jnp.sum(totals[q], axis=0, keepdims=True)
        sb[LANES * q : LANES * (q + 1), :] = jnp.broadcast_to(row, (LANES, LANES)).T


def solve_own(own, mb, pay):
    def rows_of(step, totals):
        totals = list(totals)
        for part in range(8):
            at = pl.multiple_of(step * 64 + part * 8, 8)
            m = mb[pl.ds(at, 8), :]
            for q in range(2):
                r = 2 * (part % 4) + q
                totals[r] = totals[r] + own[pl.ds(at, 8), LANES * q : LANES * (q + 1)] * m
        return tuple(totals)

    zero = jnp.zeros((8, LANES), f32)
    t = lax.fori_loop(0, KC // 64, rows_of, (zero,) * 8)
    pay[0] = zero
    for q in range(2):
        total = (t[q] + t[2 + q]) + (t[4 + q] + t[6 + q])
        pay[0, q : q + 1, :] = jnp.sum(total, axis=0, keepdims=True)


def unpack(pays, sb):
    for g in range(GROUPS):
        at = g * (KC // GROUPS)
        left = jnp.broadcast_to(pays[g, 0, 0:1, :], (LANES, LANES)).T
        right = jnp.broadcast_to(pays[g, 0, 1:2, :], (LANES, LANES)).T
        sb[at : at + LANES, :] = left
        sb[at + LANES : at + KC // GROUPS, :] = right[: KC // GROUPS - LANES]


def spread_over(gt, sb, spread):
    def spread_of(step, totals):
        totals = list(totals)
        for part in range(2):
            at = pl.multiple_of(step * 16 + part * 8, 8)
            solved = [sb[pl.ds(c * KB + at, 8), :] for c in range(3)]
            for g in range(GROUPS):
                b = gt[g, pl.ds(at, 8), :]
                for c in range(3):
                    totals[8 * c + g] = totals[8 * c + g] + b * solved[c]
        return tuple(totals)

    zero = jnp.zeros((8, LANES), f32)
    totals = lax.fori_loop(0, KB // 16, spread_of, (zero,) * 24)
    for r in range(24):
        spread[r : r + 1, :] = jnp.sum(totals[r], axis=0, keepdims=True)


def coarse(u, gt, factor, prof, mb, sb, spread):
    merge(u, gt, prof, mb)
    solve(factor, mb, sb)
    spread_over(gt, sb, spread)


def finish_direction(place, u, coef, spread, v, near, far, edge):
    for x in range(4):
        for c in range(3):
            s = 4 * c + x
            wide = jnp.broadcast_to(spread[8 * c : 8 * c + 8, :][:, None, :], (8, 8, LANES))
            v[s] = u[s] * coef[7, x] + wide.reshape(ROWS, LANES)
    for c in range(3):
        near[c] = v[4 * c + 3 - 3 * place[0]]
        far[c] = v[4 * c + 3 * place[0]]
    edge[...] = edge_of(lambda i: v[i], SLABS, lane_ids())


def basis_coefs(span, k):
    half = 0.5 * span
    if k == 0:
        return half, None, 1.0 / half
    return half, 0.5 * half, 2.0 / half


def begin_kernel(place, whole, own, vhalos, fields, gt, pay, prof, mb, arrived):
    copies = []
    for g in range(GROUPS):
        copies.append(pltpu.make_async_copy(
            whole.at[g, pl.ds(0, 16)], fields.at[:, g], arrived.at[0, g]))
    for g in range(GROUPS):
        copies.append(pltpu.make_async_copy(
            whole.at[g, pl.ds(16, KB // 8)], gt.at[g], arrived.at[1, g]))
    for copy in copies:
        copy.start()
    for i in range(4):
        pay[1 + i] = vhalos[i]
    for copy in copies:
        copy.wait()
    flat = gt.reshape(GROUPS, KB, LANES)
    merge([fields[s].reshape(ROWS, LANES) for s in range(SLABS)], flat, prof, mb)
    solve_own(own, mb, pay)


def start_kernel(place, pays, fields, gt,
                 coef, v, near, far, edge, gram, vh, sb, spread):
    unpack(pays, sb)
    for g in range(GROUPS):
        for i in range(4):
            vh[i, 8 * g : 8 * g + 8, :] = pays[g, 1 + i]
    low, high = faces_of(place, vh[0], vh[1])
    halo = merge_edges(place, vh[2], vh[3])
    store_coefs(coef, lambda x: fields[SLABS + x], low, high, halo)
    spread_over(gt, sb, spread)
    finish_direction(place, fields, coef, spread, v, near, far, edge)
    gram[...] = jnp.zeros(GRAM, f32)
    gram[0:1, :] = dot_rows(v, fields)


def image_kernel(place, v, near, far, edge_near, edge_far, coef, gram, image, sums):
    halo = merge_edges(place, edge_near[...], edge_far[...])

    def write(c, x, value):
        image[4 * c + x] = value

    stencil(coef, v, lambda c: faces_of(place, near[c], far[c]), halo, write)
    sums[...] = jnp.zeros((8, LANES), f32)
    sums[0:1, :] = gram[0:1, :]
    sums[1:2, :] = dot_rows(v, image)


def first_kernel(place, sums, image, u0, gt, own, span, u, pay, prof, mb):
    norm = jnp.sum(sums[0:1, :], axis=1, keepdims=True)
    curve = jnp.sum(sums[1:2, :], axis=1, keepdims=True)
    width = SPAN * curve / norm
    span[...] = jnp.broadcast_to(width, (8, LANES))
    shift, _, scale = basis_coefs(width, 0)
    for s in range(SLABS):
        u[s] = (image[s] - shift * u0[s]) * scale
    merge(u, gt, prof, mb)
    solve_own(own, mb, pay)


def residual_kernel(place, span, hnear, hfar, enear, efar, vk, coef, gt, own, uk, uback,
                    u, pay, prof, mb):
    next_residual(place, 1, span, vk, hnear, hfar, enear, efar, coef, uk, uback, u)
    merge(u, gt, prof, mb)
    solve_own(own, mb, pay)


def direction_kernel(place, pays, coef, gt, u, v, near, far, edge, sb, spread):
    unpack(pays, sb)
    spread_over(gt, sb, spread)
    finish_direction(place, u, coef, spread, v, near, far, edge)


def dots_kernel(place, gram_in, u, v, *refs):
    store_dots(refs[-1], gram_in, refs[:-1], u, v)


def store_dots(gram, gram_in, vs, u, v=None):
    gram[...] = gram_in[...]
    vs = list(vs) + ([] if v is None else [v])
    totals = [jnp.zeros((8, LANES), f32)] * len(vs)
    for s in range(SLABS):
        us = u[s]
        for i, vi in enumerate(vs):
            totals[i] = totals[i] + jnp.sum((vi[s] * us).reshape(8, 8, LANES), axis=0)
    level = len(vs) - (0 if v is None else 1)
    for i, total in enumerate(totals):
        r = gram_row(i, level)
        gram[r : r + 1, :] = jnp.sum(total, axis=0, keepdims=True)


def next_residual(place, k, span, vk, near, far, edge_near, edge_far, coef, uk, uback, u):
    halo = merge_edges(place, edge_near[...], edge_far[...])
    shift, back, scale = basis_coefs(span[0:1, 0:1], k)

    def write(c, x, value):
        s = 4 * c + x
        value = value - shift * uk[s]
        if k:
            value = value - back * uback[s]
        u[s] = value * scale

    stencil(coef, vk, lambda c: faces_of(place, near[c], far[c]), halo, write)


def step_kernel(k, place, span, hnear, hfar, enear, efar, vk, coef, gt, factor, uk, *refs):
    uback = None
    if k:
        uback, refs = refs[0], refs[1:]
    u, v, near, far, edge, prof, mb, sb, spread = refs
    next_residual(place, k, span, vk, hnear, hfar, enear, efar, coef, uk, uback, u)
    coarse(u, gt, factor, prof, mb, sb, spread)
    finish_direction(place, u, coef, spread, v, near, far, edge)


def last_kernel(place, span, hnear, hfar, enear, efar, coef, gram_in, uk, uback,
                v0, v1, v2, v3, v4, gram, u):
    vs = (v0, v1, v2, v3, v4)
    next_residual(place, S - 1, span, v4, hnear, hfar, enear, efar, coef, uk, uback, u)
    store_dots(gram, gram_in, vs, u)


def krylov_weights(span, sums):
    n = [[sums[gram_row(i, j) : gram_row(i, j) + 1, :] for j in range(S + 1)] for i in range(S)]
    half = 0.5 * span
    quarter = 0.5 * half

    def operate(p):
        out = [None] * (S + 1)

        def put(i, value):
            out[i] = value if out[i] is None else out[i] + value

        for j, w in enumerate(p):
            put(j, half * w)
            put(j + 1, (half if j == 0 else quarter) * w)
            if j:
                put(j - 1, quarter * w)
        return out[: len(p) + 1]

    def pair(a, b):
        total = None
        for i, ai in enumerate(a):
            part = None
            for j, bj in enumerate(b):
                term = n[i][j] * bj
                part = term if part is None else part + term
            total = ai * part if total is None else total + ai * part
        return total

    one = jnp.ones_like(span)
    r, p = [one], [one]
    x = []
    norm = n[0][0]
    for k in range(S):
        image = operate(p)
        alpha = norm / pair(p, image)
        for j, w in enumerate(p):
            if j < len(x):
                x[j] = x[j] + alpha * w
            else:
                x.append(alpha * w)
        r = [(r[j] - alpha * w) if j < len(r) else -(alpha * w) for j, w in enumerate(image)]
        if k + 1 < S:
            fresh = pair(r, r)
            beta = fresh / norm
            p = [r[j] + beta * p[j] if j < len(p) else r[j] for j in range(len(r))]
            norm = fresh
    return x


def weights_of(span, gram):
    sums = jnp.sum(gram[...], axis=1, keepdims=True)
    return krylov_weights(span[0:1, 0:1], sums)


def combine(x, parts, before=None):
    total = x[0] * parts[0]
    for j in range(1, S):
        total = total + x[j] * parts[j]
    return total if before is None else before + total


def restart_kernel(place, span, gram_in, fields, vh, gt, factor_in,
                   v0, v1, v2, v3, v4, n0, n1, n2, n3, n4, f0, f1, f2, f3, f4,
                   en0, en1, en2, en3, en4, ef0, ef1, ef2, ef3, ef4,
                   vel, vel_low, vel_high, vel_edge, coef, u, v, near, far, edge, gram, factor,
                   vis, prof, mb, sb, spread, arrived):
    fetch = pltpu.make_async_copy(factor_in, factor, arrived)
    fetch.start()
    x = weights_of(span, gram_in)
    vs = (v0, v1, v2, v3, v4)
    ns, fs = (n0, n1, n2, n3, n4), (f0, f1, f2, f3, f4)
    ens, efs = (en0, en1, en2, en3, en4), (ef0, ef1, ef2, ef3, ef4)
    for s in range(SLABS):
        vel[s] = combine(x, [t[s] for t in vs])
    for c in range(3):
        vel_low[c], vel_high[c] = faces_of(
            place, combine(x, [t[c] for t in ns]), combine(x, [t[c] for t in fs]))
    halo = merge_edges(
        place, combine(x, [t[...] for t in ens]), combine(x, [t[...] for t in efs]))
    vel_edge[...] = halo

    def thinned(viscosity, a, b, c):
        return viscosity / (1.0 + 25.0 * (a * a + b * b + c * c))

    for i in range(4):
        vis[i] = thinned(fields[SLABS + i], vel[i], vel[4 + i], vel[8 + i])
    vis_low, vis_high = faces_of(place, vh[0], vh[1])
    vis_low = thinned(vis_low, vel_low[0], vel_low[1], vel_low[2])
    vis_high = thinned(vis_high, vel_high[0], vel_high[1], vel_high[2])
    second = pltpu.roll(halo, LANES - 8, 1)
    third = pltpu.roll(halo, LANES - 16, 1)
    vis_halo = thinned(
        merge_edges(place, vh[2], vh[3]), halo, second, third)
    store_coefs(coef, lambda i: vis[i], vis_low, vis_high, vis_halo)

    def write(c, i, value):
        u[4 * c + i] = fields[4 * c + i] - value

    stencil(coef, vel, lambda c: (vel_low[c], vel_high[c]), halo, write)
    merge(u, gt, prof, mb)
    fetch.wait()
    solve(factor, mb, sb)
    spread_over(gt, sb, spread)
    finish_direction(place, u, coef, spread, v, near, far, edge)
    gram[...] = jnp.zeros(GRAM, f32)
    gram[0:1, :] = dot_rows(v, u)


def end_kernel(place, span, gram_in, fields, vel_in, vel_low, vel_high, vel_edge,
               v0, v1, v2, v3, v4, n0, n1, n2, n3, n4, f0, f1, f2, f3, f4,
               en0, en1, en2, en3, en4, ef0, ef1, ef2, ef3, ef4,
               velocity, pressure, vel, press):
    lanes, rows = lane_ids(), row_ids()
    x = weights_of(span, gram_in)
    vs = (v0, v1, v2, v3, v4)
    ns, fs = (n0, n1, n2, n3, n4), (f0, f1, f2, f3, f4)
    ens, efs = (en0, en1, en2, en3, en4), (ef0, ef1, ef2, ef3, ef4)
    at = pl.multiple_of(place[4] * 8, 8)
    for s in range(SLABS):
        vel[s] = combine(x, [t[s] for t in vs], vel_in[s])
    low, high = faces_of(
        place, combine(x, [t[0] for t in ns]), combine(x, [t[0] for t in fs]))
    low, high = vel_low[0] + low, vel_high[0] + high
    halo = vel_edge[...] + merge_edges(
        place, combine(x, [t[...] for t in ens]), combine(x, [t[...] for t in efs]))
    for i in range(4):
        flow = vel_in[i] * vel_in[i] + vel_in[4 + i] * vel_in[4 + i] + vel_in[8 + i] * vel_in[8 + i]
        vis = fields[SLABS + i] / (1.0 + 25.0 * flow)
        up = vel[i + 1] if i < 3 else high
        down = vel[i - 1] if i else low
        w = vel[4 + i]
        yp = jnp.where(rows == ROWS - 1, 0.0, pltpu.roll(w, ROWS - 1, 0))
        ym = jnp.where(rows == 0, 0.0, pltpu.roll(w, 1, 0))
        zp, zm = along_z(vel[8 + i], halo, 8 + i, lanes)
        divergence = 0.5 * (up - down) + 0.5 * (yp - ym) + 0.5 * (zp - zm)
        press[i] = -(vis / (1.0 + vis)) * divergence
    for s in range(SLABS):
        velocity[s] = vel[s, pl.ds(at, 8), :]
    for i in range(4):
        pressure[i] = press[i, pl.ds(at, 8), :]


def call(kernel, outs, scratch, place, *args, far_away=None, beside=False):
    vmem = pl.BlockSpec(memory_space=pltpu.VMEM)
    places = [pl.BlockSpec(memory_space=pltpu.SMEM)] + [vmem] * len(args)
    if far_away is not None:
        places[1 + far_away] = pl.BlockSpec(memory_space=pl.ANY)
    cost = None
    if beside:
        size = sum(a.size for a in args)
        cost = pl.CostEstimate(flops=2 * size, bytes_accessed=4 * size, transcendentals=0)
    return pl.pallas_call(
        kernel,
        out_shape=[jax.ShapeDtypeStruct(o, f32) for o in outs],
        in_specs=places,
        out_specs=[vmem] * len(outs),
        scratch_shapes=[pltpu.VMEM(s, f32) if isinstance(s, tuple) else s for s in scratch],
        cost_estimate=cost,
        compiler_params=pltpu.CompilerParams(vmem_limit_bytes=20 * 2**20),
    )(place, *args)


MERGE = ((24, LANES), (KC, LANES))
SPREAD = ((KC, LANES), (24, LANES))
DIRECTION = (FIELD, FACE, FACE, EDGE, GRAM)


def swap_near(value, axis):
    return lax.ppermute(value, axis, [(i, i ^ 1) for i in range(lax.axis_size(axis))])


def swap_far(value, axis):
    count = lax.axis_size(axis)
    pairs = [(i, (i + 1) % count) for i in range(1, count, 2)]
    return lax.ppermute(value, axis, pairs + [(b, a) for a, b in pairs])


def swapped(near, far, edge):
    return (
        swap_far(far, "cap"),
        swap_near(near, "cap"),
        swap_far(edge, "sub"),
        swap_near(edge, "sub"),
    )


def ordered(pieces):
    far_face, near_face, far_edge, near_edge = pieces
    return near_face, far_face, near_edge, far_edge


def summed(value):
    for axis in ("sub", "cap"):
        copies = jnp.broadcast_to(value[None], (lax.axis_size(axis),) + value.shape)
        value = jnp.sum(lax.all_to_all(copies, axis, 0, 0), axis=0)
    return value


def exchanged(pay):
    copies = jnp.broadcast_to(pay[None], (GROUPS,) + pay.shape)
    return lax.all_to_all(copies, "grp", 0, 0)


def body(right_side, viscosity, coarse_basis, coarse_factor):
    cap, sub = lax.axis_index("cap"), lax.axis_index("sub")
    caps, subs = lax.axis_size("cap"), lax.axis_size("sub")
    place = jnp.stack([
        cap % 2, (cap != 0) & (cap != caps - 1),
        sub % 2, (sub != 0) & (sub != subs - 1),
        lax.axis_index("grp"),
    ]).astype(jnp.int32)
    odd = cap % 2 == 1
    packed = jnp.concatenate(
        [right_side.reshape(SLABS, 8, LANES), viscosity,
         coarse_basis[0, 0].T.reshape(KB // 8, 8, LANES)], axis=0)
    whole = lax.all_gather(packed, "grp", axis=0)

    columns = []
    for x in range(4):
        columns += [viscosity[x, :, -1:], viscosity[x, :, :1]]
    own_edge = jnp.concatenate(columns + [jnp.zeros((8, LANES - 8), f32)], axis=1)
    first, last = viscosity[0], viscosity[3]
    vhalos = jnp.stack(ordered(swapped(
        jnp.where(odd, first, last), jnp.where(odd, last, first), own_edge)))
    vhalos, rows, _ = lax.optimization_barrier((vhalos, coarse_factor[0, 0], packed))
    factor = lax.all_gather(rows, "grp", axis=0, tiled=True)
    own = jnp.pad(coarse_factor[0, 0].T, ((0, 0), (0, 2 * LANES - KC // GROUPS)))

    fields, gt, pay = call(
        begin_kernel, ((16, 8, 8, LANES), (GROUPS, KB // 8, 8, LANES), (5, 8, LANES)),
        MERGE + (pltpu.SemaphoreType.DMA((2, GROUPS)),),
        place, whole, own, vhalos, far_away=0)
    fields = fields.reshape(16, ROWS, LANES)
    gt = gt.reshape(GROUPS, KB, LANES)
    coef, v, near, far, edge, gram, vh = call(
        start_kernel, (COEF,) + DIRECTION + ((4, ROWS, LANES),), SPREAD,
        place, exchanged(pay), fields, gt)
    u = fields
    span = None
    velocity = None
    for picard in range(2):
        us, vs, halos = [u], [v], []
        for k in range(S):
            beyond = ordered(swapped(near, far, edge))
            if k:
                (gram,) = call(dots_kernel, (GRAM,), (), place, gram, u, v, *vs[:-1], beside=True)
                beyond, gram = lax.optimization_barrier((beyond, gram))
            halos.append(beyond)
            if k + 1 == S:
                (gram,) = call(
                    last_kernel, (GRAM,), (FIELD,),
                    place, span, *halos[k], coef, gram, us[k], us[k - 1], *vs)
                break
            if picard == 0:
                if k == 0:
                    image, sums = call(
                        image_kernel, (FIELD, (8, LANES)), (), place, v, *halos[0], coef, gram)
                    span, u, pay = call(
                        first_kernel, ((8, LANES), FIELD, (1, 8, LANES)), MERGE,
                        place, summed(sums), image, us[0], gt, own)
                else:
                    u, pay = call(
                        residual_kernel, (FIELD, (1, 8, LANES)), MERGE,
                        place, span, *halos[k], vs[k], coef, gt, own, us[k], us[k - 1])
                v, near, far, edge = call(
                    direction_kernel, DIRECTION[:4], SPREAD,
                    place, exchanged(pay), coef, gt, u)
            else:
                back = [us[k - 1]] if k else []
                u, v, near, far, edge = call(
                    functools.partial(step_kernel, k), (FIELD,) + DIRECTION[:4], MERGE + SPREAD,
                    place, span, *halos[k], vs[k], coef, gt, factor, us[k], *back)
            us.append(u)
            vs.append(v)
        if picard == 0:
            gram, factor = lax.optimization_barrier((gram, factor))
        gram = summed(gram)
        kept = vs + [h[side] for side in range(4) for h in halos]
        if picard == 0:
            (*velocity, coef, u, v, near, far, edge, gram, factor) = call(
                restart_kernel,
                (FIELD, FACE, FACE, EDGE, COEF, FIELD) + DIRECTION + ((KC, KC),),
                ((4, ROWS, LANES),) + MERGE + SPREAD + (pltpu.SemaphoreType.DMA(()),),
                place, span, gram, fields, vh, gt, factor, *kept, far_away=5)
        else:
            result, pressure = call(
                end_kernel, ((SLABS, 8, LANES), (4, 8, LANES)), (FIELD, (4, ROWS, LANES)),
                place, span, gram, fields, *velocity, *kept)
    return result.reshape(3, 4, 8, LANES), pressure


def solution(mesh):
    placed = (
        P(None, "cap", "grp", "sub"),
        P("cap", "grp", "sub"),
        P("cap", "grp", "sub", None),
        P("cap", "sub", "grp", None),
    )
    return jax.shard_map(
        body,
        mesh=mesh,
        in_specs=placed,
        out_specs=(P(None, "cap", "grp", "sub"), P("cap", "grp", "sub")),
        check_vma=False,
    )
```

```python
import functools

import jax
import jax.numpy as jnp
from jax import lax
from jax.experimental import pallas as pl
from jax.experimental.pallas import tpu as pltpu
from jax.sharding import PartitionSpec as P

S = 5
SLABS = 12
ROWS = 64
LANES = 128
GROUPS = 8
KB = 512
KC = 1536
SPAN = 2.6
FIELD = (SLABS, ROWS, LANES)
FACE = (3, ROWS, LANES)
EDGE = (ROWS, LANES)
GRAM = (24, LANES)
PLACES = 32
FLOW = (22, ROWS, LANES)
COEF = (8, 4, ROWS, LANES)
f32 = jnp.float32


def gram_row(i, j):
    i, j = min(i, j), max(i, j)
    return sum(min(t, S - 1) + 1 for t in range(j)) + i


def lane_ids():
    return lax.broadcasted_iota(jnp.int32, (ROWS, LANES), 1)


def row_ids():
    return lax.broadcasted_iota(jnp.int32, (ROWS, LANES), 0)


def along_z(w, halo, i, lanes):
    ends = pltpu.roll(halo, LANES - 1 - 2 * i, 1)
    after = pltpu.roll(jnp.where(lanes == 0, ends, w), LANES - 1, 1)
    before = pltpu.roll(jnp.where(lanes == LANES - 1, ends, w), 1, 1)
    return after, before


def flag(place, i):
    return jnp.full((ROWS, LANES), place[i], jnp.int32) == 1


def faces_of(place, near, far):
    odd, inner = flag(place, 0), flag(place, 1)
    far = jnp.where(inner, far, 0.0)
    return jnp.where(odd, near, far), jnp.where(odd, far, near)


def merge_edges(place, near, far):
    from_near = (lane_ids() + place[2]) % 2 == 1
    return jnp.where(from_near, near, jnp.where(flag(place, 3), far, 0.0))


def edge_of(get, count, lanes):
    edge = jnp.zeros((ROWS, LANES), f32)
    for i in range(count):
        moved = pltpu.roll(get(i), 2 * i + 1, 1)
        edge = jnp.where((lanes == 2 * i) | (lanes == 2 * i + 1), moved, edge)
    return edge


def store_coefs(coef, vis, low, high, halo):
    lanes, rows = lane_ids(), row_ids()
    for x in range(4):
        v = vis(x)
        up = vis(x + 1) if x < 3 else high
        down = vis(x - 1) if x else low
        yp = jnp.where(rows == ROWS - 1, 0.0, pltpu.roll(v, ROWS - 1, 0))
        ym = jnp.where(rows == 0, 0.0, pltpu.roll(v, 1, 0))
        zp, zm = along_z(v, halo, x, lanes)
        faces = [0.5 * (v + n) for n in (up, down, yp, ym, zp, zm)]
        diagonal = 1.0 + faces[0] + faces[1] + faces[2] + faces[3] + faces[4] + faces[5]
        faces[2] = jnp.where(rows == ROWS - 1, 0.0, faces[2])
        faces[3] = jnp.where(rows == 0, 0.0, faces[3])
        coef[0, x] = diagonal
        for f in range(6):
            coef[1 + f, x] = faces[f]
        coef[7, x] = 1.0 / diagonal


def stencil(coef, field, sides, halo, write):
    lanes = lane_ids()
    beyond = [sides(c) for c in range(3)]
    for x in range(4):
        for c in range(3):
            s = 4 * c + x
            w = field[s]
            up = field[s + 1] if x < 3 else beyond[c][1]
            down = field[s - 1] if x else beyond[c][0]
            yp, ym = pltpu.roll(w, ROWS - 1, 0), pltpu.roll(w, 1, 0)
            zp, zm = along_z(w, halo, s, lanes)
            beside = coef[1, x] * up + coef[2, x] * down
            beside = beside + coef[3, x] * yp + coef[4, x] * ym
            beside = beside + coef[5, x] * zp + coef[6, x] * zm
            write(c, x, coef[0, x] * w - beside)


def dot_rows(a, b):
    total = jnp.zeros((8, LANES), f32)
    for s in range(SLABS):
        total = total + jnp.sum((a[s] * b[s]).reshape(8, 8, LANES), axis=0)
    return jnp.sum(total, axis=0, keepdims=True)


def merge(u, gt, prof, mb):
    for c in range(3):
        total = u[4 * c] + u[4 * c + 1] + u[4 * c + 2] + u[4 * c + 3]
        prof[8 * c : 8 * c + 8] = jnp.sum(total.reshape(8, 8, LANES), axis=1) * (1.0 / 32.0)

    @pl.loop(0, KB // 32, unroll=4)
    def _(step):
        at = pl.multiple_of(step * 32, 32)
        totals = [jnp.zeros((32, LANES), f32)] * 3
        for g in range(GROUPS):
            b = gt[g, pl.ds(at, 32), :]
            for c in range(3):
                totals[c] = totals[c] + b * prof[8 * c + g : 8 * c + g + 1, :]
        for c in range(3):
            total = jnp.sum(totals[c], axis=1, keepdims=True)
            mb[pl.ds(c * KB + at, 32), :] = jnp.broadcast_to(total, (32, LANES))


def solve(factor, mb, sb):
    def rows_of(step, totals):
        totals = list(totals)
        for part in range(4):
            at = pl.multiple_of(step * 32 + part * 8, 8)
            m = mb[pl.ds(at, 8), :]
            for q in range(KC // LANES):
                totals[q] = totals[q] + factor[pl.ds(at, 8), LANES * q : LANES * (q + 1)] * m
        return tuple(totals)

    zero = jnp.zeros((8, LANES), f32)
    totals = lax.fori_loop(0, KC // 32, rows_of, (zero,) * (KC // LANES))
    for q in range(KC // LANES):
        row = jnp.sum(totals[q], axis=0, keepdims=True)
        sb[LANES * q : LANES * (q + 1), :] = jnp.broadcast_to(row, (LANES, LANES)).T


def solve_own(own, mb, pay):
    def rows_of(step, totals):
        totals = list(totals)
        for part in range(8):
            at = pl.multiple_of(step * 64 + part * 8, 8)
            m = mb[pl.ds(at, 8), :]
            for q in range(2):
                r = 2 * (part % 4) + q
                totals[r] = totals[r] + own[pl.ds(at, 8), LANES * q : LANES * (q + 1)] * m
        return tuple(totals)

    zero = jnp.zeros((8, LANES), f32)
    t = lax.fori_loop(0, KC // 64, rows_of, (zero,) * 8)
    pay[0] = zero
    for q in range(2):
        total = (t[q] + t[2 + q]) + (t[4 + q] + t[6 + q])
        pay[0, q : q + 1, :] = jnp.sum(total, axis=0, keepdims=True)


def unpack(pays, sb):
    for g in range(GROUPS):
        at = g * (KC // GROUPS)
        left = jnp.broadcast_to(pays[g, 0, 0:1, :], (LANES, LANES)).T
        right = jnp.broadcast_to(pays[g, 0, 1:2, :], (LANES, LANES)).T
        sb[at : at + LANES, :] = left
        sb[at + LANES : at + KC // GROUPS, :] = right[: KC // GROUPS - LANES]


def spread_over(gt, sb, spread):
    def spread_of(step, totals):
        totals = list(totals)
        for part in range(2):
            at = pl.multiple_of(step * 16 + part * 8, 8)
            solved = [sb[pl.ds(c * KB + at, 8), :] for c in range(3)]
            for g in range(GROUPS):
                b = gt[g, pl.ds(at, 8), :]
                for c in range(3):
                    totals[8 * c + g] = totals[8 * c + g] + b * solved[c]
        return tuple(totals)

    zero = jnp.zeros((8, LANES), f32)
    totals = lax.fori_loop(0, KB // 16, spread_of, (zero,) * 24)
    for r in range(24):
        spread[r : r + 1, :] = jnp.sum(totals[r], axis=0, keepdims=True)


def coarse(u, gt, factor, prof, mb, sb, spread):
    merge(u, gt, prof, mb)
    solve(factor, mb, sb)
    spread_over(gt, sb, spread)


def finish_direction(place, u, coef, spread, v, near, far, edge):
    for x in range(4):
        for c in range(3):
            s = 4 * c + x
            wide = jnp.broadcast_to(spread[8 * c : 8 * c + 8, :][:, None, :], (8, 8, LANES))
            v[s] = u[s] * coef[7, x] + wide.reshape(ROWS, LANES)
    if near is not None:
        hand_over(place, v, near, far, edge)


def hand_over(place, v, near, far, edge):
    for c in range(3):
        near[c] = v[4 * c + 3 - 3 * place[0]]
        far[c] = v[4 * c + 3 * place[0]]
    edge[...] = edge_of(lambda i: v[i], SLABS, lane_ids())


def basis_coefs(span, k):
    half = 0.5 * span
    if k == 0:
        return half, None, 1.0 / half
    return half, 0.5 * half, 2.0 / half


def begin_kernel(place, whole, own, vhalos, fields, gt, pay, prof, mb, arrived):
    copies = []
    for g in range(GROUPS):
        copies.append(pltpu.make_async_copy(
            whole.at[g, pl.ds(0, 16)], fields.at[:, g], arrived.at[0, g]))
    for g in range(GROUPS):
        copies.append(pltpu.make_async_copy(
            whole.at[g, pl.ds(16, KB // 8)], gt.at[g], arrived.at[1, g]))
    for copy in copies:
        copy.start()
    for i in range(4):
        pay[1 + i] = vhalos[i]
    for copy in copies:
        copy.wait()
    flat = gt.reshape(GROUPS, KB, LANES)
    merge([fields[s].reshape(ROWS, LANES) for s in range(SLABS)], flat, prof, mb)
    solve_own(own, mb, pay)


def start_kernel(place, pays, fields, gt,
                 coef, v, near, far, edge, gram, vh, sb, spread):
    unpack(pays, sb)
    for g in range(GROUPS):
        for i in range(4):
            vh[i, 8 * g : 8 * g + 8, :] = pays[g, 1 + i]
    low, high = faces_of(place, vh[0], vh[1])
    halo = merge_edges(place, vh[2], vh[3])
    store_coefs(coef, lambda x: fields[SLABS + x], low, high, halo)
    spread_over(gt, sb, spread)
    finish_direction(place, fields, coef, spread, v, near, far, edge)
    gram[...] = jnp.zeros(GRAM, f32)
    gram[0:1, :] = dot_rows(v, fields)


def image_kernel(place, v, near, far, edge_near, edge_far, coef, gram, image, sums):
    halo = merge_edges(place, edge_near[...], edge_far[...])

    def write(c, x, value):
        image[4 * c + x] = value

    stencil(coef, v, lambda c: faces_of(place, near[c], far[c]), halo, write)
    sums[...] = jnp.zeros((8, LANES), f32)
    sums[0:1, :] = gram[0:1, :]
    sums[1:2, :] = dot_rows(v, image)


def merge_kernel(place, image, gt, own, pay, prof, mb):
    merge(image, gt, prof, mb)
    solve_own(own, mb, pay)


def carry_kernel(place, pay, s0, s1, s2, s3, copies):
    total = tree([s0[...], s1[...], s2[...], s3[...]])
    for g in range(GROUPS):
        copies[g, 0] = pay[0]
        copies[g, 1] = total


def first_kernel(place, pays, image, u0, v0, coef, gt,
                 span, u, v, near, far, edge, sb, spread):
    sums = jnp.sum(tree([pays[g, 1] for g in range(GROUPS)]), axis=1, keepdims=True)
    width = SPAN * sums[1:2, :] / sums[0:1, :]
    span[...] = jnp.broadcast_to(width, (8, LANES))
    shift, _, scale = basis_coefs(width, 0)
    unpack(pays, sb)
    spread_over(gt, sb, spread)
    finish_direction(place, image, coef, spread, v, None, None, None)
    for s in range(SLABS):
        u[s] = (image[s] - shift * u0[s]) * scale
        v[s] = (v[s] - shift * v0[s]) * scale
    hand_over(place, v, near, far, edge)


def residual_kernel(place, span, hnear, hfar, enear, efar, vk, coef, gt, own, uk, uback,
                    u, pay, prof, mb):
    next_residual(place, 1, span, vk, hnear, hfar, enear, efar, coef, uk, uback, u)
    merge(u, gt, prof, mb)
    solve_own(own, mb, pay)


def direction_kernel(place, pays, coef, gt, u, v, near, far, edge, sb, spread):
    unpack(pays, sb)
    spread_over(gt, sb, spread)
    finish_direction(place, u, coef, spread, v, near, far, edge)


def dots_kernel(place, gram_in, u, v, *refs):
    store_dots(refs[-1], gram_in, refs[:-1], u, v)


def tree(parts):
    while len(parts) > 1:
        parts = [parts[i] + parts[i + 1] for i in range(0, len(parts), 2)]
    return parts[0]


def pack_sums(gram, copies):
    sums = jnp.sum(gram[...], axis=1, keepdims=True)
    lanes = lax.broadcasted_iota(jnp.int32, (8, LANES), 1)
    tile = jnp.zeros((8, LANES), f32)
    for q in range(GRAM[0] // 8):
        tile = jnp.where(lanes == q, sums[8 * q : 8 * q + 8], tile)
    for i in range(PLACES):
        copies[i] = tile


def store_dots(gram, gram_in, vs, u, v=None):
    gram[...] = gram_in[...]
    vs = list(vs) + ([] if v is None else [v])
    totals = [jnp.zeros((8, LANES), f32)] * len(vs)
    for s in range(SLABS):
        us = u[s]
        for i, vi in enumerate(vs):
            totals[i] = totals[i] + jnp.sum((vi[s] * us).reshape(8, 8, LANES), axis=0)
    level = len(vs) - (0 if v is None else 1)
    for i, total in enumerate(totals):
        r = gram_row(i, level)
        gram[r : r + 1, :] = jnp.sum(total, axis=0, keepdims=True)


def next_residual(place, k, span, vk, near, far, edge_near, edge_far, coef, uk, uback, u):
    halo = merge_edges(place, edge_near[...], edge_far[...])
    shift, back, scale = basis_coefs(span[0:1, 0:1], k)

    def write(c, x, value):
        s = 4 * c + x
        value = value - shift * uk[s]
        if k:
            value = value - back * uback[s]
        u[s] = value * scale

    stencil(coef, vk, lambda c: faces_of(place, near[c], far[c]), halo, write)


def step_kernel(k, place, span, hnear, hfar, enear, efar, vk, coef, gt, factor, uk, *refs):
    uback = None
    if k:
        uback, refs = refs[0], refs[1:]
    u, v, near, far, edge, prof, mb, sb, spread = refs
    next_residual(place, k, span, vk, hnear, hfar, enear, efar, coef, uk, uback, u)
    coarse(u, gt, factor, prof, mb, sb, spread)
    finish_direction(place, u, coef, spread, v, near, far, edge)


def last_kernel(place, span, hnear, hfar, enear, efar, coef, gram_in, uk, uback,
                v0, v1, v2, v3, v4, copies, u, gram):
    vs = (v0, v1, v2, v3, v4)
    next_residual(place, S - 1, span, v4, hnear, hfar, enear, efar, coef, uk, uback, u)
    store_dots(gram, gram_in, vs, u)
    pack_sums(gram, copies)


def krylov_weights(span, sums):
    def product(i, j):
        r = gram_row(i, j)
        return sums[r // 8][r % 8 : r % 8 + 1, :]

    n = [[product(i, j) for j in range(S + 1)] for i in range(S)]
    half = 0.5 * span
    quarter = 0.5 * half

    def operate(p):
        out = [None] * (S + 1)

        def put(i, value):
            out[i] = value if out[i] is None else out[i] + value

        for j, w in enumerate(p):
            put(j, half * w)
            put(j + 1, (half if j == 0 else quarter) * w)
            if j:
                put(j - 1, quarter * w)
        return out[: len(p) + 1]

    def pair(a, b):
        total = None
        for i, ai in enumerate(a):
            part = None
            for j, bj in enumerate(b):
                term = n[i][j] * bj
                part = term if part is None else part + term
            total = ai * part if total is None else total + ai * part
        return total

    one = jnp.ones_like(span)
    r, p = [one], [one]
    x = []
    norm = n[0][0]
    for k in range(S):
        image = operate(p)
        alpha = norm / pair(p, image)
        for j, w in enumerate(p):
            if j < len(x):
                x[j] = x[j] + alpha * w
            else:
                x.append(alpha * w)
        r = [(r[j] - alpha * w) if j < len(r) else -(alpha * w) for j, w in enumerate(image)]
        if k + 1 < S:
            fresh = pair(r, r)
            beta = fresh / norm
            p = [r[j] + beta * p[j] if j < len(p) else r[j] for j in range(len(r))]
            norm = fresh
    return x


def weights_of(span, tiles):
    total = tree([tiles[i] for i in range(PLACES)])
    columns = [total[:, q : q + 1] for q in range(GRAM[0] // 8)]
    return krylov_weights(span[0:1, 0:1], columns)


def combine(x, parts, before=None):
    total = x[0] * parts[0]
    for j in range(1, S):
        total = total + x[j] * parts[j]
    return total if before is None else before + total


def combine_kernel(place, span, tiles, fields, vh,
                   v0, v1, v2, v3, v4, n0, n1, n2, n3, n4, f0, f1, f2, f3, f4,
                   en0, en1, en2, en3, en4, ef0, ef1, ef2, ef3, ef4,
                   flow, coef, u):
    x = weights_of(span, tiles)
    vs = (v0, v1, v2, v3, v4)
    ns, fs = (n0, n1, n2, n3, n4), (f0, f1, f2, f3, f4)
    ens, efs = (en0, en1, en2, en3, en4), (ef0, ef1, ef2, ef3, ef4)
    for s in range(SLABS):
        flow[s] = combine(x, [t[s] for t in vs])
    for c in range(3):
        flow[12 + c], flow[15 + c] = faces_of(
            place, combine(x, [t[c] for t in ns]), combine(x, [t[c] for t in fs]))
    halo = merge_edges(
        place, combine(x, [t[...] for t in ens]), combine(x, [t[...] for t in efs]))

    def thinned(viscosity, a, b, c):
        return viscosity / (1.0 + 25.0 * (a * a + b * b + c * c))

    for i in range(4):
        flow[18 + i] = thinned(fields[SLABS + i], flow[i], flow[4 + i], flow[8 + i])
    vis_low, vis_high = faces_of(place, vh[0], vh[1])
    vis_low = thinned(vis_low, flow[12], flow[13], flow[14])
    vis_high = thinned(vis_high, flow[15], flow[16], flow[17])
    second = pltpu.roll(halo, LANES - 8, 1)
    third = pltpu.roll(halo, LANES - 16, 1)
    vis_halo = thinned(merge_edges(place, vh[2], vh[3]), halo, second, third)
    store_coefs(coef, lambda i: flow[18 + i], vis_low, vis_high, vis_halo)

    def write(c, i, value):
        u[4 * c + i] = fields[4 * c + i] - value

    stencil(coef, flow, lambda c: (flow[12 + c], flow[15 + c]), halo, write)
    flow[13] = halo


def restart_kernel(place, u, coef, gt, factor_in, v, near, far, edge, gram, factor,
                   prof, mb, sb, spread, arrived):
    fetch = pltpu.make_async_copy(factor_in, factor, arrived)
    fetch.start()
    merge(u, gt, prof, mb)
    fetch.wait()
    solve(factor, mb, sb)
    spread_over(gt, sb, spread)
    finish_direction(place, u, coef, spread, v, near, far, edge)
    gram[...] = jnp.zeros(GRAM, f32)
    gram[0:1, :] = dot_rows(v, u)


def end_kernel(place, span, tiles, flow,
               v0, v1, v2, v3, v4, n0, n1, n2, n3, n4, f0, f1, f2, f3, f4,
               en0, en1, en2, en3, en4, ef0, ef1, ef2, ef3, ef4,
               velocity, pressure, vel, press):
    lanes, rows = lane_ids(), row_ids()
    x = weights_of(span, tiles)
    vs = (v0, v1, v2, v3, v4)
    ns, fs = (n0, n1, n2, n3, n4), (f0, f1, f2, f3, f4)
    ens, efs = (en0, en1, en2, en3, en4), (ef0, ef1, ef2, ef3, ef4)
    at = pl.multiple_of(place[4] * 8, 8)
    for s in range(SLABS):
        vel[s] = combine(x, [t[s] for t in vs], flow[s])
    low, high = faces_of(
        place, combine(x, [t[0] for t in ns]), combine(x, [t[0] for t in fs]))
    low, high = flow[12] + low, flow[15] + high
    halo = flow[13] + merge_edges(
        place, combine(x, [t[...] for t in ens]), combine(x, [t[...] for t in efs]))
    for i in range(4):
        vis = flow[18 + i]
        up = vel[i + 1] if i < 3 else high
        down = vel[i - 1] if i else low
        w = vel[4 + i]
        yp = jnp.where(rows == ROWS - 1, 0.0, pltpu.roll(w, ROWS - 1, 0))
        ym = jnp.where(rows == 0, 0.0, pltpu.roll(w, 1, 0))
        zp, zm = along_z(vel[8 + i], halo, 8 + i, lanes)
        divergence = 0.5 * (up - down) + 0.5 * (yp - ym) + 0.5 * (zp - zm)
        press[i] = -(vis / (1.0 + vis)) * divergence
    for s in range(SLABS):
        velocity[s] = vel[s, pl.ds(at, 8), :]
    for i in range(4):
        pressure[i] = press[i, pl.ds(at, 8), :]


def call(kernel, outs, scratch, place, *args, far_away=None, beside=False):
    vmem = pl.BlockSpec(memory_space=pltpu.VMEM)
    places = [pl.BlockSpec(memory_space=pltpu.SMEM)] + [vmem] * len(args)
    if far_away is not None:
        places[1 + far_away] = pl.BlockSpec(memory_space=pl.ANY)
    cost = None
    if beside:
        size = sum(a.size for a in args)
        cost = pl.CostEstimate(flops=2 * size, bytes_accessed=4 * size, transcendentals=0)
    return pl.pallas_call(
        kernel,
        out_shape=[jax.ShapeDtypeStruct(o, f32) for o in outs],
        in_specs=places,
        out_specs=[vmem] * len(outs),
        scratch_shapes=[pltpu.VMEM(s, f32) if isinstance(s, tuple) else s for s in scratch],
        cost_estimate=cost,
        compiler_params=pltpu.CompilerParams(vmem_limit_bytes=20 * 2**20),
    )(place, *args)


MERGE = ((24, LANES), (KC, LANES))
SPREAD = ((KC, LANES), (24, LANES))
DIRECTION = (FIELD, FACE, FACE, EDGE, GRAM)


def swap_near(value, axis):
    return lax.ppermute(value, axis, [(i, i ^ 1) for i in range(lax.axis_size(axis))])


def swap_far(value, axis):
    count = lax.axis_size(axis)
    pairs = [(i, (i + 1) % count) for i in range(1, count, 2)]
    return lax.ppermute(value, axis, pairs + [(b, a) for a, b in pairs])


def swapped(near, far, edge):
    return (
        swap_far(far, "cap"),
        swap_near(near, "cap"),
        swap_far(edge, "sub"),
        swap_near(edge, "sub"),
    )


def ordered(pieces):
    far_face, near_face, far_edge, near_edge = pieces
    return near_face, far_face, near_edge, far_edge


def shared(copies):
    return lax.all_to_all(copies, ("cap", "sub"), 0, 0)


def crossed(value, step):
    caps, groups, subs = (lax.axis_size(axis) for axis in ("cap", "grp", "sub"))

    def at(cap, grp, sub):
        return (cap * groups + grp) * subs + sub

    pairs = [
        (at(c ^ g, g, b ^ step), at(c, g, b))
        for c in range(caps) for g in range(groups) for b in range(subs)
    ]
    return lax.ppermute(value, ("cap", "grp", "sub"), pairs)


def exchanged(pay):
    copies = jnp.broadcast_to(pay[None], (GROUPS,) + pay.shape)
    return lax.all_to_all(copies, "grp", 0, 0)


def body(right_side, viscosity, coarse_basis, coarse_factor):
    cap, sub = lax.axis_index("cap"), lax.axis_index("sub")
    caps, subs = lax.axis_size("cap"), lax.axis_size("sub")
    place = jnp.stack([
        cap % 2, (cap != 0) & (cap != caps - 1),
        sub % 2, (sub != 0) & (sub != subs - 1),
        lax.axis_index("grp"),
    ]).astype(jnp.int32)
    odd = cap % 2 == 1
    packed = jnp.concatenate(
        [right_side.reshape(SLABS, 8, LANES), viscosity,
         coarse_basis[0, 0].T.reshape(KB // 8, 8, LANES)], axis=0)
    whole = lax.all_gather(packed, "grp", axis=0)

    columns = []
    for x in range(4):
        columns += [viscosity[x, :, -1:], viscosity[x, :, :1]]
    own_edge = jnp.concatenate(columns + [jnp.zeros((8, LANES - 8), f32)], axis=1)
    first, last = viscosity[0], viscosity[3]
    vhalos = jnp.stack(ordered(swapped(
        jnp.where(odd, first, last), jnp.where(odd, last, first), own_edge)))
    vhalos, rows, _ = lax.optimization_barrier((vhalos, coarse_factor[0, 0], packed))
    factor = lax.all_gather(rows, "grp", axis=0, tiled=True)
    own = jnp.pad(coarse_factor[0, 0].T, ((0, 0), (0, 2 * LANES - KC // GROUPS)))

    fields, gt, pay = call(
        begin_kernel, ((16, 8, 8, LANES), (GROUPS, KB // 8, 8, LANES), (5, 8, LANES)),
        MERGE + (pltpu.SemaphoreType.DMA((2, GROUPS)),),
        place, whole, own, vhalos, far_away=0)
    fields = fields.reshape(16, ROWS, LANES)
    gt = gt.reshape(GROUPS, KB, LANES)
    coef, v, near, far, edge, gram, vh = call(
        start_kernel, (COEF,) + DIRECTION + ((4, ROWS, LANES),), SPREAD,
        place, exchanged(pay), fields, gt)
    u = fields
    for picard in range(2):
        us, vs, halos = [u], [v], []
        for k in range(S):
            beyond = ordered(swapped(near, far, edge))
            if k:
                (gram,) = call(dots_kernel, (GRAM,), (), place, gram, u, v, *vs[:-1], beside=True)
                beyond, gram = lax.optimization_barrier((beyond, gram))
            halos.append(beyond)
            if k + 1 == S:
                (copies,) = call(
                    last_kernel, ((PLACES, 8, LANES),), (FIELD, GRAM),
                    place, span, *halos[k], coef, gram, us[k], us[k - 1], *vs)
                break
            if picard == 0 and k == 0:
                image, sums = call(
                    image_kernel, (FIELD, (8, LANES)), (), place, v, *halos[0], coef, gram)
                parts = [crossed(sums, step) for step in range(4)]
                (pay,) = call(
                    merge_kernel, ((1, 8, LANES),), MERGE, place, image, gt, own, beside=True)
                (pays,) = call(carry_kernel, ((GROUPS, 2, 8, LANES),), (), place, pay, *parts)
                span, u, v, near, far, edge = call(
                    first_kernel, ((8, LANES), FIELD) + DIRECTION[:4], SPREAD,
                    place, lax.all_to_all(pays, "grp", 0, 0), image, u, v, coef, gt)
            elif picard == 0:
                u, pay = call(
                    residual_kernel, (FIELD, (1, 8, LANES)), MERGE,
                    place, span, *halos[k], vs[k], coef, gt, own, us[k], us[k - 1])
                v, near, far, edge = call(
                    direction_kernel, DIRECTION[:4], SPREAD,
                    place, exchanged(pay), coef, gt, u)
            else:
                back = [us[k - 1]] if k else []
                u, v, near, far, edge = call(
                    functools.partial(step_kernel, k), (FIELD,) + DIRECTION[:4], MERGE + SPREAD,
                    place, span, *halos[k], vs[k], coef, gt, factor, us[k], *back)
            us.append(u)
            vs.append(v)
        tiles = shared(copies)
        kept = vs + [h[side] for side in range(4) for h in halos]
        if picard == 0:
            flow, coef, u = call(
                combine_kernel, (FLOW, COEF, FIELD), (), place, span, tiles, fields, vh, *kept)
            v, near, far, edge, gram, factor = call(
                restart_kernel, DIRECTION + ((KC, KC),),
                MERGE + SPREAD + (pltpu.SemaphoreType.DMA(()),),
                place, u, coef, gt, factor, far_away=3)
        else:
            result, pressure = call(
                end_kernel, ((SLABS, 8, LANES), (4, 8, LANES)), (FIELD, (4, ROWS, LANES)),
                place, span, tiles, flow, *kept)
    return result.reshape(3, 4, 8, LANES), pressure


def solution(mesh):
    placed = (
        P(None, "cap", "grp", "sub"),
        P("cap", "grp", "sub"),
        P("cap", "grp", "sub", None),
        P("cap", "sub", "grp", None),
    )
    return jax.shard_map(
        body,
        mesh=mesh,
        in_specs=placed,
        out_specs=(P(None, "cap", "grp", "sub"), P("cap", "grp", "sub")),
        check_vma=False,
    )
```

```python
import functools

import jax
import jax.numpy as jnp
from jax import lax
from jax.experimental import pallas as pl
from jax.experimental.pallas import tpu as pltpu
from jax.sharding import PartitionSpec as P

S = 5
SLABS = 12
ROWS = 64
LANES = 128
GROUPS = 8
KB = 512
KC = 1536
SPAN = 2.6
FIELD = (SLABS, ROWS, LANES)
FACE = (3, ROWS, LANES)
EDGE = (ROWS, LANES)
GRAM = (24, LANES)
PLACES = 32
FLOW = (22, ROWS, LANES)
COEF = (9, 4, ROWS, LANES)
f32 = jnp.float32


def gram_row(i, j):
    i, j = min(i, j), max(i, j)
    return sum(min(t, S - 1) + 1 for t in range(j)) + i


def lane_ids():
    return lax.broadcasted_iota(jnp.int32, (ROWS, LANES), 1)


def row_ids():
    return lax.broadcasted_iota(jnp.int32, (ROWS, LANES), 0)


def ends_of(halo, i):
    return pltpu.roll(halo, LANES - 1 - 2 * i, 1)


def along_z(w, halo, i, lanes):
    ends = ends_of(halo, i)
    after = jnp.where(lanes == LANES - 1, ends, pltpu.roll(w, LANES - 1, 1))
    before = jnp.where(lanes == 0, ends, pltpu.roll(w, 1, 1))
    return after, before


def flag(place, i):
    return jnp.full((ROWS, LANES), place[i], jnp.int32) == 1


def faces_of(place, near, far):
    odd, inner = flag(place, 0), flag(place, 1)
    far = jnp.where(inner, far, 0.0)
    return jnp.where(odd, near, far), jnp.where(odd, far, near)


def merge_edges(place, near, far):
    far = jnp.where(flag(place, 3), far, 0.0)
    odd = flag(place, 2)
    low, high = jnp.where(odd, near, far), jnp.where(odd, far, near)
    return jnp.where(lane_ids() % 2 == 1, pltpu.roll(low, 1, 1), pltpu.roll(high, LANES - 1, 1))


def edge_of(get, count, lanes):
    edge = jnp.zeros((ROWS, LANES), f32)
    for i in range(count):
        moved = pltpu.roll(get(i), 2 * i + 1, 1)
        edge = jnp.where((lanes == 2 * i) | (lanes == 2 * i + 1), moved, edge)
    return edge


def store_coefs(coef, vis, low, high, halo):
    lanes, rows = lane_ids(), row_ids()
    for x in range(4):
        v = vis(x)
        up = vis(x + 1) if x < 3 else high
        down = vis(x - 1) if x else low
        yp = jnp.where(rows == ROWS - 1, 0.0, pltpu.roll(v, ROWS - 1, 0))
        ym = jnp.where(rows == 0, 0.0, pltpu.roll(v, 1, 0))
        zp, zm = along_z(v, halo, x, lanes)
        faces = [0.5 * (v + n) for n in (up, down, yp, ym, zp, zm)]
        diagonal = 1.0 + faces[0] + faces[1] + faces[2] + faces[3] + faces[4] + faces[5]
        faces[2] = jnp.where(rows == ROWS - 1, 0.0, faces[2])
        faces[3] = jnp.where(rows == 0, 0.0, faces[3])
        first, last = lanes == 0, lanes == LANES - 1
        coef[8, x] = jnp.where(first, faces[5], jnp.where(last, faces[4], 0.0))
        faces[4] = jnp.where(last, 0.0, faces[4])
        faces[5] = jnp.where(first, 0.0, faces[5])
        coef[0, x] = diagonal
        for f in range(6):
            coef[1 + f, x] = faces[f]
        coef[7, x] = 1.0 / diagonal


def stencil_inside(coef, field, write):
    for x in range(4):
        for c in range(3):
            w = field[4 * c + x]
            beside = coef[3, x] * pltpu.roll(w, ROWS - 1, 0) + coef[4, x] * pltpu.roll(w, 1, 0)
            beside = beside + coef[5, x] * pltpu.roll(w, LANES - 1, 1)
            beside = beside + coef[6, x] * pltpu.roll(w, 1, 1)
            if x < 3:
                beside = beside + coef[1, x] * field[4 * c + x + 1]
            if x:
                beside = beside + coef[2, x] * field[4 * c + x - 1]
            write(c, x, coef[0, x] * w - beside)


def stencil_beyond(coef, sides, halo, write):
    for c in range(3):
        low, high = sides(c)
        for x in range(4):
            beside = coef[8, x] * ends_of(halo, 4 * c + x)
            if x == 0:
                beside = beside + coef[2, x] * low
            if x == 3:
                beside = beside + coef[1, x] * high
            write(c, x, beside)


def dot_rows(a, b):
    total = jnp.zeros((8, LANES), f32)
    for s in range(SLABS):
        total = total + jnp.sum((a[s] * b[s]).reshape(8, 8, LANES), axis=0)
    return jnp.sum(total, axis=0, keepdims=True)


def merge(u, gt, prof, mb):
    for c in range(3):
        total = u[4 * c] + u[4 * c + 1] + u[4 * c + 2] + u[4 * c + 3]
        prof[8 * c : 8 * c + 8] = jnp.sum(total.reshape(8, 8, LANES), axis=1) * (1.0 / 32.0)

    @pl.loop(0, KB // 32, unroll=4)
    def _(step):
        at = pl.multiple_of(step * 32, 32)
        totals = [jnp.zeros((32, LANES), f32)] * 3
        for g in range(GROUPS):
            b = gt[g, pl.ds(at, 32), :]
            for c in range(3):
                totals[c] = totals[c] + b * prof[8 * c + g : 8 * c + g + 1, :]
        for c in range(3):
            total = jnp.sum(totals[c], axis=1, keepdims=True)
            mb[pl.ds(c * KB + at, 32), :] = jnp.broadcast_to(total, (32, LANES))


def solve(factor, mb, sb):
    def rows_of(step, totals):
        totals = list(totals)
        for part in range(4):
            at = pl.multiple_of(step * 32 + part * 8, 8)
            m = mb[pl.ds(at, 8), :]
            for q in range(KC // LANES):
                totals[q] = totals[q] + factor[pl.ds(at, 8), LANES * q : LANES * (q + 1)] * m
        return tuple(totals)

    zero = jnp.zeros((8, LANES), f32)
    totals = lax.fori_loop(0, KC // 32, rows_of, (zero,) * (KC // LANES))
    for q in range(KC // LANES):
        row = jnp.sum(totals[q], axis=0, keepdims=True)
        sb[LANES * q : LANES * (q + 1), :] = jnp.broadcast_to(row, (LANES, LANES)).T


def solve_own(own, mb, pay):
    def rows_of(step, totals):
        totals = list(totals)
        for part in range(8):
            at = pl.multiple_of(step * 64 + part * 8, 8)
            m = mb[pl.ds(at, 8), :]
            for q in range(2):
                r = 2 * (part % 4) + q
                totals[r] = totals[r] + own[pl.ds(at, 8), LANES * q : LANES * (q + 1)] * m
        return tuple(totals)

    zero = jnp.zeros((8, LANES), f32)
    t = lax.fori_loop(0, KC // 64, rows_of, (zero,) * 8)
    pay[0] = zero
    for q in range(2):
        total = (t[q] + t[2 + q]) + (t[4 + q] + t[6 + q])
        pay[0, q : q + 1, :] = jnp.sum(total, axis=0, keepdims=True)


def unpack(pays, sb):
    for g in range(GROUPS):
        at = g * (KC // GROUPS)
        left = jnp.broadcast_to(pays[g, 0, 0:1, :], (LANES, LANES)).T
        right = jnp.broadcast_to(pays[g, 0, 1:2, :], (LANES, LANES)).T
        sb[at : at + LANES, :] = left
        sb[at + LANES : at + KC // GROUPS, :] = right[: KC // GROUPS - LANES]


def spread_over(gt, sb, spread):
    def spread_of(step, totals):
        totals = list(totals)
        for part in range(2):
            at = pl.multiple_of(step * 16 + part * 8, 8)
            solved = [sb[pl.ds(c * KB + at, 8), :] for c in range(3)]
            for g in range(GROUPS):
                b = gt[g, pl.ds(at, 8), :]
                for c in range(3):
                    totals[8 * c + g] = totals[8 * c + g] + b * solved[c]
        return tuple(totals)

    zero = jnp.zeros((8, LANES), f32)
    totals = lax.fori_loop(0, KB // 16, spread_of, (zero,) * 24)
    for r in range(24):
        spread[r : r + 1, :] = jnp.sum(totals[r], axis=0, keepdims=True)


def coarse(u, gt, factor, prof, mb, sb, spread):
    merge(u, gt, prof, mb)
    solve(factor, mb, sb)
    spread_over(gt, sb, spread)


def finish_direction(place, u, coef, spread, v, near, far, edge):
    for x in range(4):
        for c in range(3):
            s = 4 * c + x
            wide = jnp.broadcast_to(spread[8 * c : 8 * c + 8, :][:, None, :], (8, 8, LANES))
            v[s] = u[s] * coef[7, x] + wide.reshape(ROWS, LANES)
    if near is not None:
        hand_over(place, v, near, far, edge)


def hand_over(place, v, near, far, edge):
    for c in range(3):
        near[c] = v[4 * c + 3 - 3 * place[0]]
        far[c] = v[4 * c + 3 * place[0]]
    edge[...] = edge_of(lambda i: v[i], SLABS, lane_ids())


def basis_coefs(span, k):
    half = 0.5 * span
    if k == 0:
        return half, None, 1.0 / half
    return half, 0.5 * half, 2.0 / half


def local_kernel(place, force, viscosity, basis, copies):
    shares = []
    for c in range(3):
        total = force[4 * c] + force[4 * c + 1] + force[4 * c + 2] + force[4 * c + 3]
        row = jnp.sum(total, axis=0, keepdims=True) * (1.0 / 32.0)
        column = jnp.broadcast_to(row, (LANES, LANES)).T
        for q in range(KB // LANES):
            part = basis[:, LANES * q : LANES * (q + 1)] * column
            shares.append(jnp.sum(part, axis=0, keepdims=True))
    rows = lax.broadcasted_iota(jnp.int32, (8, LANES), 0)
    tiles = [force[s] for s in range(SLABS)] + [viscosity[x] for x in range(4)]
    for q in range(2):
        tile = jnp.zeros((8, LANES), f32)
        for r in range(8):
            if 8 * q + r < len(shares):
                tile = jnp.where(rows == r, shares[8 * q + r], tile)
        tiles.append(tile)
    for g in range(GROUPS):
        for i, tile in enumerate(tiles):
            copies[g, i] = tile


def begin_kernel(place, pays, own, vhalos, fields, copies, mb, pay):
    for q in range(2):
        total = tree([pays[g, 16 + q] for g in range(GROUPS)])
        for r in range(8):
            at = LANES * (8 * q + r)
            if at < KC:
                row = jnp.broadcast_to(total[r : r + 1, :], (LANES, LANES))
                mb[at : at + LANES, :] = row.T
    for g in range(GROUPS):
        for s in range(16):
            fields[s, 8 * g : 8 * g + 8, :] = pays[g, s]
    solve_own(own, mb, pay)
    for g in range(GROUPS):
        copies[g, 0] = pay[0]
        for i in range(4):
            copies[g, 1 + i] = vhalos[i]


def start_kernel(place, pays, fields, gt,
                 coef, v, near, far, edge, gram, vh, sb, spread):
    unpack(pays, sb)
    for g in range(GROUPS):
        for i in range(4):
            vh[i, 8 * g : 8 * g + 8, :] = pays[g, 1 + i]
    low, high = faces_of(place, vh[0], vh[1])
    halo = merge_edges(place, vh[2], vh[3])
    store_coefs(coef, lambda x: fields[SLABS + x], low, high, halo)
    spread_over(gt, sb, spread)
    finish_direction(place, fields, coef, spread, v, near, far, edge)
    gram[...] = jnp.zeros(GRAM, f32)
    gram[0:1, :] = dot_rows(v, fields)


def inside_kernel(place, v, coef, image):
    def write(c, x, value):
        image[4 * c + x] = value

    stencil_inside(coef, v, write)


def image_kernel(place, v, near, far, edge_near, edge_far, coef, gram, inside, image, sums):
    halo = merge_edges(place, edge_near[...], edge_far[...])

    def write(c, x, value):
        image[4 * c + x] = inside[4 * c + x] - value

    stencil_beyond(coef, lambda c: faces_of(place, near[c], far[c]), halo, write)
    sums[...] = jnp.zeros((8, LANES), f32)
    sums[0:1, :] = gram[0:1, :]
    sums[1:2, :] = dot_rows(v, image)


def merge_kernel(place, image, gt, own, pay, prof, mb):
    merge(image, gt, prof, mb)
    solve_own(own, mb, pay)


def carry_kernel(place, pay, s0, s1, s2, s3, copies):
    total = tree([s0[...], s1[...], s2[...], s3[...]])
    for g in range(GROUPS):
        copies[g, 0] = pay[0]
        copies[g, 1] = total


def first_kernel(place, pays, image, u0, v0, coef, gt,
                 span, u, v, near, far, edge, sb, spread):
    sums = jnp.sum(tree([pays[g, 1] for g in range(GROUPS)]), axis=1, keepdims=True)
    width = SPAN * sums[1:2, :] / sums[0:1, :]
    span[...] = jnp.broadcast_to(width, (8, LANES))
    shift, _, scale = basis_coefs(width, 0)
    unpack(pays, sb)
    spread_over(gt, sb, spread)
    finish_direction(place, image, coef, spread, v, None, None, None)
    for s in range(SLABS):
        u[s] = (image[s] - shift * u0[s]) * scale
        v[s] = (v[s] - shift * v0[s]) * scale
    hand_over(place, v, near, far, edge)


def residual_kernel(place, span, hnear, hfar, enear, efar, coef, inside, gt, own,
                    u, pay, prof, mb):
    next_residual(place, False, span, hnear, hfar, enear, efar, coef, inside, u)
    merge(u, gt, prof, mb)
    solve_own(own, mb, pay)


def direction_kernel(place, pays, coef, gt, u, v, near, far, edge, sb, spread):
    unpack(pays, sb)
    spread_over(gt, sb, spread)
    finish_direction(place, u, coef, spread, v, near, far, edge)


def beside_kernel(k, place, span, gram_in, coef, *refs):
    refs, (gram, inside) = refs[:-2], refs[-2:]
    vs, us = refs[: k + 1], refs[k + 1 :]
    uk = us[0]
    if k:
        store_dots(gram, gram_in, vs[:-1], uk, vs[-1])
    else:
        gram[...] = gram_in[...]
    shift, back, scale = basis_coefs(span[0:1, 0:1], k)

    def write(c, x, value):
        s = 4 * c + x
        value = value - shift * uk[s]
        if k:
            value = value - back * us[1][s]
        inside[s] = value * scale

    stencil_inside(coef, vs[-1], write)


def tree(parts):
    while len(parts) > 1:
        parts = [parts[i] + parts[i + 1] for i in range(0, len(parts), 2)]
    return parts[0]


def pack_sums(gram, copies):
    sums = jnp.sum(gram[...], axis=1, keepdims=True)
    lanes = lax.broadcasted_iota(jnp.int32, (8, LANES), 1)
    tile = jnp.zeros((8, LANES), f32)
    for q in range(GRAM[0] // 8):
        tile = jnp.where(lanes == q, sums[8 * q : 8 * q + 8], tile)
    for i in range(PLACES):
        copies[i] = tile


def store_dots(gram, gram_in, vs, u, v=None):
    gram[...] = gram_in[...]
    vs = list(vs) + ([] if v is None else [v])
    totals = [jnp.zeros((8, LANES), f32)] * len(vs)
    for s in range(SLABS):
        us = u[s]
        for i, vi in enumerate(vs):
            totals[i] = totals[i] + jnp.sum((vi[s] * us).reshape(8, 8, LANES), axis=0)
    level = len(vs) - (0 if v is None else 1)
    for i, total in enumerate(totals):
        r = gram_row(i, level)
        gram[r : r + 1, :] = jnp.sum(total, axis=0, keepdims=True)


def next_residual(place, first, span, near, far, edge_near, edge_far, coef, inside, u):
    halo = merge_edges(place, edge_near[...], edge_far[...])
    scale = basis_coefs(span[0:1, 0:1], 0 if first else 1)[2]

    def write(c, x, value):
        u[4 * c + x] = inside[4 * c + x] - value * scale

    stencil_beyond(coef, lambda c: faces_of(place, near[c], far[c]), halo, write)


def step_kernel(first, place, span, hnear, hfar, enear, efar, coef, inside, gt, factor,
                u, v, near, far, edge, prof, mb, sb, spread):
    next_residual(place, first, span, hnear, hfar, enear, efar, coef, inside, u)
    coarse(u, gt, factor, prof, mb, sb, spread)
    finish_direction(place, u, coef, spread, v, near, far, edge)


def last_kernel(place, span, hnear, hfar, enear, efar, coef, inside, gram_in,
                v0, v1, v2, v3, v4, copies, u, gram):
    vs = (v0, v1, v2, v3, v4)
    next_residual(place, False, span, hnear, hfar, enear, efar, coef, inside, u)
    store_dots(gram, gram_in, vs, u)
    pack_sums(gram, copies)


def krylov_weights(span, sums):
    def product(i, j):
        r = gram_row(i, j)
        return sums[r // 8][r % 8 : r % 8 + 1, :]

    n = [[product(i, j) for j in range(S + 1)] for i in range(S)]
    half = 0.5 * span
    quarter = 0.5 * half

    def operate(p):
        out = [None] * (S + 1)

        def put(i, value):
            out[i] = value if out[i] is None else out[i] + value

        for j, w in enumerate(p):
            put(j, half * w)
            put(j + 1, (half if j == 0 else quarter) * w)
            if j:
                put(j - 1, quarter * w)
        return out[: len(p) + 1]

    def pair(a, b):
        total = None
        for i, ai in enumerate(a):
            part = None
            for j, bj in enumerate(b):
                term = n[i][j] * bj
                part = term if part is None else part + term
            total = ai * part if total is None else total + ai * part
        return total

    one = jnp.ones_like(span)
    r, p = [one], [one]
    x = []
    norm = n[0][0]
    for k in range(S):
        image = operate(p)
        alpha = norm / pair(p, image)
        for j, w in enumerate(p):
            if j < len(x):
                x[j] = x[j] + alpha * w
            else:
                x.append(alpha * w)
        r = [(r[j] - alpha * w) if j < len(r) else -(alpha * w) for j, w in enumerate(image)]
        if k + 1 < S:
            fresh = pair(r, r)
            beta = fresh / norm
            p = [r[j] + beta * p[j] if j < len(p) else r[j] for j in range(len(r))]
            norm = fresh
    return x


def weights_of(span, tiles):
    total = tree([tiles[i] for i in range(PLACES)])
    columns = [total[:, q : q + 1] for q in range(GRAM[0] // 8)]
    return krylov_weights(span[0:1, 0:1], columns)


def combine(x, parts, before=None):
    total = x[0] * parts[0]
    for j in range(1, S):
        total = total + x[j] * parts[j]
    return total if before is None else before + total


def combine_kernel(place, span, tiles, fields, vh,
                   v0, v1, v2, v3, v4, n0, n1, n2, n3, n4, f0, f1, f2, f3, f4,
                   en0, en1, en2, en3, en4, ef0, ef1, ef2, ef3, ef4,
                   flow, coef, u):
    x = weights_of(span, tiles)
    vs = (v0, v1, v2, v3, v4)
    ns, fs = (n0, n1, n2, n3, n4), (f0, f1, f2, f3, f4)
    ens, efs = (en0, en1, en2, en3, en4), (ef0, ef1, ef2, ef3, ef4)
    for s in range(SLABS):
        flow[s] = combine(x, [t[s] for t in vs])
    for c in range(3):
        flow[12 + c], flow[15 + c] = faces_of(
            place, combine(x, [t[c] for t in ns]), combine(x, [t[c] for t in fs]))
    halo = merge_edges(
        place, combine(x, [t[...] for t in ens]), combine(x, [t[...] for t in efs]))

    def thinned(viscosity, a, b, c):
        return viscosity / (1.0 + 25.0 * (a * a + b * b + c * c))

    for i in range(4):
        flow[18 + i] = thinned(fields[SLABS + i], flow[i], flow[4 + i], flow[8 + i])
    vis_low, vis_high = faces_of(place, vh[0], vh[1])
    vis_low = thinned(vis_low, flow[12], flow[13], flow[14])
    vis_high = thinned(vis_high, flow[15], flow[16], flow[17])
    second = pltpu.roll(halo, LANES - 8, 1)
    third = pltpu.roll(halo, LANES - 16, 1)
    vis_halo = thinned(merge_edges(place, vh[2], vh[3]), halo, second, third)
    store_coefs(coef, lambda i: flow[18 + i], vis_low, vis_high, vis_halo)

    def write(c, i, value):
        u[4 * c + i] = fields[4 * c + i] - value

    stencil_inside(coef, flow, write)

    def write_beyond(c, i, value):
        u[4 * c + i] = u[4 * c + i] + value

    stencil_beyond(coef, lambda c: (flow[12 + c], flow[15 + c]), halo, write_beyond)
    flow[13] = halo


def restart_kernel(place, u, coef, gt, factor_in, v, near, far, edge, gram, factor,
                   prof, mb, sb, spread, arrived):
    fetch = pltpu.make_async_copy(factor_in, factor, arrived)
    fetch.start()
    merge(u, gt, prof, mb)
    fetch.wait()
    solve(factor, mb, sb)
    spread_over(gt, sb, spread)
    finish_direction(place, u, coef, spread, v, near, far, edge)
    gram[...] = jnp.zeros(GRAM, f32)
    gram[0:1, :] = dot_rows(v, u)


def end_kernel(place, span, tiles, flow,
               v0, v1, v2, v3, v4, n0, n1, n2, n3, n4, f0, f1, f2, f3, f4,
               en0, en1, en2, en3, en4, ef0, ef1, ef2, ef3, ef4,
               velocity, pressure, vel, press):
    lanes, rows = lane_ids(), row_ids()
    x = weights_of(span, tiles)
    vs = (v0, v1, v2, v3, v4)
    ns, fs = (n0, n1, n2, n3, n4), (f0, f1, f2, f3, f4)
    ens, efs = (en0, en1, en2, en3, en4), (ef0, ef1, ef2, ef3, ef4)
    at = pl.multiple_of(place[4] * 8, 8)
    for s in range(SLABS):
        vel[s] = combine(x, [t[s] for t in vs], flow[s])
    low, high = faces_of(
        place, combine(x, [t[0] for t in ns]), combine(x, [t[0] for t in fs]))
    low, high = flow[12] + low, flow[15] + high
    halo = flow[13] + merge_edges(
        place, combine(x, [t[...] for t in ens]), combine(x, [t[...] for t in efs]))
    for i in range(4):
        vis = flow[18 + i]
        up = vel[i + 1] if i < 3 else high
        down = vel[i - 1] if i else low
        w = vel[4 + i]
        yp = jnp.where(rows == ROWS - 1, 0.0, pltpu.roll(w, ROWS - 1, 0))
        ym = jnp.where(rows == 0, 0.0, pltpu.roll(w, 1, 0))
        zp, zm = along_z(vel[8 + i], halo, 8 + i, lanes)
        divergence = 0.5 * (up - down) + 0.5 * (yp - ym) + 0.5 * (zp - zm)
        press[i] = -(vis / (1.0 + vis)) * divergence
    for s in range(SLABS):
        velocity[s] = vel[s, pl.ds(at, 8), :]
    for i in range(4):
        pressure[i] = press[i, pl.ds(at, 8), :]


def call(kernel, outs, scratch, place, *args, far_away=None, beside=False):
    vmem = pl.BlockSpec(memory_space=pltpu.VMEM)
    places = [pl.BlockSpec(memory_space=pltpu.SMEM)] + [vmem] * len(args)
    if far_away is not None:
        places[1 + far_away] = pl.BlockSpec(memory_space=pl.ANY)
    cost = None
    if beside:
        size = sum(a.size for a in args)
        cost = pl.CostEstimate(flops=2 * size, bytes_accessed=4 * size, transcendentals=0)
    return pl.pallas_call(
        kernel,
        out_shape=[jax.ShapeDtypeStruct(o, f32) for o in outs],
        in_specs=places,
        out_specs=[vmem] * len(outs),
        scratch_shapes=[pltpu.VMEM(s, f32) if isinstance(s, tuple) else s for s in scratch],
        cost_estimate=cost,
        compiler_params=pltpu.CompilerParams(vmem_limit_bytes=20 * 2**20),
    )(place, *args)


MERGE = ((24, LANES), (KC, LANES))
SPREAD = ((KC, LANES), (24, LANES))
DIRECTION = (FIELD, FACE, FACE, EDGE, GRAM)


def swap_near(value, axis):
    return lax.ppermute(value, axis, [(i, i ^ 1) for i in range(lax.axis_size(axis))])


def swap_far(value, axis):
    count = lax.axis_size(axis)
    pairs = [(i, (i + 1) % count) for i in range(1, count, 2)]
    return lax.ppermute(value, axis, pairs + [(b, a) for a, b in pairs])


def swapped(near, far, edge):
    return (
        swap_far(far, "cap"),
        swap_near(near, "cap"),
        swap_far(edge, "sub"),
        swap_near(edge, "sub"),
    )


def ordered(pieces):
    far_face, near_face, far_edge, near_edge = pieces
    return near_face, far_face, near_edge, far_edge


def shared(copies):
    return lax.all_to_all(copies, ("cap", "sub"), 0, 0)


def crossed(value, step):
    caps, groups, subs = (lax.axis_size(axis) for axis in ("cap", "grp", "sub"))

    def at(cap, grp, sub):
        return (cap * groups + grp) * subs + sub

    pairs = [
        (at(c ^ g, g, b ^ step), at(c, g, b))
        for c in range(caps) for g in range(groups) for b in range(subs)
    ]
    return lax.ppermute(value, ("cap", "grp", "sub"), pairs)


def exchanged(pay):
    copies = jnp.broadcast_to(pay[None], (GROUPS,) + pay.shape)
    return lax.all_to_all(copies, "grp", 0, 0)


def body(right_side, viscosity, coarse_basis, coarse_factor):
    cap, sub = lax.axis_index("cap"), lax.axis_index("sub")
    caps, subs = lax.axis_size("cap"), lax.axis_size("sub")
    place = jnp.stack([
        cap % 2, (cap != 0) & (cap != caps - 1),
        sub % 2, (sub != 0) & (sub != subs - 1),
        lax.axis_index("grp"),
    ]).astype(jnp.int32)
    odd = cap % 2 == 1
    basis = coarse_basis[0, 0]
    tiles = basis.T.reshape(KB // 8, 8, LANES)
    gt = lax.all_gather(tiles, "grp", axis=0).reshape(GROUPS, KB, LANES)
    columns = []
    for x in range(4):
        columns += [viscosity[x, :, -1:], viscosity[x, :, :1]]
    own_edge = jnp.concatenate(columns + [jnp.zeros((8, LANES - 8), f32)], axis=1)
    first, last = viscosity[0], viscosity[3]
    vhalos = jnp.stack(ordered(swapped(
        jnp.where(odd, first, last), jnp.where(odd, last, first), own_edge)))
    vhalos, rows, _ = lax.optimization_barrier((vhalos, coarse_factor[0, 0], tiles))
    factor = lax.all_gather(rows, "grp", axis=0, tiled=True)
    own = jnp.pad(coarse_factor[0, 0].T, ((0, 0), (0, 2 * LANES - KC // GROUPS)))

    (copies,) = call(
        local_kernel, ((GROUPS, 18, 8, LANES),), (),
        place, right_side.reshape(SLABS, 8, LANES), viscosity, basis)
    fields, copies = call(
        begin_kernel, ((16, ROWS, LANES), (GROUPS, 5, 8, LANES)),
        ((KC, LANES), (1, 8, LANES)),
        place, lax.all_to_all(copies, "grp", 0, 0), own, vhalos)
    coef, v, near, far, edge, gram, vh = call(
        start_kernel, (COEF,) + DIRECTION + ((4, ROWS, LANES),), SPREAD,
        place, lax.all_to_all(copies, "grp", 0, 0), fields, gt)
    u = fields
    for picard in range(2):
        us, vs, halos = [u], [v], []
        for k in range(S):
            beyond = ordered(swapped(near, far, edge))
            if picard == 0 and k == 0:
                (inside,) = call(inside_kernel, (FIELD,), (), place, v, coef, beside=True)
            else:
                gram, inside = call(
                    functools.partial(beside_kernel, k), (GRAM, FIELD), (),
                    place, span, gram, coef, *vs, *us[::-1][:2], beside=True)
            beyond, gram, inside = lax.optimization_barrier((beyond, gram, inside))
            halos.append(beyond)
            if k + 1 == S:
                (copies,) = call(
                    last_kernel, ((PLACES, 8, LANES),), (FIELD, GRAM),
                    place, span, *beyond, coef, inside, gram, *vs)
                break
            if picard == 0 and k == 0:
                image, sums = call(
                    image_kernel, (FIELD, (8, LANES)), (),
                    place, v, *beyond, coef, gram, inside)
                parts = [crossed(sums, step) for step in range(4)]
                (pay,) = call(
                    merge_kernel, ((1, 8, LANES),), MERGE, place, image, gt, own, beside=True)
                (pays,) = call(carry_kernel, ((GROUPS, 2, 8, LANES),), (), place, pay, *parts)
                span, u, v, near, far, edge = call(
                    first_kernel, ((8, LANES), FIELD) + DIRECTION[:4], SPREAD,
                    place, lax.all_to_all(pays, "grp", 0, 0), image, u, v, coef, gt)
            elif picard == 0:
                u, pay = call(
                    residual_kernel, (FIELD, (1, 8, LANES)), MERGE,
                    place, span, *beyond, coef, inside, gt, own)
                v, near, far, edge = call(
                    direction_kernel, DIRECTION[:4], SPREAD,
                    place, exchanged(pay), coef, gt, u)
            else:
                u, v, near, far, edge = call(
                    functools.partial(step_kernel, k == 0), (FIELD,) + DIRECTION[:4],
                    MERGE + SPREAD, place, span, *beyond, coef, inside, gt, factor)
            us.append(u)
            vs.append(v)
        tiles = shared(copies)
        kept = vs + [h[side] for side in range(4) for h in halos]
        if picard == 0:
            flow, coef, u = call(
                combine_kernel, (FLOW, COEF, FIELD), (), place, span, tiles, fields, vh, *kept)
            v, near, far, edge, gram, factor = call(
                restart_kernel, DIRECTION + ((KC, KC),),
                MERGE + SPREAD + (pltpu.SemaphoreType.DMA(()),),
                place, u, coef, gt, factor, far_away=3)
        else:
            result, pressure = call(
                end_kernel, ((SLABS, 8, LANES), (4, 8, LANES)), (FIELD, (4, ROWS, LANES)),
                place, span, tiles, flow, *kept)
    return result.reshape(3, 4, 8, LANES), pressure


def solution(mesh):
    placed = (
        P(None, "cap", "grp", "sub"),
        P("cap", "grp", "sub"),
        P("cap", "grp", "sub", None),
        P("cap", "sub", "grp", None),
    )
    return jax.shard_map(
        body,
        mesh=mesh,
        in_specs=placed,
        out_specs=(P(None, "cap", "grp", "sub"), P("cap", "grp", "sub")),
        check_vma=False,
    )
```

```python
import functools

import jax
import jax.numpy as jnp
from jax import lax
from jax.experimental import pallas as pl
from jax.experimental.pallas import tpu as pltpu
from jax.sharding import PartitionSpec as P

S = 5
SLABS = 12
ROWS = 64
LANES = 128
GROUPS = 8
KB = 512
KC = 1536
SPAN = 2.6
FIELD = (SLABS, ROWS, LANES)
FACE = (3, ROWS, LANES)
EDGE = (ROWS, LANES)
GRAM = (24, LANES)
PLACES = 32
FLOW = (22, ROWS, LANES)
COEF = (9, 4, ROWS, LANES)
f32 = jnp.float32


def gram_row(i, j):
    i, j = min(i, j), max(i, j)
    return sum(min(t, S - 1) + 1 for t in range(j)) + i


def lane_ids():
    return lax.broadcasted_iota(jnp.int32, (ROWS, LANES), 1)


def row_ids():
    return lax.broadcasted_iota(jnp.int32, (ROWS, LANES), 0)


def ends_of(halo, i):
    return pltpu.roll(halo, LANES - 1 - 2 * i, 1)


def along_z(w, halo, i, lanes):
    ends = ends_of(halo, i)
    after = jnp.where(lanes == LANES - 1, ends, pltpu.roll(w, LANES - 1, 1))
    before = jnp.where(lanes == 0, ends, pltpu.roll(w, 1, 1))
    return after, before


def flag(place, i):
    return jnp.full((ROWS, LANES), place[i], jnp.int32) == 1


def faces_of(place, near, far):
    odd, inner = flag(place, 0), flag(place, 1)
    far = jnp.where(inner, far, 0.0)
    return jnp.where(odd, near, far), jnp.where(odd, far, near)


def merge_edges(place, near, far):
    far = jnp.where(flag(place, 3), far, 0.0)
    odd = flag(place, 2)
    low, high = jnp.where(odd, near, far), jnp.where(odd, far, near)
    return jnp.where(lane_ids() % 2 == 1, pltpu.roll(low, 1, 1), pltpu.roll(high, LANES - 1, 1))


def edge_of(get, count, lanes):
    edge = jnp.zeros((ROWS, LANES), f32)
    for i in range(count):
        moved = pltpu.roll(get(i), 2 * i + 1, 1)
        edge = jnp.where((lanes == 2 * i) | (lanes == 2 * i + 1), moved, edge)
    return edge


def store_coefs(coef, vis, low, high, halo):
    lanes, rows = lane_ids(), row_ids()
    for x in range(4):
        v = vis(x)
        up = vis(x + 1) if x < 3 else high
        down = vis(x - 1) if x else low
        yp = jnp.where(rows == ROWS - 1, 0.0, pltpu.roll(v, ROWS - 1, 0))
        ym = jnp.where(rows == 0, 0.0, pltpu.roll(v, 1, 0))
        zp, zm = along_z(v, halo, x, lanes)
        faces = [0.5 * (v + n) for n in (up, down, yp, ym, zp, zm)]
        diagonal = 1.0 + faces[0] + faces[1] + faces[2] + faces[3] + faces[4] + faces[5]
        faces[2] = jnp.where(rows == ROWS - 1, 0.0, faces[2])
        faces[3] = jnp.where(rows == 0, 0.0, faces[3])
        first, last = lanes == 0, lanes == LANES - 1
        coef[8, x] = jnp.where(first, faces[5], jnp.where(last, faces[4], 0.0))
        faces[4] = jnp.where(last, 0.0, faces[4])
        faces[5] = jnp.where(first, 0.0, faces[5])
        coef[0, x] = diagonal
        for f in range(6):
            coef[1 + f, x] = faces[f]
        coef[7, x] = 1.0 / diagonal


def stencil_inside(coef, field, write):
    for x in range(4):
        for c in range(3):
            w = field[4 * c + x]
            beside = coef[3, x] * pltpu.roll(w, ROWS - 1, 0) + coef[4, x] * pltpu.roll(w, 1, 0)
            beside = beside + coef[5, x] * pltpu.roll(w, LANES - 1, 1)
            beside = beside + coef[6, x] * pltpu.roll(w, 1, 1)
            if x < 3:
                beside = beside + coef[1, x] * field[4 * c + x + 1]
            if x:
                beside = beside + coef[2, x] * field[4 * c + x - 1]
            write(c, x, coef[0, x] * w - beside)


def stencil_beyond(coef, sides, halo, write):
    for c in range(3):
        low, high = sides(c)
        for x in range(4):
            beside = coef[8, x] * ends_of(halo, 4 * c + x)
            if x == 0:
                beside = beside + coef[2, x] * low
            if x == 3:
                beside = beside + coef[1, x] * high
            write(c, x, beside)


def dot_rows(a, b):
    total = jnp.zeros((8, LANES), f32)
    for s in range(SLABS):
        total = total + jnp.sum((a[s] * b[s]).reshape(8, 8, LANES), axis=0)
    return jnp.sum(total, axis=0, keepdims=True)


def merge(u, gt, prof, mb):
    for c in range(3):
        total = u[4 * c] + u[4 * c + 1] + u[4 * c + 2] + u[4 * c + 3]
        prof[8 * c : 8 * c + 8] = jnp.sum(total.reshape(8, 8, LANES), axis=1) * (1.0 / 32.0)

    @pl.loop(0, KB // 32, unroll=4)
    def _(step):
        at = pl.multiple_of(step * 32, 32)
        totals = [jnp.zeros((32, LANES), f32)] * 3
        for g in range(GROUPS):
            b = gt[g, pl.ds(at, 32), :]
            for c in range(3):
                totals[c] = totals[c] + b * prof[8 * c + g : 8 * c + g + 1, :]
        for c in range(3):
            total = jnp.sum(totals[c], axis=1, keepdims=True)
            mb[pl.ds(c * KB + at, 32), :] = jnp.broadcast_to(total, (32, LANES))


def solve(factor, mb, sb):
    def rows_of(step, totals):
        totals = list(totals)
        for part in range(4):
            at = pl.multiple_of(step * 32 + part * 8, 8)
            m = mb[pl.ds(at, 8), :]
            for q in range(KC // LANES):
                totals[q] = totals[q] + factor[pl.ds(at, 8), LANES * q : LANES * (q + 1)] * m
        return tuple(totals)

    zero = jnp.zeros((8, LANES), f32)
    totals = lax.fori_loop(0, KC // 32, rows_of, (zero,) * (KC // LANES))
    for q in range(KC // LANES):
        row = jnp.sum(totals[q], axis=0, keepdims=True)
        sb[LANES * q : LANES * (q + 1), :] = jnp.broadcast_to(row, (LANES, LANES)).T


def solve_own(own, mb, pay):
    def rows_of(step, totals):
        totals = list(totals)
        for part in range(8):
            at = pl.multiple_of(step * 64 + part * 8, 8)
            m = mb[pl.ds(at, 8), :]
            for q in range(2):
                r = 2 * (part % 4) + q
                totals[r] = totals[r] + own[pl.ds(at, 8), LANES * q : LANES * (q + 1)] * m
        return tuple(totals)

    zero = jnp.zeros((8, LANES), f32)
    t = lax.fori_loop(0, KC // 64, rows_of, (zero,) * 8)
    pay[0] = zero
    for q in range(2):
        total = (t[q] + t[2 + q]) + (t[4 + q] + t[6 + q])
        pay[0, q : q + 1, :] = jnp.sum(total, axis=0, keepdims=True)


def unpack(pays, sb):
    for g in range(GROUPS):
        at = g * (KC // GROUPS)
        left = jnp.broadcast_to(pays[g, 0, 0:1, :], (LANES, LANES)).T
        right = jnp.broadcast_to(pays[g, 0, 1:2, :], (LANES, LANES)).T
        sb[at : at + LANES, :] = left
        sb[at + LANES : at + KC // GROUPS, :] = right[: KC // GROUPS - LANES]


def spread_over(gt, sb, spread):
    def spread_of(step, totals):
        totals = list(totals)
        for part in range(2):
            at = pl.multiple_of(step * 16 + part * 8, 8)
            solved = [sb[pl.ds(c * KB + at, 8), :] for c in range(3)]
            for g in range(GROUPS):
                b = gt[g, pl.ds(at, 8), :]
                for c in range(3):
                    totals[8 * c + g] = totals[8 * c + g] + b * solved[c]
        return tuple(totals)

    zero = jnp.zeros((8, LANES), f32)
    totals = lax.fori_loop(0, KB // 16, spread_of, (zero,) * 24)
    for r in range(24):
        spread[r : r + 1, :] = jnp.sum(totals[r], axis=0, keepdims=True)


def coarse(u, gt, factor, prof, mb, sb, spread):
    merge(u, gt, prof, mb)
    solve(factor, mb, sb)
    spread_over(gt, sb, spread)


def finish_direction(place, u, coef, spread, v, near, far, edge):
    for x in range(4):
        for c in range(3):
            s = 4 * c + x
            wide = jnp.broadcast_to(spread[8 * c : 8 * c + 8, :][:, None, :], (8, 8, LANES))
            v[s] = u[s] * coef[7, x] + wide.reshape(ROWS, LANES)
    if near is not None:
        hand_over(place, v, near, far, edge)


def hand_over(place, v, near, far, edge):
    for c in range(3):
        near[c] = v[4 * c + 3 - 3 * place[0]]
        far[c] = v[4 * c + 3 * place[0]]
    edge[...] = edge_of(lambda i: v[i], SLABS, lane_ids())


def basis_coefs(span, k):
    half = 0.5 * span
    if k == 0:
        return half, None, 1.0 / half
    return half, 0.5 * half, 2.0 / half


def local_kernel(place, force, viscosity, basis, copies, near, far, edge):
    shares = []
    for c in range(3):
        total = force[4 * c] + force[4 * c + 1] + force[4 * c + 2] + force[4 * c + 3]
        row = jnp.sum(total, axis=0, keepdims=True) * (1.0 / 32.0)
        column = jnp.broadcast_to(row, (LANES, LANES)).T
        for q in range(KB // LANES):
            part = basis[:, LANES * q : LANES * (q + 1)] * column
            shares.append(jnp.sum(part, axis=0, keepdims=True))
    rows = lax.broadcasted_iota(jnp.int32, (8, LANES), 0)
    lanes = lax.broadcasted_iota(jnp.int32, (8, LANES), 1)
    for q in range(2):
        tile = jnp.zeros((8, LANES), f32)
        for r in range(8):
            if 8 * q + r < len(shares):
                tile = jnp.where(rows == r, shares[8 * q + r], tile)
        for g in range(GROUPS):
            copies[g, q] = tile
    near[...] = viscosity[3 - 3 * place[0]]
    far[...] = viscosity[3 * place[0]]
    columns = jnp.zeros((8, LANES), f32)
    for x in range(4):
        moved = pltpu.roll(viscosity[x], 2 * x + 1, 1)
        columns = jnp.where((lanes == 2 * x) | (lanes == 2 * x + 1), moved, columns)
    edge[...] = columns


def begin_kernel(place, pays, own, vnear, vfar, enear, efar, copies, mb, pay):
    for q in range(2):
        total = tree([pays[g, q] for g in range(GROUPS)])
        for r in range(8):
            at = LANES * (8 * q + r)
            if at < KC:
                row = jnp.broadcast_to(total[r : r + 1, :], (LANES, LANES))
                mb[at : at + LANES, :] = row.T
    solve_own(own, mb, pay)
    for g in range(GROUPS):
        copies[g, 0] = pay[0]
        for i, tile in enumerate((vnear, vfar, enear, efar)):
            copies[g, 1 + i] = tile[...]


def start_kernel(place, pays, gt,
                 coef, v, near, far, edge, gram, vh, fields, sb, spread):
    unpack(pays, sb)
    for g in range(GROUPS):
        for s in range(SLABS + 4):
            fields[s, 8 * g : 8 * g + 8, :] = gt[g, KB + 8 * s : KB + 8 * s + 8, :]
        for i in range(4):
            vh[i, 8 * g : 8 * g + 8, :] = pays[g, 1 + i]
    low, high = faces_of(place, vh[0], vh[1])
    halo = merge_edges(place, vh[2], vh[3])
    store_coefs(coef, lambda x: fields[SLABS + x], low, high, halo)
    spread_over(gt, sb, spread)
    finish_direction(place, fields, coef, spread, v, near, far, edge)
    gram[...] = jnp.zeros(GRAM, f32)
    gram[0:1, :] = dot_rows(v, fields)


def inside_kernel(place, v, coef, image):
    def write(c, x, value):
        image[4 * c + x] = value

    stencil_inside(coef, v, write)


def image_kernel(place, v, near, far, edge_near, edge_far, coef, gram, inside, image, sums):
    halo = merge_edges(place, edge_near[...], edge_far[...])

    def write(c, x, value):
        image[4 * c + x] = inside[4 * c + x] - value

    stencil_beyond(coef, lambda c: faces_of(place, near[c], far[c]), halo, write)
    sums[...] = jnp.zeros((8, LANES), f32)
    sums[0:1, :] = gram[0:1, :]
    sums[1:2, :] = dot_rows(v, image)


def merge_kernel(place, image, gt, own, pay, prof, mb):
    merge(image, gt, prof, mb)
    solve_own(own, mb, pay)


def carry_kernel(place, pay, s0, s1, s2, s3, copies):
    total = tree([s0[...], s1[...], s2[...], s3[...]])
    for g in range(GROUPS):
        copies[g, 0] = pay[0]
        copies[g, 1] = total


def first_kernel(place, pays, image, u0, v0, coef, gt,
                 span, u, v, near, far, edge, sb, spread):
    sums = jnp.sum(tree([pays[g, 1] for g in range(GROUPS)]), axis=1, keepdims=True)
    width = SPAN * sums[1:2, :] / sums[0:1, :]
    span[...] = jnp.broadcast_to(width, (8, LANES))
    shift, _, scale = basis_coefs(width, 0)
    unpack(pays, sb)
    spread_over(gt, sb, spread)
    finish_direction(place, image, coef, spread, v, None, None, None)
    for s in range(SLABS):
        u[s] = (image[s] - shift * u0[s]) * scale
        v[s] = (v[s] - shift * v0[s]) * scale
    hand_over(place, v, near, far, edge)


def residual_kernel(place, span, hnear, hfar, enear, efar, coef, inside, gt, own,
                    u, pay, prof, mb):
    next_residual(place, False, span, hnear, hfar, enear, efar, coef, inside, u)
    merge(u, gt, prof, mb)
    solve_own(own, mb, pay)


def direction_kernel(place, pays, coef, gt, u, v, near, far, edge, sb, spread):
    unpack(pays, sb)
    spread_over(gt, sb, spread)
    finish_direction(place, u, coef, spread, v, near, far, edge)


def beside_kernel(k, place, span, gram_in, coef, *refs):
    refs, (gram, inside) = refs[:-2], refs[-2:]
    vs, us = refs[: k + 1], refs[k + 1 :]
    uk = us[0]
    if k:
        store_dots(gram, gram_in, vs[:-1], uk, vs[-1])
    else:
        gram[...] = gram_in[...]
    shift, back, scale = basis_coefs(span[0:1, 0:1], k)

    def write(c, x, value):
        s = 4 * c + x
        value = value - shift * uk[s]
        if k:
            value = value - back * us[1][s]
        inside[s] = value * scale

    stencil_inside(coef, vs[-1], write)


def tree(parts):
    while len(parts) > 1:
        parts = [parts[i] + parts[i + 1] for i in range(0, len(parts), 2)]
    return parts[0]


def pack_sums(gram, copies):
    sums = jnp.sum(gram[...], axis=1, keepdims=True)
    lanes = lax.broadcasted_iota(jnp.int32, (8, LANES), 1)
    tile = jnp.zeros((8, LANES), f32)
    for q in range(GRAM[0] // 8):
        tile = jnp.where(lanes == q, sums[8 * q : 8 * q + 8], tile)
    for i in range(PLACES):
        copies[i] = tile


def store_dots(gram, gram_in, vs, u, v=None):
    gram[...] = gram_in[...]
    vs = list(vs) + ([] if v is None else [v])
    totals = [jnp.zeros((8, LANES), f32)] * len(vs)
    for s in range(SLABS):
        us = u[s]
        for i, vi in enumerate(vs):
            totals[i] = totals[i] + jnp.sum((vi[s] * us).reshape(8, 8, LANES), axis=0)
    level = len(vs) - (0 if v is None else 1)
    for i, total in enumerate(totals):
        r = gram_row(i, level)
        gram[r : r + 1, :] = jnp.sum(total, axis=0, keepdims=True)


def next_residual(place, first, span, near, far, edge_near, edge_far, coef, inside, u):
    halo = merge_edges(place, edge_near[...], edge_far[...])
    scale = basis_coefs(span[0:1, 0:1], 0 if first else 1)[2]

    def write(c, x, value):
        u[4 * c + x] = inside[4 * c + x] - value * scale

    stencil_beyond(coef, lambda c: faces_of(place, near[c], far[c]), halo, write)


def step_kernel(first, place, span, hnear, hfar, enear, efar, coef, inside, gt, factor,
                u, v, near, far, edge, prof, mb, sb, spread):
    next_residual(place, first, span, hnear, hfar, enear, efar, coef, inside, u)
    coarse(u, gt, factor, prof, mb, sb, spread)
    finish_direction(place, u, coef, spread, v, near, far, edge)


def last_kernel(place, span, hnear, hfar, enear, efar, coef, inside, gram_in,
                v0, v1, v2, v3, v4, copies, u, gram):
    vs = (v0, v1, v2, v3, v4)
    next_residual(place, False, span, hnear, hfar, enear, efar, coef, inside, u)
    store_dots(gram, gram_in, vs, u)
    pack_sums(gram, copies)


def krylov_weights(span, sums):
    def product(i, j):
        r = gram_row(i, j)
        return sums[r // 8][r % 8 : r % 8 + 1, :]

    n = [[product(i, j) for j in range(S + 1)] for i in range(S)]
    half = 0.5 * span
    quarter = 0.5 * half

    def operate(p):
        out = [None] * (S + 1)

        def put(i, value):
            out[i] = value if out[i] is None else out[i] + value

        for j, w in enumerate(p):
            put(j, half * w)
            put(j + 1, (half if j == 0 else quarter) * w)
            if j:
                put(j - 1, quarter * w)
        return out[: len(p) + 1]

    def pair(a, b):
        total = None
        for i, ai in enumerate(a):
            part = None
            for j, bj in enumerate(b):
                term = n[i][j] * bj
                part = term if part is None else part + term
            total = ai * part if total is None else total + ai * part
        return total

    one = jnp.ones_like(span)
    r, p = [one], [one]
    x = []
    norm = n[0][0]
    for k in range(S):
        image = operate(p)
        alpha = norm / pair(p, image)
        for j, w in enumerate(p):
            if j < len(x):
                x[j] = x[j] + alpha * w
            else:
                x.append(alpha * w)
        r = [(r[j] - alpha * w) if j < len(r) else -(alpha * w) for j, w in enumerate(image)]
        if k + 1 < S:
            fresh = pair(r, r)
            beta = fresh / norm
            p = [r[j] + beta * p[j] if j < len(p) else r[j] for j in range(len(r))]
            norm = fresh
    return x


def weights_of(span, tiles):
    total = tree([tiles[i] for i in range(PLACES)])
    columns = [total[:, q : q + 1] for q in range(GRAM[0] // 8)]
    return krylov_weights(span[0:1, 0:1], columns)


def combine(x, parts, before=None):
    total = x[0] * parts[0]
    for j in range(1, S):
        total = total + x[j] * parts[j]
    return total if before is None else before + total


def combine_kernel(place, span, tiles, fields, vh,
                   v0, v1, v2, v3, v4, n0, n1, n2, n3, n4, f0, f1, f2, f3, f4,
                   en0, en1, en2, en3, en4, ef0, ef1, ef2, ef3, ef4,
                   flow, coef, u):
    x = weights_of(span, tiles)
    vs = (v0, v1, v2, v3, v4)
    ns, fs = (n0, n1, n2, n3, n4), (f0, f1, f2, f3, f4)
    ens, efs = (en0, en1, en2, en3, en4), (ef0, ef1, ef2, ef3, ef4)
    for s in range(SLABS):
        flow[s] = combine(x, [t[s] for t in vs])
    for c in range(3):
        flow[12 + c], flow[15 + c] = faces_of(
            place, combine(x, [t[c] for t in ns]), combine(x, [t[c] for t in fs]))
    halo = merge_edges(
        place, combine(x, [t[...] for t in ens]), combine(x, [t[...] for t in efs]))

    def thinned(viscosity, a, b, c):
        return viscosity / (1.0 + 25.0 * (a * a + b * b + c * c))

    for i in range(4):
        flow[18 + i] = thinned(fields[SLABS + i], flow[i], flow[4 + i], flow[8 + i])
    vis_low, vis_high = faces_of(place, vh[0], vh[1])
    vis_low = thinned(vis_low, flow[12], flow[13], flow[14])
    vis_high = thinned(vis_high, flow[15], flow[16], flow[17])
    second = pltpu.roll(halo, LANES - 8, 1)
    third = pltpu.roll(halo, LANES - 16, 1)
    vis_halo = thinned(merge_edges(place, vh[2], vh[3]), halo, second, third)
    store_coefs(coef, lambda i: flow[18 + i], vis_low, vis_high, vis_halo)

    def write(c, i, value):
        u[4 * c + i] = fields[4 * c + i] - value

    stencil_inside(coef, flow, write)

    def write_beyond(c, i, value):
        u[4 * c + i] = u[4 * c + i] + value

    stencil_beyond(coef, lambda c: (flow[12 + c], flow[15 + c]), halo, write_beyond)
    flow[13] = halo


def restart_kernel(place, u, coef, gt, factor_in, v, near, far, edge, gram, factor,
                   prof, mb, sb, spread, arrived):
    fetch = pltpu.make_async_copy(factor_in, factor, arrived)
    fetch.start()
    merge(u, gt, prof, mb)
    fetch.wait()
    solve(factor, mb, sb)
    spread_over(gt, sb, spread)
    finish_direction(place, u, coef, spread, v, near, far, edge)
    gram[...] = jnp.zeros(GRAM, f32)
    gram[0:1, :] = dot_rows(v, u)


def end_kernel(place, span, tiles, flow,
               v0, v1, v2, v3, v4, n0, n1, n2, n3, n4, f0, f1, f2, f3, f4,
               en0, en1, en2, en3, en4, ef0, ef1, ef2, ef3, ef4,
               velocity, pressure, vel, press):
    lanes, rows = lane_ids(), row_ids()
    x = weights_of(span, tiles)
    vs = (v0, v1, v2, v3, v4)
    ns, fs = (n0, n1, n2, n3, n4), (f0, f1, f2, f3, f4)
    ens, efs = (en0, en1, en2, en3, en4), (ef0, ef1, ef2, ef3, ef4)
    at = pl.multiple_of(place[4] * 8, 8)
    for s in range(SLABS):
        vel[s] = combine(x, [t[s] for t in vs], flow[s])
    low, high = faces_of(
        place, combine(x, [t[0] for t in ns]), combine(x, [t[0] for t in fs]))
    low, high = flow[12] + low, flow[15] + high
    halo = flow[13] + merge_edges(
        place, combine(x, [t[...] for t in ens]), combine(x, [t[...] for t in efs]))
    for i in range(4):
        vis = flow[18 + i]
        up = vel[i + 1] if i < 3 else high
        down = vel[i - 1] if i else low
        w = vel[4 + i]
        yp = jnp.where(rows == ROWS - 1, 0.0, pltpu.roll(w, ROWS - 1, 0))
        ym = jnp.where(rows == 0, 0.0, pltpu.roll(w, 1, 0))
        zp, zm = along_z(vel[8 + i], halo, 8 + i, lanes)
        divergence = 0.5 * (up - down) + 0.5 * (yp - ym) + 0.5 * (zp - zm)
        press[i] = -(vis / (1.0 + vis)) * divergence
    for s in range(SLABS):
        velocity[s] = vel[s, pl.ds(at, 8), :]
    for i in range(4):
        pressure[i] = press[i, pl.ds(at, 8), :]


def call(kernel, outs, scratch, place, *args, far_away=None, beside=False):
    vmem = pl.BlockSpec(memory_space=pltpu.VMEM)
    places = [pl.BlockSpec(memory_space=pltpu.SMEM)] + [vmem] * len(args)
    if far_away is not None:
        places[1 + far_away] = pl.BlockSpec(memory_space=pl.ANY)
    cost = None
    if beside:
        size = sum(a.size for a in args)
        cost = pl.CostEstimate(flops=2 * size, bytes_accessed=4 * size, transcendentals=0)
    return pl.pallas_call(
        kernel,
        out_shape=[jax.ShapeDtypeStruct(o, f32) for o in outs],
        in_specs=places,
        out_specs=[vmem] * len(outs),
        scratch_shapes=[pltpu.VMEM(s, f32) if isinstance(s, tuple) else s for s in scratch],
        cost_estimate=cost,
        compiler_params=pltpu.CompilerParams(vmem_limit_bytes=20 * 2**20),
    )(place, *args)


MERGE = ((24, LANES), (KC, LANES))
SPREAD = ((KC, LANES), (24, LANES))
DIRECTION = (FIELD, FACE, FACE, EDGE, GRAM)


def swap_near(value, axis):
    return lax.ppermute(value, axis, [(i, i ^ 1) for i in range(lax.axis_size(axis))])


def swap_far(value, axis):
    count = lax.axis_size(axis)
    pairs = [(i, (i + 1) % count) for i in range(1, count, 2)]
    return lax.ppermute(value, axis, pairs + [(b, a) for a, b in pairs])


def swapped(near, far, edge):
    return (
        swap_far(far, "cap"),
        swap_near(near, "cap"),
        swap_far(edge, "sub"),
        swap_near(edge, "sub"),
    )


def ordered(pieces):
    far_face, near_face, far_edge, near_edge = pieces
    return near_face, far_face, near_edge, far_edge


def shared(copies):
    return lax.all_to_all(copies, ("cap", "sub"), 0, 0)


def crossed(value, step):
    caps, groups, subs = (lax.axis_size(axis) for axis in ("cap", "grp", "sub"))

    def at(cap, grp, sub):
        return (cap * groups + grp) * subs + sub

    pairs = [
        (at(c ^ g, g, b ^ step), at(c, g, b))
        for c in range(caps) for g in range(groups) for b in range(subs)
    ]
    return lax.ppermute(value, ("cap", "grp", "sub"), pairs)


def exchanged(pay):
    copies = jnp.broadcast_to(pay[None], (GROUPS,) + pay.shape)
    return lax.all_to_all(copies, "grp", 0, 0)


def body(right_side, viscosity, coarse_basis, coarse_factor):
    cap, sub = lax.axis_index("cap"), lax.axis_index("sub")
    caps, subs = lax.axis_size("cap"), lax.axis_size("sub")
    place = jnp.stack([
        cap % 2, (cap != 0) & (cap != caps - 1),
        sub % 2, (sub != 0) & (sub != subs - 1),
        lax.axis_index("grp"),
    ]).astype(jnp.int32)
    basis = coarse_basis[0, 0]
    force = right_side.reshape(SLABS, 8, LANES)
    own_gt = jnp.concatenate(
        [basis.T.reshape(KB // 8, 8, LANES), force, viscosity], axis=0)
    gt = lax.all_gather(own_gt, "grp", axis=0).reshape(GROUPS, -1, LANES)

    copies, near, far, edge = call(
        local_kernel, ((GROUPS, 2, 8, LANES),) + ((8, LANES),) * 3, (),
        place, force, viscosity, basis)
    vhalos = ordered(swapped(near, far, edge))
    vhalos, rows, _ = lax.optimization_barrier((vhalos, coarse_factor[0, 0], own_gt))
    factor = lax.all_gather(rows, "grp", axis=0, tiled=True)
    own = jnp.pad(coarse_factor[0, 0].T, ((0, 0), (0, 2 * LANES - KC // GROUPS)))
    (copies,) = call(
        begin_kernel, ((GROUPS, 5, 8, LANES),), ((KC, LANES), (1, 8, LANES)),
        place, lax.all_to_all(copies, "grp", 0, 0), own, *vhalos)
    coef, v, near, far, edge, gram, vh, fields = call(
        start_kernel,
        (COEF,) + DIRECTION + ((4, ROWS, LANES), (SLABS + 4, ROWS, LANES)), SPREAD,
        place, lax.all_to_all(copies, "grp", 0, 0), gt)
    u = fields
    for picard in range(2):
        us, vs, halos = [u], [v], []
        for k in range(S):
            beyond = ordered(swapped(near, far, edge))
            if picard == 0 and k == 0:
                (inside,) = call(inside_kernel, (FIELD,), (), place, v, coef, beside=True)
            else:
                gram, inside = call(
                    functools.partial(beside_kernel, k), (GRAM, FIELD), (),
                    place, span, gram, coef, *vs, *us[::-1][:2], beside=True)
            beyond, gram, inside = lax.optimization_barrier((beyond, gram, inside))
            halos.append(beyond)
            if k + 1 == S:
                (copies,) = call(
                    last_kernel, ((PLACES, 8, LANES),), (FIELD, GRAM),
                    place, span, *beyond, coef, inside, gram, *vs)
                break
            if picard == 0 and k == 0:
                image, sums = call(
                    image_kernel, (FIELD, (8, LANES)), (),
                    place, v, *beyond, coef, gram, inside)
                parts = [crossed(sums, step) for step in range(4)]
                (pay,) = call(
                    merge_kernel, ((1, 8, LANES),), MERGE, place, image, gt, own, beside=True)
                (pays,) = call(carry_kernel, ((GROUPS, 2, 8, LANES),), (), place, pay, *parts)
                span, u, v, near, far, edge = call(
                    first_kernel, ((8, LANES), FIELD) + DIRECTION[:4], SPREAD,
                    place, lax.all_to_all(pays, "grp", 0, 0), image, u, v, coef, gt)
            elif picard == 0:
                u, pay = call(
                    residual_kernel, (FIELD, (1, 8, LANES)), MERGE,
                    place, span, *beyond, coef, inside, gt, own)
                v, near, far, edge = call(
                    direction_kernel, DIRECTION[:4], SPREAD,
                    place, exchanged(pay), coef, gt, u)
            else:
                u, v, near, far, edge = call(
                    functools.partial(step_kernel, k == 0), (FIELD,) + DIRECTION[:4],
                    MERGE + SPREAD, place, span, *beyond, coef, inside, gt, factor)
            us.append(u)
            vs.append(v)
        tiles = shared(copies)
        kept = vs + [h[side] for side in range(4) for h in halos]
        if picard == 0:
            flow, coef, u = call(
                combine_kernel, (FLOW, COEF, FIELD), (), place, span, tiles, fields, vh, *kept)
            v, near, far, edge, gram, factor = call(
                restart_kernel, DIRECTION + ((KC, KC),),
                MERGE + SPREAD + (pltpu.SemaphoreType.DMA(()),),
                place, u, coef, gt, factor, far_away=3)
        else:
            result, pressure = call(
                end_kernel, ((SLABS, 8, LANES), (4, 8, LANES)), (FIELD, (4, ROWS, LANES)),
                place, span, tiles, flow, *kept)
    return result.reshape(3, 4, 8, LANES), pressure


def solution(mesh):
    placed = (
        P(None, "cap", "grp", "sub"),
        P("cap", "grp", "sub"),
        P("cap", "grp", "sub", None),
        P("cap", "sub", "grp", None),
    )
    return jax.shard_map(
        body,
        mesh=mesh,
        in_specs=placed,
        out_specs=(P(None, "cap", "grp", "sub"), P("cap", "grp", "sub")),
        check_vma=False,
    )
```

```python
import functools

import jax
import jax.numpy as jnp
from jax import lax
from jax.experimental import pallas as pl
from jax.experimental.pallas import tpu as pltpu
from jax.sharding import PartitionSpec as P

S = 5
SLABS = 12
ROWS = 64
LANES = 128
GROUPS = 8
KB = 512
KC = 1536
APART = 1e-3
SPAN = 2.6
FIELD = (SLABS, ROWS, LANES)
FACE = (3, ROWS, LANES)
EDGE = (ROWS, LANES)
GRAM = (24, LANES)
PLACES = 32
FLOW = (22, ROWS, LANES)
COEF = (9, 4, ROWS, LANES)
f32 = jnp.float32


def gram_row(i, j):
    i, j = min(i, j), max(i, j)
    return sum(min(t, S - 1) + 1 for t in range(j)) + i


def lane_ids():
    return lax.broadcasted_iota(jnp.int32, (ROWS, LANES), 1)


def row_ids():
    return lax.broadcasted_iota(jnp.int32, (ROWS, LANES), 0)


def ends_of(halo, i):
    return pltpu.roll(halo, LANES - 1 - 2 * i, 1)


def along_z(w, halo, i, lanes):
    ends = ends_of(halo, i)
    after = jnp.where(lanes == LANES - 1, ends, pltpu.roll(w, LANES - 1, 1))
    before = jnp.where(lanes == 0, ends, pltpu.roll(w, 1, 1))
    return after, before


def flag(place, i):
    return jnp.full((ROWS, LANES), place[i], jnp.int32) == 1


def faces_of(place, near, far):
    odd, inner = flag(place, 0), flag(place, 1)
    far = jnp.where(inner, far, 0.0)
    return jnp.where(odd, near, far), jnp.where(odd, far, near)


def merge_edges(place, near, far):
    far = jnp.where(flag(place, 3), far, 0.0)
    odd = flag(place, 2)
    low, high = jnp.where(odd, near, far), jnp.where(odd, far, near)
    return jnp.where(lane_ids() % 2 == 1, pltpu.roll(low, 1, 1), pltpu.roll(high, LANES - 1, 1))


def edge_of(get, count, lanes):
    edge = jnp.zeros((ROWS, LANES), f32)
    for i in range(count):
        moved = pltpu.roll(get(i), 2 * i + 1, 1)
        edge = jnp.where((lanes == 2 * i) | (lanes == 2 * i + 1), moved, edge)
    return edge


def store_coefs(coef, vis, low, high, halo):
    lanes, rows = lane_ids(), row_ids()
    for x in range(4):
        v = vis(x)
        up = vis(x + 1) if x < 3 else high
        down = vis(x - 1) if x else low
        yp = jnp.where(rows == ROWS - 1, 0.0, pltpu.roll(v, ROWS - 1, 0))
        ym = jnp.where(rows == 0, 0.0, pltpu.roll(v, 1, 0))
        zp, zm = along_z(v, halo, x, lanes)
        faces = [0.5 * (v + n) for n in (up, down, yp, ym, zp, zm)]
        diagonal = 1.0 + faces[0] + faces[1] + faces[2] + faces[3] + faces[4] + faces[5]
        faces[2] = jnp.where(rows == ROWS - 1, 0.0, faces[2])
        faces[3] = jnp.where(rows == 0, 0.0, faces[3])
        first, last = lanes == 0, lanes == LANES - 1
        coef[8, x] = jnp.where(first, faces[5], jnp.where(last, faces[4], 0.0))
        faces[4] = jnp.where(last, 0.0, faces[4])
        faces[5] = jnp.where(first, 0.0, faces[5])
        coef[0, x] = diagonal
        for f in range(6):
            coef[1 + f, x] = faces[f]
        coef[7, x] = 1.0 / diagonal


def stencil_inside(coef, field, write):
    for x in range(4):
        for c in range(3):
            w = field[4 * c + x]
            beside = coef[3, x] * pltpu.roll(w, ROWS - 1, 0) + coef[4, x] * pltpu.roll(w, 1, 0)
            beside = beside + coef[5, x] * pltpu.roll(w, LANES - 1, 1)
            beside = beside + coef[6, x] * pltpu.roll(w, 1, 1)
            if x < 3:
                beside = beside + coef[1, x] * field[4 * c + x + 1]
            if x:
                beside = beside + coef[2, x] * field[4 * c + x - 1]
            write(c, x, coef[0, x] * w - beside)


def stencil_beyond(coef, sides, halo, write):
    for c in range(3):
        low, high = sides(c)
        for x in range(4):
            beside = coef[8, x] * ends_of(halo, 4 * c + x)
            if x == 0:
                beside = beside + coef[2, x] * low
            if x == 3:
                beside = beside + coef[1, x] * high
            write(c, x, beside)


def dot_rows(a, b):
    total = jnp.zeros((8, LANES), f32)
    for s in range(SLABS):
        total = total + jnp.sum((a[s] * b[s]).reshape(8, 8, LANES), axis=0)
    return jnp.sum(total, axis=0, keepdims=True)


def merge(u, gt, prof, mb):
    for c in range(3):
        total = u[4 * c] + u[4 * c + 1] + u[4 * c + 2] + u[4 * c + 3]
        prof[8 * c : 8 * c + 8] = jnp.sum(total.reshape(8, 8, LANES), axis=1) * (1.0 / 32.0)

    @pl.loop(0, KB // 32, unroll=4)
    def _(step):
        at = pl.multiple_of(step * 32, 32)
        totals = [jnp.zeros((32, LANES), f32)] * 3
        for g in range(GROUPS):
            b = gt[g, pl.ds(at, 32), :]
            for c in range(3):
                totals[c] = totals[c] + b * prof[8 * c + g : 8 * c + g + 1, :]
        for c in range(3):
            total = jnp.sum(totals[c], axis=1, keepdims=True)
            mb[pl.ds(c * KB + at, 32), :] = jnp.broadcast_to(total, (32, LANES))


def solve(factor, mb, sb):
    def rows_of(step, totals):
        totals = list(totals)
        for part in range(4):
            at = pl.multiple_of(step * 32 + part * 8, 8)
            m = mb[pl.ds(at, 8), :]
            for q in range(KC // LANES):
                totals[q] = totals[q] + factor[pl.ds(at, 8), LANES * q : LANES * (q + 1)] * m
        return tuple(totals)

    zero = jnp.zeros((8, LANES), f32)
    totals = lax.fori_loop(0, KC // 32, rows_of, (zero,) * (KC // LANES))
    for q in range(KC // LANES):
        row = jnp.sum(totals[q], axis=0, keepdims=True)
        sb[LANES * q : LANES * (q + 1), :] = jnp.broadcast_to(row, (LANES, LANES)).T


def solve_own(own, mb, pay):
    def rows_of(step, totals):
        totals = list(totals)
        for part in range(8):
            at = pl.multiple_of(step * 64 + part * 8, 8)
            m = mb[pl.ds(at, 8), :]
            for q in range(2):
                r = 2 * (part % 4) + q
                totals[r] = totals[r] + own[pl.ds(at, 8), LANES * q : LANES * (q + 1)] * m
        return tuple(totals)

    zero = jnp.zeros((8, LANES), f32)
    t = lax.fori_loop(0, KC // 64, rows_of, (zero,) * 8)
    pay[0] = zero
    for q in range(2):
        total = (t[q] + t[2 + q]) + (t[4 + q] + t[6 + q])
        pay[0, q : q + 1, :] = jnp.sum(total, axis=0, keepdims=True)


def unpack(pays, sb):
    for g in range(GROUPS):
        at = g * (KC // GROUPS)
        left = jnp.broadcast_to(pays[g, 0, 0:1, :], (LANES, LANES)).T
        right = jnp.broadcast_to(pays[g, 0, 1:2, :], (LANES, LANES)).T
        sb[at : at + LANES, :] = left
        sb[at + LANES : at + KC // GROUPS, :] = right[: KC // GROUPS - LANES]


def spread_over(gt, sb, spread):
    def spread_of(step, totals):
        totals = list(totals)
        for part in range(2):
            at = pl.multiple_of(step * 16 + part * 8, 8)
            solved = [sb[pl.ds(c * KB + at, 8), :] for c in range(3)]
            for g in range(GROUPS):
                b = gt[g, pl.ds(at, 8), :]
                for c in range(3):
                    totals[8 * c + g] = totals[8 * c + g] + b * solved[c]
        return tuple(totals)

    zero = jnp.zeros((8, LANES), f32)
    totals = lax.fori_loop(0, KB // 16, spread_of, (zero,) * 24)
    for r in range(24):
        spread[r : r + 1, :] = jnp.sum(totals[r], axis=0, keepdims=True)


def coarse(u, gt, factor, prof, mb, sb, spread):
    merge(u, gt, prof, mb)
    solve(factor, mb, sb)
    spread_over(gt, sb, spread)


def finish_direction(place, u, coef, spread, v, near, far, edge):
    for x in range(4):
        for c in range(3):
            s = 4 * c + x
            wide = jnp.broadcast_to(spread[8 * c : 8 * c + 8, :][:, None, :], (8, 8, LANES))
            v[s] = u[s] * coef[7, x] + wide.reshape(ROWS, LANES)
    if near is not None:
        hand_over(place, v, near, far, edge)


def hand_over(place, v, near, far, edge):
    for c in range(3):
        near[c] = v[4 * c + 3 - 3 * place[0]]
        far[c] = v[4 * c + 3 * place[0]]
    edge[...] = edge_of(lambda i: v[i], SLABS, lane_ids())


def basis_coefs(span, k):
    half = 0.5 * span
    if k == 0:
        return half, None, 1.0 / half
    return half, 0.5 * half, 2.0 / half


def local_kernel(place, force, viscosity, basis, copies, near, far, edge):
    shares = []
    for c in range(3):
        total = force[4 * c] + force[4 * c + 1] + force[4 * c + 2] + force[4 * c + 3]
        row = jnp.sum(total, axis=0, keepdims=True) * (1.0 / 32.0)
        column = jnp.broadcast_to(row, (LANES, LANES)).T
        for q in range(KB // LANES):
            part = basis[:, LANES * q : LANES * (q + 1)] * column
            shares.append(jnp.sum(part, axis=0, keepdims=True))
    rows = lax.broadcasted_iota(jnp.int32, (8, LANES), 0)
    lanes = lax.broadcasted_iota(jnp.int32, (8, LANES), 1)
    for q in range(2):
        tile = jnp.zeros((8, LANES), f32)
        for r in range(8):
            if 8 * q + r < len(shares):
                tile = jnp.where(rows == r, shares[8 * q + r], tile)
        for g in range(GROUPS):
            copies[g, q] = tile
    near[...] = viscosity[3 - 3 * place[0]]
    far[...] = viscosity[3 * place[0]]
    columns = jnp.zeros((8, LANES), f32)
    for x in range(4):
        moved = pltpu.roll(viscosity[x], 2 * x + 1, 1)
        columns = jnp.where((lanes == 2 * x) | (lanes == 2 * x + 1), moved, columns)
    edge[...] = columns


def begin_kernel(place, pays, own, vnear, vfar, enear, efar, copies, mb, pay):
    for q in range(2):
        total = tree([pays[g, q] for g in range(GROUPS)])
        for r in range(8):
            at = LANES * (8 * q + r)
            if at < KC:
                row = jnp.broadcast_to(total[r : r + 1, :], (LANES, LANES))
                mb[at : at + LANES, :] = row.T
    solve_own(own, mb, pay)
    for g in range(GROUPS):
        copies[g, 0] = pay[0]
        for i, tile in enumerate((vnear, vfar, enear, efar)):
            copies[g, 1 + i] = tile[...]


def start_kernel(place, pays, gt,
                 coef, v, near, far, edge, gram, vh, fields, sb, spread):
    unpack(pays, sb)
    for g in range(GROUPS):
        for s in range(SLABS + 4):
            fields[s, 8 * g : 8 * g + 8, :] = gt[g, KB + 8 * s : KB + 8 * s + 8, :]
        for i in range(4):
            vh[i, 8 * g : 8 * g + 8, :] = pays[g, 1 + i]
    low, high = faces_of(place, vh[0], vh[1])
    halo = merge_edges(place, vh[2], vh[3])
    store_coefs(coef, lambda x: fields[SLABS + x], low, high, halo)
    spread_over(gt, sb, spread)
    finish_direction(place, fields, coef, spread, v, near, far, edge)
    gram[...] = jnp.zeros(GRAM, f32)
    gram[0:1, :] = dot_rows(v, fields)


def inside_kernel(place, v, coef, image):
    def write(c, x, value):
        image[4 * c + x] = value

    stencil_inside(coef, v, write)


def image_kernel(place, v, near, far, edge_near, edge_far, coef, gram, inside, image, copies):
    halo = merge_edges(place, edge_near[...], edge_far[...])

    def write(c, x, value):
        image[4 * c + x] = inside[4 * c + x] - value

    stencil_beyond(coef, lambda c: faces_of(place, near[c], far[c]), halo, write)
    rows = lax.broadcasted_iota(jnp.int32, (8, LANES), 0)
    tile = jnp.where(rows == 0, gram[0:1, :], jnp.where(rows == 1, dot_rows(v, image), 0.0))
    for i in range(PLACES):
        copies[i] = tile


def merge_kernel(place, image, gt, own, pay, prof, mb):
    merge(image, gt, prof, mb)
    solve_own(own, mb, pay)


def first_kernel(place, tiles, pays, image, u0, v0, coef, gt,
                 span, u, v, near, far, edge, sb, spread):
    sums = jnp.sum(tree([tiles[i] for i in range(PLACES)]), axis=1, keepdims=True)
    width = SPAN * sums[1:2, :] / sums[0:1, :]
    span[...] = jnp.broadcast_to(width, (8, LANES))
    shift, _, scale = basis_coefs(width, 0)
    unpack(pays, sb)
    spread_over(gt, sb, spread)
    finish_direction(place, image, coef, spread, v, None, None, None)
    for s in range(SLABS):
        u[s] = (image[s] - shift * u0[s]) * scale
        v[s] = (v[s] - shift * v0[s]) * scale
    hand_over(place, v, near, far, edge)


def residual_kernel(place, span, hnear, hfar, enear, efar, coef, inside, gt, own,
                    u, pay, prof, mb):
    next_residual(place, False, span, hnear, hfar, enear, efar, coef, inside, u)
    merge(u, gt, prof, mb)
    solve_own(own, mb, pay)


def direction_kernel(place, pays, coef, gt, u, v, near, far, edge, sb, spread):
    unpack(pays, sb)
    spread_over(gt, sb, spread)
    finish_direction(place, u, coef, spread, v, near, far, edge)


def beside_kernel(k, place, span, gram_in, coef, *refs):
    refs, (gram, inside) = refs[:-2], refs[-2:]
    vs, us = refs[: k + 1], refs[k + 1 :]
    uk = us[0]
    if k:
        store_dots(gram, gram_in, vs[:-1], uk, vs[-1])
    else:
        gram[...] = gram_in[...]
    shift, back, scale = basis_coefs(span[0:1, 0:1], k)

    def write(c, x, value):
        s = 4 * c + x
        value = value - shift * uk[s]
        if k:
            value = value - back * us[1][s]
        inside[s] = value * scale

    stencil_inside(coef, vs[-1], write)


def tree(parts):
    while len(parts) > 1:
        parts = [parts[i] + parts[i + 1] for i in range(0, len(parts), 2)]
    return parts[0]


def pack_sums(gram, copies):
    sums = jnp.sum(gram[...], axis=1, keepdims=True)
    lanes = lax.broadcasted_iota(jnp.int32, (8, LANES), 1)
    tile = jnp.zeros((8, LANES), f32)
    for q in range(GRAM[0] // 8):
        tile = jnp.where(lanes == q, sums[8 * q : 8 * q + 8], tile)
    for i in range(PLACES):
        copies[i] = tile


def store_dots(gram, gram_in, vs, u, v=None):
    gram[...] = gram_in[...]
    vs = list(vs) + ([] if v is None else [v])
    totals = [jnp.zeros((8, LANES), f32)] * len(vs)
    for s in range(SLABS):
        us = u[s]
        for i, vi in enumerate(vs):
            totals[i] = totals[i] + jnp.sum((vi[s] * us).reshape(8, 8, LANES), axis=0)
    level = len(vs) - (0 if v is None else 1)
    for i, total in enumerate(totals):
        r = gram_row(i, level)
        gram[r : r + 1, :] = jnp.sum(total, axis=0, keepdims=True)


def next_residual(place, first, span, near, far, edge_near, edge_far, coef, inside, u):
    halo = merge_edges(place, edge_near[...], edge_far[...])
    scale = basis_coefs(span[0:1, 0:1], 0 if first else 1)[2]

    def write(c, x, value):
        u[4 * c + x] = inside[4 * c + x] - value * scale

    stencil_beyond(coef, lambda c: faces_of(place, near[c], far[c]), halo, write)


def step_kernel(first, place, span, hnear, hfar, enear, efar, coef, inside, gt, factor,
                u, v, near, far, edge, prof, mb, sb, spread):
    next_residual(place, first, span, hnear, hfar, enear, efar, coef, inside, u)
    coarse(u, gt, factor, prof, mb, sb, spread)
    finish_direction(place, u, coef, spread, v, near, far, edge)


def last_kernel(place, span, hnear, hfar, enear, efar, coef, inside, gram_in,
                v0, v1, v2, v3, v4, copies, u, gram):
    vs = (v0, v1, v2, v3, v4)
    next_residual(place, False, span, hnear, hfar, enear, efar, coef, inside, u)
    store_dots(gram, gram_in, vs, u)
    pack_sums(gram, copies)


def well_posed(n):
    rows = []
    good = None
    for j in range(S):
        row = []
        pivot = n[j][j]
        for i in range(j):
            value = n[i][j]
            for t in range(i):
                value = value - rows[i][t] * row[t]
            row.append(value)
            pivot = pivot - value * value / rows[i][i]
        row.append(pivot)
        apart = jnp.where(pivot > APART * n[j][j], 1.0, 0.0)
        good = apart if good is None else good * apart
        rows.append([value / rows[i][i] for i, value in enumerate(row[:j])] + [pivot])
    return good


def krylov_weights(span, sums):
    def product(i, j):
        r = gram_row(i, j)
        return sums[r // 8][r % 8 : r % 8 + 1, :]

    n = [[product(i, j) for j in range(S + 1)] for i in range(S)]
    half = 0.5 * span
    quarter = 0.5 * half

    def operate(p):
        out = [None] * (S + 1)

        def put(i, value):
            out[i] = value if out[i] is None else out[i] + value

        for j, w in enumerate(p):
            put(j, half * w)
            put(j + 1, (half if j == 0 else quarter) * w)
            if j:
                put(j - 1, quarter * w)
        return out[: len(p) + 1]

    def pair(a, b):
        total = None
        for i, ai in enumerate(a):
            part = None
            for j, bj in enumerate(b):
                term = n[i][j] * bj
                part = term if part is None else part + term
            total = ai * part if total is None else total + ai * part
        return total

    one = jnp.ones_like(span)
    r, p = [one], [one]
    x = []
    norm = n[0][0]
    for k in range(S):
        image = operate(p)
        alpha = norm / pair(p, image)
        for j, w in enumerate(p):
            if j < len(x):
                x[j] = x[j] + alpha * w
            else:
                x.append(alpha * w)
        r = [(r[j] - alpha * w) if j < len(r) else -(alpha * w) for j, w in enumerate(image)]
        if k + 1 < S:
            fresh = pair(r, r)
            beta = fresh / norm
            p = [r[j] + beta * p[j] if j < len(p) else r[j] for j in range(len(r))]
            norm = fresh
    return x, well_posed(n)


def weights_of(span, tiles):
    total = tree([tiles[i] for i in range(PLACES)])
    columns = [total[:, q : q + 1] for q in range(GRAM[0] // 8)]
    return krylov_weights(span[0:1, 0:1], columns)


def combine(x, parts, before=None):
    total = x[0] * parts[0]
    for j in range(1, S):
        total = total + x[j] * parts[j]
    return total if before is None else before + total


def combine_kernel(place, span, tiles, fields, vh,
                   v0, v1, v2, v3, v4, n0, n1, n2, n3, n4, f0, f1, f2, f3, f4,
                   en0, en1, en2, en3, en4, ef0, ef1, ef2, ef3, ef4,
                   flow, coef, u):
    x, good = weights_of(span, tiles)
    vs = (v0, v1, v2, v3, v4)
    ns, fs = (n0, n1, n2, n3, n4), (f0, f1, f2, f3, f4)
    ens, efs = (en0, en1, en2, en3, en4), (ef0, ef1, ef2, ef3, ef4)
    for s in range(SLABS):
        flow[s] = combine(x, [t[s] for t in vs])
    for c in range(3):
        flow[12 + c], flow[15 + c] = faces_of(
            place, combine(x, [t[c] for t in ns]), combine(x, [t[c] for t in fs]))
    halo = merge_edges(
        place, combine(x, [t[...] for t in ens]), combine(x, [t[...] for t in efs]))

    def thinned(viscosity, a, b, c):
        return viscosity / (1.0 + 25.0 * (a * a + b * b + c * c))

    for i in range(4):
        flow[18 + i] = thinned(fields[SLABS + i], flow[i], flow[4 + i], flow[8 + i])
    vis_low, vis_high = faces_of(place, vh[0], vh[1])
    vis_low = thinned(vis_low, flow[12], flow[13], flow[14])
    vis_high = thinned(vis_high, flow[15], flow[16], flow[17])
    second = pltpu.roll(halo, LANES - 8, 1)
    third = pltpu.roll(halo, LANES - 16, 1)
    vis_halo = thinned(merge_edges(place, vh[2], vh[3]), halo, second, third)
    store_coefs(coef, lambda i: flow[18 + i], vis_low, vis_high, vis_halo)

    def write(c, i, value):
        u[4 * c + i] = fields[4 * c + i] - value

    stencil_inside(coef, flow, write)

    def write_beyond(c, i, value):
        u[4 * c + i] = u[4 * c + i] + value

    stencil_beyond(coef, lambda c: (flow[12 + c], flow[15 + c]), halo, write_beyond)
    flow[13] = halo
    flow[14] = jnp.broadcast_to(good, EDGE)


def restart_kernel(place, u, coef, gt, factor_in, v, near, far, edge, gram, factor,
                   prof, mb, sb, spread, arrived):
    fetch = pltpu.make_async_copy(factor_in, factor, arrived)
    fetch.start()
    merge(u, gt, prof, mb)
    fetch.wait()
    solve(factor, mb, sb)
    spread_over(gt, sb, spread)
    finish_direction(place, u, coef, spread, v, near, far, edge)
    gram[...] = jnp.zeros(GRAM, f32)
    gram[0:1, :] = dot_rows(v, u)


def end_kernel(place, span, tiles, flow,
               v0, v1, v2, v3, v4, n0, n1, n2, n3, n4, f0, f1, f2, f3, f4,
               en0, en1, en2, en3, en4, ef0, ef1, ef2, ef3, ef4,
               velocity, pressure, good, vel, press):
    lanes, rows = lane_ids(), row_ids()
    x, good_now = weights_of(span, tiles)
    good[...] = jnp.broadcast_to(good_now * flow[14][0:1, 0:1], (8, LANES))
    vs = (v0, v1, v2, v3, v4)
    ns, fs = (n0, n1, n2, n3, n4), (f0, f1, f2, f3, f4)
    ens, efs = (en0, en1, en2, en3, en4), (ef0, ef1, ef2, ef3, ef4)
    at = pl.multiple_of(place[4] * 8, 8)
    for s in range(SLABS):
        vel[s] = combine(x, [t[s] for t in vs], flow[s])
    low, high = faces_of(
        place, combine(x, [t[0] for t in ns]), combine(x, [t[0] for t in fs]))
    low, high = flow[12] + low, flow[15] + high
    halo = flow[13] + merge_edges(
        place, combine(x, [t[...] for t in ens]), combine(x, [t[...] for t in efs]))
    for i in range(4):
        vis = flow[18 + i]
        up = vel[i + 1] if i < 3 else high
        down = vel[i - 1] if i else low
        w = vel[4 + i]
        yp = jnp.where(rows == ROWS - 1, 0.0, pltpu.roll(w, ROWS - 1, 0))
        ym = jnp.where(rows == 0, 0.0, pltpu.roll(w, 1, 0))
        zp, zm = along_z(vel[8 + i], halo, 8 + i, lanes)
        divergence = 0.5 * (up - down) + 0.5 * (yp - ym) + 0.5 * (zp - zm)
        press[i] = -(vis / (1.0 + vis)) * divergence
    for s in range(SLABS):
        velocity[s] = vel[s, pl.ds(at, 8), :]
    for i in range(4):
        pressure[i] = press[i, pl.ds(at, 8), :]


def call(kernel, outs, scratch, place, *args, far_away=None, beside=False):
    vmem = pl.BlockSpec(memory_space=pltpu.VMEM)
    places = [pl.BlockSpec(memory_space=pltpu.SMEM)] + [vmem] * len(args)
    if far_away is not None:
        places[1 + far_away] = pl.BlockSpec(memory_space=pl.ANY)
    cost = None
    if beside:
        size = sum(a.size for a in args)
        cost = pl.CostEstimate(flops=2 * size, bytes_accessed=4 * size, transcendentals=0)
    return pl.pallas_call(
        kernel,
        out_shape=[jax.ShapeDtypeStruct(o, f32) for o in outs],
        in_specs=places,
        out_specs=[vmem] * len(outs),
        scratch_shapes=[pltpu.VMEM(s, f32) if isinstance(s, tuple) else s for s in scratch],
        cost_estimate=cost,
        compiler_params=pltpu.CompilerParams(vmem_limit_bytes=20 * 2**20),
    )(place, *args)


MERGE = ((24, LANES), (KC, LANES))
SPREAD = ((KC, LANES), (24, LANES))
DIRECTION = (FIELD, FACE, FACE, EDGE, GRAM)


def swap_near(value, axis):
    return lax.ppermute(value, axis, [(i, i ^ 1) for i in range(lax.axis_size(axis))])


def swap_far(value, axis):
    count = lax.axis_size(axis)
    pairs = [(i, (i + 1) % count) for i in range(1, count, 2)]
    return lax.ppermute(value, axis, pairs + [(b, a) for a, b in pairs])


def swapped(near, far, edge):
    return (
        swap_far(far, "cap"),
        swap_near(near, "cap"),
        swap_far(edge, "sub"),
        swap_near(edge, "sub"),
    )


def ordered(pieces):
    far_face, near_face, far_edge, near_edge = pieces
    return near_face, far_face, near_edge, far_edge


def shared(copies):
    return lax.all_to_all(copies, ("cap", "sub"), 0, 0)


def exchanged(pay):
    copies = jnp.broadcast_to(pay[None], (GROUPS,) + pay.shape)
    return lax.all_to_all(copies, "grp", 0, 0)


def body(right_side, viscosity, coarse_basis, coarse_factor):
    cap, sub = lax.axis_index("cap"), lax.axis_index("sub")
    caps, subs = lax.axis_size("cap"), lax.axis_size("sub")
    place = jnp.stack([
        cap % 2, (cap != 0) & (cap != caps - 1),
        sub % 2, (sub != 0) & (sub != subs - 1),
        lax.axis_index("grp"),
    ]).astype(jnp.int32)
    basis = coarse_basis[0, 0]
    force = right_side.reshape(SLABS, 8, LANES)
    own_gt = jnp.concatenate(
        [basis.T.reshape(KB // 8, 8, LANES), force, viscosity], axis=0)
    gt = lax.all_gather(own_gt, "grp", axis=0).reshape(GROUPS, -1, LANES)

    copies, near, far, edge = call(
        local_kernel, ((GROUPS, 2, 8, LANES),) + ((8, LANES),) * 3, (),
        place, force, viscosity, basis)
    vhalos = ordered(swapped(near, far, edge))
    vhalos, rows, _ = lax.optimization_barrier((vhalos, coarse_factor[0, 0], own_gt))
    factor = gathered = lax.all_gather(rows, "grp", axis=0, tiled=True)
    own = jnp.pad(coarse_factor[0, 0].T, ((0, 0), (0, 2 * LANES - KC // GROUPS)))
    (copies,) = call(
        begin_kernel, ((GROUPS, 5, 8, LANES),), ((KC, LANES), (1, 8, LANES)),
        place, lax.all_to_all(copies, "grp", 0, 0), own, *vhalos)
    coef, v, near, far, edge, gram, vh, fields = call(
        start_kernel,
        (COEF,) + DIRECTION + ((4, ROWS, LANES), (SLABS + 4, ROWS, LANES)), SPREAD,
        place, lax.all_to_all(copies, "grp", 0, 0), gt)
    u = fields
    for picard in range(2):
        us, vs, halos = [u], [v], []
        for k in range(S):
            beyond = ordered(swapped(near, far, edge))
            if picard == 0 and k == 0:
                (inside,) = call(inside_kernel, (FIELD,), (), place, v, coef, beside=True)
            else:
                gram, inside = call(
                    functools.partial(beside_kernel, k), (GRAM, FIELD), (),
                    place, span, gram, coef, *vs, *us[::-1][:2], beside=True)
            beyond, gram, inside = lax.optimization_barrier((beyond, gram, inside))
            halos.append(beyond)
            if k + 1 == S:
                (copies,) = call(
                    last_kernel, ((PLACES, 8, LANES),), (FIELD, GRAM),
                    place, span, *beyond, coef, inside, gram, *vs)
                break
            if picard == 0 and k == 0:
                image, copies = call(
                    image_kernel, (FIELD, (PLACES, 8, LANES)), (),
                    place, v, *beyond, coef, gram, inside)
                (pay,) = call(
                    merge_kernel, ((1, 8, LANES),), MERGE, place, image, gt, own, beside=True)
                span, u, v, near, far, edge = call(
                    first_kernel, ((8, LANES), FIELD) + DIRECTION[:4], SPREAD,
                    place, shared(copies), exchanged(pay), image, u, v, coef, gt)
            elif picard == 0:
                u, pay = call(
                    residual_kernel, (FIELD, (1, 8, LANES)), MERGE,
                    place, span, *beyond, coef, inside, gt, own)
                v, near, far, edge = call(
                    direction_kernel, DIRECTION[:4], SPREAD,
                    place, exchanged(pay), coef, gt, u)
            else:
                u, v, near, far, edge = call(
                    functools.partial(step_kernel, k == 0), (FIELD,) + DIRECTION[:4],
                    MERGE + SPREAD, place, span, *beyond, coef, inside, gt, factor)
            us.append(u)
            vs.append(v)
        tiles = shared(copies)
        kept = vs + [h[side] for side in range(4) for h in halos]
        if picard == 0:
            flow, coef, u = call(
                combine_kernel, (FLOW, COEF, FIELD), (), place, span, tiles, fields, vh, *kept)
            v, near, far, edge, gram, factor = call(
                restart_kernel, DIRECTION + ((KC, KC),),
                MERGE + SPREAD + (pltpu.SemaphoreType.DMA(()),),
                place, u, coef, gt, factor, far_away=3)
        else:
            result, pressure, good = call(
                end_kernel, ((SLABS, 8, LANES), (4, 8, LANES), (8, LANES)),
                (FIELD, (4, ROWS, LANES)), place, span, tiles, flow, *kept)
    return lax.cond(
        good[0, 0] > 0.5,
        lambda *_: (result.reshape(3, 4, 8, LANES), pressure),
        stepwise,
        right_side, viscosity, coarse_basis, gathered)


exact_mode = lax.Precision.HIGHEST


def padded_2(block, sides, width):
    for axis, dim in sides:
        count = lax.axis_size(axis)
        forward = [(i, i + 1) for i in range(count - 1)]
        backward = [(target, source) for source, target in forward]
        low = lax.ppermute(
            lax.slice_in_dim(block, block.shape[dim] - width, None, axis=dim), axis, forward
        )
        high = lax.ppermute(lax.slice_in_dim(block, 0, width, axis=dim), axis, backward)
        block = jnp.concatenate([low, block, high], axis=dim)
    return block


def stencil_faces(padded):
    centre = padded[1:-1, 1:-1, 1:-1]
    faces = (
        0.5 * (centre + padded[2:, 1:-1, 1:-1]),
        0.5 * (centre + padded[:-2, 1:-1, 1:-1]),
        0.5 * (centre + padded[1:-1, 2:, 1:-1]),
        0.5 * (centre + padded[1:-1, :-2, 1:-1]),
        0.5 * (centre + padded[1:-1, 1:-1, 2:]),
        0.5 * (centre + padded[1:-1, 1:-1, :-2]),
    )
    diagonal = 1.0 + faces[0] + faces[1] + faces[2] + faces[3] + faces[4] + faces[5]
    return (faces, diagonal)


def apply_stencil(padded_field, field, faces, diagonal):
    beside = (
        faces[0] * padded_field[:, 2:, 1:-1, 1:-1] + faces[1] * padded_field[:, :-2, 1:-1, 1:-1]
    )
    beside = (
        beside
        + faces[2] * padded_field[:, 1:-1, 2:, 1:-1]
        + faces[3] * padded_field[:, 1:-1, :-2, 1:-1]
    )
    beside = (
        beside
        + faces[4] * padded_field[:, 1:-1, 1:-1, 2:]
        + faces[5] * padded_field[:, 1:-1, 1:-1, :-2]
    )
    return diagonal * field - beside


def divergence_of(padded_field):
    result = 0.5 * (padded_field[0, 2:, 1:-1, 1:-1] - padded_field[0, :-2, 1:-1, 1:-1])
    result = result + 0.5 * (padded_field[1, 1:-1, 2:, 1:-1] - padded_field[1, 1:-1, :-2, 1:-1])
    return result + 0.5 * (padded_field[2, 1:-1, 1:-1, 2:] - padded_field[2, 1:-1, 1:-1, :-2])


def velocity_padded(field):
    return padded_2(field, (("cap", 1), ("grp", 2), ("sub", 3)), 1)


def curvature_sum(direction, image):
    return lax.psum(jnp.sum(direction * image), ("cap", "grp", "sub"))


def norm_sum(residual, precond):
    return lax.psum(jnp.sum(residual * precond), ("cap", "grp", "sub"))


def stepwise(right_side, viscosity, coarse_basis, whole_factor):
    basis_local = coarse_basis[0, 0]

    def precondition(residual, diagonal):
        profile = jnp.mean(residual, axis=(1, 2))
        local = jnp.dot(profile, basis_local, precision=exact_mode)
        merged = lax.psum(local, "grp").reshape(-1)
        solved = jnp.dot(whole_factor, merged, precision=exact_mode)
        spread = jnp.dot(solved.reshape(3, -1), basis_local.T, precision=exact_mode)
        return residual / diagonal + spread[:, None, None, :]

    velocity = jnp.zeros_like(right_side)
    viscous = viscosity
    for picard in range(2):
        if picard > 0:
            viscous = viscosity / (1.0 + 25.0 * jnp.sum(velocity * velocity, axis=0))
        padded_viscous = padded_2(viscous, (("cap", 0), ("grp", 1), ("sub", 2)), 1)
        faces, diagonal = stencil_faces(padded_viscous)

        def operate(field):
            return apply_stencil(velocity_padded(field), field, faces, diagonal)

        residual = right_side - operate(velocity)
        precond = precondition(residual, diagonal)
        norm_now = norm_sum(residual, precond)
        direction = precond
        for krylov_step in range(S):
            image = operate(direction)
            alpha = norm_now / curvature_sum(direction, image)
            velocity = velocity + alpha * direction
            residual = residual - alpha * image
            if krylov_step + 1 < S:
                precond = precondition(residual, diagonal)
                fresh = norm_sum(residual, precond)
                direction = precond + fresh / norm_now * direction
                norm_now = fresh
    pressure = -(viscous / (1.0 + viscous)) * divergence_of(velocity_padded(velocity))
    return (velocity, pressure)


def solution(mesh):
    placed = (
        P(None, "cap", "grp", "sub"),
        P("cap", "grp", "sub"),
        P("cap", "grp", "sub", None),
        P("cap", "sub", "grp", None),
    )
    return jax.shard_map(
        body,
        mesh=mesh,
        in_specs=placed,
        out_specs=(P(None, "cap", "grp", "sub"), P("cap", "grp", "sub")),
        check_vma=False,
    )
```

```python
import functools

import jax
import jax.numpy as jnp
from jax import lax
from jax.experimental import pallas as pl
from jax.experimental.pallas import tpu as pltpu
from jax.sharding import PartitionSpec as P

S = 5
SLABS = 12
ROWS = 64
LANES = 128
GROUPS = 8
KB = 512
KC = 1536
APART = 1e-3
SPAN = 2.6
FIELD = (SLABS, ROWS, LANES)
FACE = (3, ROWS, LANES)
EDGE = (ROWS, LANES)
GRAM = (24, LANES)
PLACES = 32
FLOW = (22, ROWS, LANES)
COEF = (9, 4, ROWS, LANES)
f32 = jnp.float32


def gram_row(i, j):
    i, j = min(i, j), max(i, j)
    return sum(min(t, S - 1) + 1 for t in range(j)) + i


def lane_ids():
    return lax.broadcasted_iota(jnp.int32, (ROWS, LANES), 1)


def row_ids():
    return lax.broadcasted_iota(jnp.int32, (ROWS, LANES), 0)


def ends_of(halo, i):
    return pltpu.roll(halo, LANES - 1 - 2 * i, 1)


def along_z(w, halo, i, lanes):
    ends = ends_of(halo, i)
    after = jnp.where(lanes == LANES - 1, ends, pltpu.roll(w, LANES - 1, 1))
    before = jnp.where(lanes == 0, ends, pltpu.roll(w, 1, 1))
    return after, before


def flag(place, i):
    return jnp.full((ROWS, LANES), place[i], jnp.int32) == 1


def faces_of(place, near, far):
    odd, inner = flag(place, 0), flag(place, 1)
    far = jnp.where(inner, far, 0.0)
    return jnp.where(odd, near, far), jnp.where(odd, far, near)


def merge_edges(place, near, far):
    far = jnp.where(flag(place, 3), far, 0.0)
    odd = flag(place, 2)
    low, high = jnp.where(odd, near, far), jnp.where(odd, far, near)
    return jnp.where(lane_ids() % 2 == 1, pltpu.roll(low, 1, 1), pltpu.roll(high, LANES - 1, 1))


def edge_of(get, count, lanes):
    edge = jnp.zeros((ROWS, LANES), f32)
    for i in range(count):
        moved = pltpu.roll(get(i), 2 * i + 1, 1)
        edge = jnp.where((lanes == 2 * i) | (lanes == 2 * i + 1), moved, edge)
    return edge


def store_coefs(coef, vis, low, high, halo):
    lanes, rows = lane_ids(), row_ids()
    for x in range(4):
        v = vis(x)
        up = vis(x + 1) if x < 3 else high
        down = vis(x - 1) if x else low
        yp = jnp.where(rows == ROWS - 1, 0.0, pltpu.roll(v, ROWS - 1, 0))
        ym = jnp.where(rows == 0, 0.0, pltpu.roll(v, 1, 0))
        zp, zm = along_z(v, halo, x, lanes)
        faces = [0.5 * (v + n) for n in (up, down, yp, ym, zp, zm)]
        diagonal = 1.0 + faces[0] + faces[1] + faces[2] + faces[3] + faces[4] + faces[5]
        faces[2] = jnp.where(rows == ROWS - 1, 0.0, faces[2])
        faces[3] = jnp.where(rows == 0, 0.0, faces[3])
        first, last = lanes == 0, lanes == LANES - 1
        coef[8, x] = jnp.where(first, faces[5], jnp.where(last, faces[4], 0.0))
        faces[4] = jnp.where(last, 0.0, faces[4])
        faces[5] = jnp.where(first, 0.0, faces[5])
        coef[0, x] = diagonal
        for f in range(6):
            coef[1 + f, x] = faces[f]
        coef[7, x] = 1.0 / diagonal


def stencil_inside(coef, field, write):
    for x in range(4):
        for c in range(3):
            w = field[4 * c + x]
            beside = coef[3, x] * pltpu.roll(w, ROWS - 1, 0) + coef[4, x] * pltpu.roll(w, 1, 0)
            beside = beside + coef[5, x] * pltpu.roll(w, LANES - 1, 1)
            beside = beside + coef[6, x] * pltpu.roll(w, 1, 1)
            if x < 3:
                beside = beside + coef[1, x] * field[4 * c + x + 1]
            if x:
                beside = beside + coef[2, x] * field[4 * c + x - 1]
            write(c, x, coef[0, x] * w - beside)


def stencil_beyond(coef, sides, halo, write):
    for c in range(3):
        low, high = sides(c)
        for x in range(4):
            beside = coef[8, x] * ends_of(halo, 4 * c + x)
            if x == 0:
                beside = beside + coef[2, x] * low
            if x == 3:
                beside = beside + coef[1, x] * high
            write(c, x, beside)


def dot_rows(a, b):
    total = jnp.zeros((8, LANES), f32)
    for s in range(SLABS):
        total = total + jnp.sum((a[s] * b[s]).reshape(8, 8, LANES), axis=0)
    return jnp.sum(total, axis=0, keepdims=True)


def merge(u, gt, prof, mb):
    for c in range(3):
        total = u[4 * c] + u[4 * c + 1] + u[4 * c + 2] + u[4 * c + 3]
        prof[8 * c : 8 * c + 8] = jnp.sum(total.reshape(8, 8, LANES), axis=1) * (1.0 / 32.0)

    @pl.loop(0, KB // 32, unroll=8)
    def _(step):
        at = pl.multiple_of(step * 32, 32)
        totals = [jnp.zeros((32, LANES), f32)] * 3
        for g in range(GROUPS):
            b = gt[g, pl.ds(at, 32), :]
            for c in range(3):
                totals[c] = totals[c] + b * prof[8 * c + g : 8 * c + g + 1, :]
        for c in range(3):
            total = jnp.sum(totals[c], axis=1, keepdims=True)
            mb[pl.ds(c * KB + at, 32), :] = jnp.broadcast_to(total, (32, LANES))


def solve(factor, mb, sb):
    def rows_of(step, totals):
        totals = list(totals)
        for part in range(16):
            at = pl.multiple_of(step * 128 + part * 8, 8)
            m = mb[pl.ds(at, 8), :]
            for q in range(KC // LANES):
                totals[q] = totals[q] + factor[pl.ds(at, 8), LANES * q : LANES * (q + 1)] * m
        return tuple(totals)

    zero = jnp.zeros((8, LANES), f32)
    totals = lax.fori_loop(0, KC // 128, rows_of, (zero,) * (KC // LANES))
    for q in range(KC // LANES):
        row = jnp.sum(totals[q], axis=0, keepdims=True)
        sb[LANES * q : LANES * (q + 1), :] = jnp.broadcast_to(row, (LANES, LANES)).T


def solve_own(own, mb, pay):
    def rows_of(step, totals):
        totals = list(totals)
        for part in range(32):
            at = pl.multiple_of(step * 256 + part * 8, 8)
            m = mb[pl.ds(at, 8), :]
            for q in range(2):
                r = 2 * (part % 4) + q
                totals[r] = totals[r] + own[pl.ds(at, 8), LANES * q : LANES * (q + 1)] * m
        return tuple(totals)

    zero = jnp.zeros((8, LANES), f32)
    t = lax.fori_loop(0, KC // 256, rows_of, (zero,) * 8)
    pay[0] = zero
    for q in range(2):
        total = (t[q] + t[2 + q]) + (t[4 + q] + t[6 + q])
        pay[0, q : q + 1, :] = jnp.sum(total, axis=0, keepdims=True)


def unpack(pays, sb):
    for g in range(GROUPS):
        at = g * (KC // GROUPS)
        left = jnp.broadcast_to(pays[g, 0, 0:1, :], (LANES, LANES)).T
        right = jnp.broadcast_to(pays[g, 0, 1:2, :], (LANES, LANES)).T
        sb[at : at + LANES, :] = left
        sb[at + LANES : at + KC // GROUPS, :] = right[: KC // GROUPS - LANES]


def spread_over(gt, sb, spread):
    def spread_of(step, totals):
        totals = list(totals)
        for part in range(8):
            at = pl.multiple_of(step * 64 + part * 8, 8)
            solved = [sb[pl.ds(c * KB + at, 8), :] for c in range(3)]
            for g in range(GROUPS):
                b = gt[g, pl.ds(at, 8), :]
                for c in range(3):
                    totals[8 * c + g] = totals[8 * c + g] + b * solved[c]
        return tuple(totals)

    zero = jnp.zeros((8, LANES), f32)
    totals = lax.fori_loop(0, KB // 64, spread_of, (zero,) * 24)
    for r in range(24):
        spread[r : r + 1, :] = jnp.sum(totals[r], axis=0, keepdims=True)


def coarse(u, gt, factor, prof, mb, sb, spread):
    merge(u, gt, prof, mb)
    solve(factor, mb, sb)
    spread_over(gt, sb, spread)


def finish_direction(place, u, coef, spread, v, near, far, edge):
    for x in range(4):
        for c in range(3):
            s = 4 * c + x
            wide = jnp.broadcast_to(spread[8 * c : 8 * c + 8, :][:, None, :], (8, 8, LANES))
            v[s] = u[s] * coef[7, x] + wide.reshape(ROWS, LANES)
    if near is not None:
        hand_over(place, v, near, far, edge)


def hand_over(place, v, near, far, edge):
    for c in range(3):
        near[c] = v[4 * c + 3 - 3 * place[0]]
        far[c] = v[4 * c + 3 * place[0]]
    edge[...] = edge_of(lambda i: v[i], SLABS, lane_ids())


def basis_coefs(span, k):
    half = 0.5 * span
    if k == 0:
        return half, None, 1.0 / half
    return half, 0.5 * half, 2.0 / half


def local_kernel(place, force, viscosity, basis, copies, near, far, edge):
    shares = []
    for c in range(3):
        total = force[4 * c] + force[4 * c + 1] + force[4 * c + 2] + force[4 * c + 3]
        row = jnp.sum(total, axis=0, keepdims=True) * (1.0 / 32.0)
        column = jnp.broadcast_to(row, (LANES, LANES)).T
        for q in range(KB // LANES):
            part = basis[:, LANES * q : LANES * (q + 1)] * column
            shares.append(jnp.sum(part, axis=0, keepdims=True))
    rows = lax.broadcasted_iota(jnp.int32, (8, LANES), 0)
    lanes = lax.broadcasted_iota(jnp.int32, (8, LANES), 1)
    for q in range(2):
        tile = jnp.zeros((8, LANES), f32)
        for r in range(8):
            if 8 * q + r < len(shares):
                tile = jnp.where(rows == r, shares[8 * q + r], tile)
        for g in range(GROUPS):
            copies[g, q] = tile
    near[...] = viscosity[3 - 3 * place[0]]
    far[...] = viscosity[3 * place[0]]
    columns = jnp.zeros((8, LANES), f32)
    for x in range(4):
        moved = pltpu.roll(viscosity[x], 2 * x + 1, 1)
        columns = jnp.where((lanes == 2 * x) | (lanes == 2 * x + 1), moved, columns)
    edge[...] = columns


def begin_kernel(place, pays, own, vnear, vfar, enear, efar, copies, mb, pay):
    for q in range(2):
        total = tree([pays[g, q] for g in range(GROUPS)])
        for r in range(8):
            at = LANES * (8 * q + r)
            if at < KC:
                row = jnp.broadcast_to(total[r : r + 1, :], (LANES, LANES))
                mb[at : at + LANES, :] = row.T
    solve_own(own, mb, pay)
    for g in range(GROUPS):
        copies[g, 0] = pay[0]
        for i, tile in enumerate((vnear, vfar, enear, efar)):
            copies[g, 1 + i] = tile[...]


def start_kernel(place, pays, whole,
                 coef, v, near, far, edge, gram, vh, fields, gt, sb, spread, arrived):
    copy = pltpu.make_async_copy(whole.at[:, pl.ds(0, KB)], gt, arrived)
    copy.start()
    unpack(pays, sb)
    for g in range(GROUPS):
        for s in range(SLABS + 4):
            fields[s, 8 * g : 8 * g + 8, :] = whole[g, KB + 8 * s : KB + 8 * s + 8, :]
        for i in range(4):
            vh[i, 8 * g : 8 * g + 8, :] = pays[g, 1 + i]
    low, high = faces_of(place, vh[0], vh[1])
    halo = merge_edges(place, vh[2], vh[3])
    store_coefs(coef, lambda x: fields[SLABS + x], low, high, halo)
    copy.wait()
    spread_over(gt, sb, spread)
    finish_direction(place, fields, coef, spread, v, near, far, edge)
    gram[...] = jnp.zeros(GRAM, f32)
    gram[0:1, :] = dot_rows(v, fields)


def inside_kernel(place, v, coef, image):
    def write(c, x, value):
        image[4 * c + x] = value

    stencil_inside(coef, v, write)


def image_kernel(place, v, near, far, edge_near, edge_far, coef, gram, inside, image, copies):
    halo = merge_edges(place, edge_near[...], edge_far[...])

    def write(c, x, value):
        image[4 * c + x] = inside[4 * c + x] - value

    stencil_beyond(coef, lambda c: faces_of(place, near[c], far[c]), halo, write)
    rows = lax.broadcasted_iota(jnp.int32, (8, LANES), 0)
    tile = jnp.where(rows == 0, gram[0:1, :], jnp.where(rows == 1, dot_rows(v, image), 0.0))
    for i in range(PLACES):
        copies[i] = tile


def merge_kernel(place, image, gt, own, pay, prof, mb):
    merge(image, gt, prof, mb)
    solve_own(own, mb, pay)


def first_kernel(place, tiles, pays, image, u0, v0, coef, gt,
                 span, u, v, near, far, edge, sb, spread):
    sums = jnp.sum(tree([tiles[i] for i in range(PLACES)]), axis=1, keepdims=True)
    width = SPAN * sums[1:2, :] / sums[0:1, :]
    span[...] = jnp.broadcast_to(width, (8, LANES))
    shift, _, scale = basis_coefs(width, 0)
    unpack(pays, sb)
    spread_over(gt, sb, spread)
    finish_direction(place, image, coef, spread, v, None, None, None)
    for s in range(SLABS):
        u[s] = (image[s] - shift * u0[s]) * scale
        v[s] = (v[s] - shift * v0[s]) * scale
    hand_over(place, v, near, far, edge)


def residual_kernel(place, span, hnear, hfar, enear, efar, coef, inside, gt, own,
                    u, pay, prof, mb):
    next_residual(place, False, span, hnear, hfar, enear, efar, coef, inside, u)
    merge(u, gt, prof, mb)
    solve_own(own, mb, pay)


def direction_kernel(place, pays, coef, gt, u, v, near, far, edge, sb, spread):
    unpack(pays, sb)
    spread_over(gt, sb, spread)
    finish_direction(place, u, coef, spread, v, near, far, edge)


def beside_kernel(k, place, span, gram_in, coef, *refs):
    refs, (gram, inside) = refs[:-2], refs[-2:]
    vs, us = refs[: k + 1], refs[k + 1 :]
    uk = us[0]
    if k:
        store_dots(gram, gram_in, vs[:-1], uk, vs[-1])
    else:
        gram[...] = gram_in[...]
    shift, back, scale = basis_coefs(span[0:1, 0:1], k)

    def write(c, x, value):
        s = 4 * c + x
        value = value - shift * uk[s]
        if k:
            value = value - back * us[1][s]
        inside[s] = value * scale

    stencil_inside(coef, vs[-1], write)


def tree(parts):
    while len(parts) > 1:
        parts = [parts[i] + parts[i + 1] for i in range(0, len(parts), 2)]
    return parts[0]


def pack_sums(gram, copies):
    sums = jnp.sum(gram[...], axis=1, keepdims=True)
    lanes = lax.broadcasted_iota(jnp.int32, (8, LANES), 1)
    tile = jnp.zeros((8, LANES), f32)
    for q in range(GRAM[0] // 8):
        tile = jnp.where(lanes == q, sums[8 * q : 8 * q + 8], tile)
    for i in range(PLACES):
        copies[i] = tile


def store_dots(gram, gram_in, vs, u, v=None):
    gram[...] = gram_in[...]
    vs = list(vs) + ([] if v is None else [v])
    totals = [jnp.zeros((8, LANES), f32)] * len(vs)
    for s in range(SLABS):
        us = u[s]
        for i, vi in enumerate(vs):
            totals[i] = totals[i] + jnp.sum((vi[s] * us).reshape(8, 8, LANES), axis=0)
    level = len(vs) - (0 if v is None else 1)
    for i, total in enumerate(totals):
        r = gram_row(i, level)
        gram[r : r + 1, :] = jnp.sum(total, axis=0, keepdims=True)


def next_residual(place, first, span, near, far, edge_near, edge_far, coef, inside, u):
    halo = merge_edges(place, edge_near[...], edge_far[...])
    scale = basis_coefs(span[0:1, 0:1], 0 if first else 1)[2]

    def write(c, x, value):
        u[4 * c + x] = inside[4 * c + x] - value * scale

    stencil_beyond(coef, lambda c: faces_of(place, near[c], far[c]), halo, write)


def step_kernel(first, place, span, hnear, hfar, enear, efar, coef, inside, gt, factor,
                u, v, near, far, edge, prof, mb, sb, spread):
    next_residual(place, first, span, hnear, hfar, enear, efar, coef, inside, u)
    coarse(u, gt, factor, prof, mb, sb, spread)
    finish_direction(place, u, coef, spread, v, near, far, edge)


def last_kernel(place, span, hnear, hfar, enear, efar, coef, inside, gram_in,
                v0, v1, v2, v3, v4, copies, u, gram):
    vs = (v0, v1, v2, v3, v4)
    next_residual(place, False, span, hnear, hfar, enear, efar, coef, inside, u)
    store_dots(gram, gram_in, vs, u)
    pack_sums(gram, copies)


def well_posed(n):
    rows = []
    good = None
    for j in range(S):
        row = []
        pivot = n[j][j]
        for i in range(j):
            value = n[i][j]
            for t in range(i):
                value = value - rows[i][t] * row[t]
            row.append(value)
            pivot = pivot - value * value / rows[i][i]
        row.append(pivot)
        apart = jnp.where(pivot > APART * n[j][j], 1.0, 0.0)
        good = apart if good is None else good * apart
        rows.append([value / rows[i][i] for i, value in enumerate(row[:j])] + [pivot])
    return good


def krylov_weights(span, sums):
    def product(i, j):
        r = gram_row(i, j)
        return sums[r // 8][r % 8 : r % 8 + 1, :]

    n = [[product(i, j) for j in range(S + 1)] for i in range(S)]
    half = 0.5 * span
    quarter = 0.5 * half

    def operate(p):
        out = [None] * (S + 1)

        def put(i, value):
            out[i] = value if out[i] is None else out[i] + value

        for j, w in enumerate(p):
            put(j, half * w)
            put(j + 1, (half if j == 0 else quarter) * w)
            if j:
                put(j - 1, quarter * w)
        return out[: len(p) + 1]

    def pair(a, b):
        total = None
        for i, ai in enumerate(a):
            part = None
            for j, bj in enumerate(b):
                term = n[i][j] * bj
                part = term if part is None else part + term
            total = ai * part if total is None else total + ai * part
        return total

    one = jnp.ones_like(span)
    r, p = [one], [one]
    x = []
    norm = n[0][0]
    for k in range(S):
        image = operate(p)
        alpha = norm / pair(p, image)
        for j, w in enumerate(p):
            if j < len(x):
                x[j] = x[j] + alpha * w
            else:
                x.append(alpha * w)
        r = [(r[j] - alpha * w) if j < len(r) else -(alpha * w) for j, w in enumerate(image)]
        if k + 1 < S:
            fresh = pair(r, r)
            beta = fresh / norm
            p = [r[j] + beta * p[j] if j < len(p) else r[j] for j in range(len(r))]
            norm = fresh
    return x, well_posed(n)


def weights_of(span, tiles):
    total = tree([tiles[i] for i in range(PLACES)])
    columns = [total[:, q : q + 1] for q in range(GRAM[0] // 8)]
    return krylov_weights(span[0:1, 0:1], columns)


def combine(x, parts, before=None):
    total = x[0] * parts[0]
    for j in range(1, S):
        total = total + x[j] * parts[j]
    return total if before is None else before + total


def combine_kernel(place, span, tiles, fields, vh,
                   v0, v1, v2, v3, v4, n0, n1, n2, n3, n4, f0, f1, f2, f3, f4,
                   en0, en1, en2, en3, en4, ef0, ef1, ef2, ef3, ef4,
                   flow, coef, u):
    x, good = weights_of(span, tiles)
    vs = (v0, v1, v2, v3, v4)
    ns, fs = (n0, n1, n2, n3, n4), (f0, f1, f2, f3, f4)
    ens, efs = (en0, en1, en2, en3, en4), (ef0, ef1, ef2, ef3, ef4)
    for s in range(SLABS):
        flow[s] = combine(x, [t[s] for t in vs])
    for c in range(3):
        flow[12 + c], flow[15 + c] = faces_of(
            place, combine(x, [t[c] for t in ns]), combine(x, [t[c] for t in fs]))
    halo = merge_edges(
        place, combine(x, [t[...] for t in ens]), combine(x, [t[...] for t in efs]))

    def thinned(viscosity, a, b, c):
        return viscosity / (1.0 + 25.0 * (a * a + b * b + c * c))

    for i in range(4):
        flow[18 + i] = thinned(fields[SLABS + i], flow[i], flow[4 + i], flow[8 + i])
    vis_low, vis_high = faces_of(place, vh[0], vh[1])
    vis_low = thinned(vis_low, flow[12], flow[13], flow[14])
    vis_high = thinned(vis_high, flow[15], flow[16], flow[17])
    second = pltpu.roll(halo, LANES - 8, 1)
    third = pltpu.roll(halo, LANES - 16, 1)
    vis_halo = thinned(merge_edges(place, vh[2], vh[3]), halo, second, third)
    store_coefs(coef, lambda i: flow[18 + i], vis_low, vis_high, vis_halo)

    def write(c, i, value):
        u[4 * c + i] = fields[4 * c + i] - value

    stencil_inside(coef, flow, write)

    def write_beyond(c, i, value):
        u[4 * c + i] = u[4 * c + i] + value

    stencil_beyond(coef, lambda c: (flow[12 + c], flow[15 + c]), halo, write_beyond)
    flow[13] = halo
    flow[14] = jnp.broadcast_to(good, EDGE)


def restart_kernel(place, u, coef, gt, factor_in, v, near, far, edge, gram, factor,
                   prof, mb, sb, spread, arrived):
    fetch = pltpu.make_async_copy(factor_in, factor, arrived)
    fetch.start()
    merge(u, gt, prof, mb)
    fetch.wait()
    solve(factor, mb, sb)
    spread_over(gt, sb, spread)
    finish_direction(place, u, coef, spread, v, near, far, edge)
    gram[...] = jnp.zeros(GRAM, f32)
    gram[0:1, :] = dot_rows(v, u)


def end_kernel(place, span, tiles, flow,
               v0, v1, v2, v3, v4, n0, n1, n2, n3, n4, f0, f1, f2, f3, f4,
               en0, en1, en2, en3, en4, ef0, ef1, ef2, ef3, ef4,
               velocity, pressure, good, vel, press):
    lanes, rows = lane_ids(), row_ids()
    x, good_now = weights_of(span, tiles)
    good[...] = jnp.broadcast_to(good_now * flow[14][0:1, 0:1], (8, LANES))
    vs = (v0, v1, v2, v3, v4)
    ns, fs = (n0, n1, n2, n3, n4), (f0, f1, f2, f3, f4)
    ens, efs = (en0, en1, en2, en3, en4), (ef0, ef1, ef2, ef3, ef4)
    at = pl.multiple_of(place[4] * 8, 8)
    for s in range(SLABS):
        vel[s] = combine(x, [t[s] for t in vs], flow[s])
    low, high = faces_of(
        place, combine(x, [t[0] for t in ns]), combine(x, [t[0] for t in fs]))
    low, high = flow[12] + low, flow[15] + high
    halo = flow[13] + merge_edges(
        place, combine(x, [t[...] for t in ens]), combine(x, [t[...] for t in efs]))
    for i in range(4):
        vis = flow[18 + i]
        up = vel[i + 1] if i < 3 else high
        down = vel[i - 1] if i else low
        w = vel[4 + i]
        yp = jnp.where(rows == ROWS - 1, 0.0, pltpu.roll(w, ROWS - 1, 0))
        ym = jnp.where(rows == 0, 0.0, pltpu.roll(w, 1, 0))
        zp, zm = along_z(vel[8 + i], halo, 8 + i, lanes)
        divergence = 0.5 * (up - down) + 0.5 * (yp - ym) + 0.5 * (zp - zm)
        press[i] = -(vis / (1.0 + vis)) * divergence
    for s in range(SLABS):
        velocity[s] = vel[s, pl.ds(at, 8), :]
    for i in range(4):
        pressure[i] = press[i, pl.ds(at, 8), :]


def call(kernel, outs, scratch, place, *args, far_away=None, beside=False):
    vmem = pl.BlockSpec(memory_space=pltpu.VMEM)
    places = [pl.BlockSpec(memory_space=pltpu.SMEM)] + [vmem] * len(args)
    if far_away is not None:
        places[1 + far_away] = pl.BlockSpec(memory_space=pl.ANY)
    cost = None
    if beside:
        size = sum(a.size for a in args)
        cost = pl.CostEstimate(flops=2 * size, bytes_accessed=4 * size, transcendentals=0)
    return pl.pallas_call(
        kernel,
        out_shape=[jax.ShapeDtypeStruct(o, f32) for o in outs],
        in_specs=places,
        out_specs=[vmem] * len(outs),
        scratch_shapes=[pltpu.VMEM(s, f32) if isinstance(s, tuple) else s for s in scratch],
        cost_estimate=cost,
        compiler_params=pltpu.CompilerParams(vmem_limit_bytes=20 * 2**20),
    )(place, *args)


MERGE = ((24, LANES), (KC, LANES))
SPREAD = ((KC, LANES), (24, LANES))
DIRECTION = (FIELD, FACE, FACE, EDGE, GRAM)


def swap_near(value, axis):
    return lax.ppermute(value, axis, [(i, i ^ 1) for i in range(lax.axis_size(axis))])


def swap_far(value, axis):
    count = lax.axis_size(axis)
    pairs = [(i, (i + 1) % count) for i in range(1, count, 2)]
    return lax.ppermute(value, axis, pairs + [(b, a) for a, b in pairs])


def swapped(near, far, edge):
    near_face = swap_near(near, "cap")
    far_face = swap_far(far, "cap")
    near_edge = swap_near(edge, "sub")
    far_edge = swap_far(edge, "sub")
    return near_face, far_face, near_edge, far_edge


def shared(copies):
    return lax.all_to_all(copies, ("cap", "sub"), 0, 0)


def exchanged(pay):
    copies = jnp.broadcast_to(pay[None], (GROUPS,) + pay.shape)
    return lax.all_to_all(copies, "grp", 0, 0)


def body(right_side, viscosity, coarse_basis, coarse_factor):
    cap, sub = lax.axis_index("cap"), lax.axis_index("sub")
    caps, subs = lax.axis_size("cap"), lax.axis_size("sub")
    place = jnp.stack([
        cap % 2, (cap != 0) & (cap != caps - 1),
        sub % 2, (sub != 0) & (sub != subs - 1),
        lax.axis_index("grp"),
    ]).astype(jnp.int32)
    basis = coarse_basis[0, 0]
    force = right_side.reshape(SLABS, 8, LANES)
    own_gt = jnp.concatenate(
        [basis.T.reshape(KB // 8, 8, LANES), force, viscosity], axis=0)
    whole = lax.all_gather(own_gt, "grp", axis=0).reshape(GROUPS, -1, LANES)

    copies, near, far, edge = call(
        local_kernel, ((GROUPS, 2, 8, LANES),) + ((8, LANES),) * 3, (),
        place, force, viscosity, basis)
    vhalos = swapped(near, far, edge)
    vhalos, rows, _ = lax.optimization_barrier((vhalos, coarse_factor[0, 0], own_gt))
    factor = gathered = lax.all_gather(rows, "grp", axis=0, tiled=True)
    own = jnp.pad(coarse_factor[0, 0].T, ((0, 0), (0, 2 * LANES - KC // GROUPS)))
    (copies,) = call(
        begin_kernel, ((GROUPS, 5, 8, LANES),), ((KC, LANES), (1, 8, LANES)),
        place, lax.all_to_all(copies, "grp", 0, 0), own, *vhalos)
    coef, v, near, far, edge, gram, vh, fields, gt = call(
        start_kernel,
        (COEF,) + DIRECTION
        + ((4, ROWS, LANES), (SLABS + 4, ROWS, LANES), (GROUPS, KB, LANES)),
        SPREAD + (pltpu.SemaphoreType.DMA(()),),
        place, lax.all_to_all(copies, "grp", 0, 0), whole)
    u = fields
    for picard in range(2):
        us, vs, halos = [u], [v], []
        for k in range(S):
            beyond = swapped(near, far, edge)
            if picard == 0 and k == 0:
                (inside,) = call(inside_kernel, (FIELD,), (), place, v, coef, beside=True)
            else:
                gram, inside = call(
                    functools.partial(beside_kernel, k), (GRAM, FIELD), (),
                    place, span, gram, coef, *vs, *us[::-1][:2], beside=True)
            beyond, gram, inside = lax.optimization_barrier((beyond, gram, inside))
            halos.append(beyond)
            if k + 1 == S:
                (copies,) = call(
                    last_kernel, ((PLACES, 8, LANES),), (FIELD, GRAM),
                    place, span, *beyond, coef, inside, gram, *vs)
                break
            if picard == 0 and k == 0:
                image, copies = call(
                    image_kernel, (FIELD, (PLACES, 8, LANES)), (),
                    place, v, *beyond, coef, gram, inside)
                (pay,) = call(
                    merge_kernel, ((1, 8, LANES),), MERGE, place, image, gt, own, beside=True)
                span, u, v, near, far, edge = call(
                    first_kernel, ((8, LANES), FIELD) + DIRECTION[:4], SPREAD,
                    place, shared(copies), exchanged(pay), image, u, v, coef, gt)
            elif picard == 0:
                u, pay = call(
                    residual_kernel, (FIELD, (1, 8, LANES)), MERGE,
                    place, span, *beyond, coef, inside, gt, own)
                v, near, far, edge = call(
                    direction_kernel, DIRECTION[:4], SPREAD,
                    place, exchanged(pay), coef, gt, u)
            else:
                u, v, near, far, edge = call(
                    functools.partial(step_kernel, k == 0), (FIELD,) + DIRECTION[:4],
                    MERGE + SPREAD, place, span, *beyond, coef, inside, gt, factor)
            us.append(u)
            vs.append(v)
        tiles = shared(copies)
        kept = vs + [h[side] for side in range(4) for h in halos]
        if picard == 0:
            flow, coef, u = call(
                combine_kernel, (FLOW, COEF, FIELD), (), place, span, tiles, fields, vh, *kept)
            v, near, far, edge, gram, factor = call(
                restart_kernel, DIRECTION + ((KC, KC),),
                MERGE + SPREAD + (pltpu.SemaphoreType.DMA(()),),
                place, u, coef, gt, factor, far_away=3)
        else:
            result, pressure, good = call(
                end_kernel, ((SLABS, 8, LANES), (4, 8, LANES), (8, LANES)),
                (FIELD, (4, ROWS, LANES)), place, span, tiles, flow, *kept)
    given, good = lax.optimization_barrier(
        ((right_side, viscosity, coarse_basis, gathered), good))
    return lax.cond(
        good[0, 0] > 0.5,
        lambda *_: (result.reshape(3, 4, 8, LANES), pressure),
        stepwise,
        *given)


exact_mode = lax.Precision.HIGHEST


def padded_2(block, sides, width):
    for axis, dim in sides:
        count = lax.axis_size(axis)
        forward = [(i, i + 1) for i in range(count - 1)]
        backward = [(target, source) for source, target in forward]
        low = lax.ppermute(
            lax.slice_in_dim(block, block.shape[dim] - width, None, axis=dim), axis, forward
        )
        high = lax.ppermute(lax.slice_in_dim(block, 0, width, axis=dim), axis, backward)
        block = jnp.concatenate([low, block, high], axis=dim)
    return block


def stencil_faces(padded):
    centre = padded[1:-1, 1:-1, 1:-1]
    faces = (
        0.5 * (centre + padded[2:, 1:-1, 1:-1]),
        0.5 * (centre + padded[:-2, 1:-1, 1:-1]),
        0.5 * (centre + padded[1:-1, 2:, 1:-1]),
        0.5 * (centre + padded[1:-1, :-2, 1:-1]),
        0.5 * (centre + padded[1:-1, 1:-1, 2:]),
        0.5 * (centre + padded[1:-1, 1:-1, :-2]),
    )
    diagonal = 1.0 + faces[0] + faces[1] + faces[2] + faces[3] + faces[4] + faces[5]
    return (faces, diagonal)


def apply_stencil(padded_field, field, faces, diagonal):
    beside = (
        faces[0] * padded_field[:, 2:, 1:-1, 1:-1] + faces[1] * padded_field[:, :-2, 1:-1, 1:-1]
    )
    beside = (
        beside
        + faces[2] * padded_field[:, 1:-1, 2:, 1:-1]
        + faces[3] * padded_field[:, 1:-1, :-2, 1:-1]
    )
    beside = (
        beside
        + faces[4] * padded_field[:, 1:-1, 1:-1, 2:]
        + faces[5] * padded_field[:, 1:-1, 1:-1, :-2]
    )
    return diagonal * field - beside


def divergence_of(padded_field):
    result = 0.5 * (padded_field[0, 2:, 1:-1, 1:-1] - padded_field[0, :-2, 1:-1, 1:-1])
    result = result + 0.5 * (padded_field[1, 1:-1, 2:, 1:-1] - padded_field[1, 1:-1, :-2, 1:-1])
    return result + 0.5 * (padded_field[2, 1:-1, 1:-1, 2:] - padded_field[2, 1:-1, 1:-1, :-2])


def velocity_padded(field):
    return padded_2(field, (("cap", 1), ("grp", 2), ("sub", 3)), 1)


def curvature_sum(direction, image):
    return lax.psum(jnp.sum(direction * image), ("cap", "grp", "sub"))


def norm_sum(residual, precond):
    return lax.psum(jnp.sum(residual * precond), ("cap", "grp", "sub"))


def stepwise(right_side, viscosity, coarse_basis, whole_factor):
    basis_local = coarse_basis[0, 0]

    def precondition(residual, diagonal):
        profile = jnp.mean(residual, axis=(1, 2))
        local = jnp.dot(profile, basis_local, precision=exact_mode)
        merged = lax.psum(local, "grp").reshape(-1)
        solved = jnp.dot(whole_factor, merged, precision=exact_mode)
        spread = jnp.dot(solved.reshape(3, -1), basis_local.T, precision=exact_mode)
        return residual / diagonal + spread[:, None, None, :]

    velocity = jnp.zeros_like(right_side)
    viscous = viscosity
    for picard in range(2):
        if picard > 0:
            viscous = viscosity / (1.0 + 25.0 * jnp.sum(velocity * velocity, axis=0))
        padded_viscous = padded_2(viscous, (("cap", 0), ("grp", 1), ("sub", 2)), 1)
        faces, diagonal = stencil_faces(padded_viscous)

        def operate(field):
            return apply_stencil(velocity_padded(field), field, faces, diagonal)

        residual = right_side - operate(velocity)
        precond = precondition(residual, diagonal)
        norm_now = norm_sum(residual, precond)
        direction = precond
        for krylov_step in range(S):
            image = operate(direction)
            alpha = norm_now / curvature_sum(direction, image)
            velocity = velocity + alpha * direction
            residual = residual - alpha * image
            if krylov_step + 1 < S:
                precond = precondition(residual, diagonal)
                fresh = norm_sum(residual, precond)
                direction = precond + fresh / norm_now * direction
                norm_now = fresh
    pressure = -(viscous / (1.0 + viscous)) * divergence_of(velocity_padded(velocity))
    return (velocity, pressure)


def solution(mesh):
    placed = (
        P(None, "cap", "grp", "sub"),
        P("cap", "grp", "sub"),
        P("cap", "grp", "sub", None),
        P("cap", "sub", "grp", None),
    )
    return jax.shard_map(
        body,
        mesh=mesh,
        in_specs=placed,
        out_specs=(P(None, "cap", "grp", "sub"), P("cap", "grp", "sub")),
        check_vma=False,
    )
```

```python
import functools

import jax
import jax.numpy as jnp
from jax import lax
from jax.experimental import pallas as pl
from jax.experimental.pallas import tpu as pltpu
from jax.sharding import PartitionSpec as P

S = 5
SLABS = 12
ROWS = 64
LANES = 128
GROUPS = 8
KB = 512
KC = 1536
APART = 1e-3
SPAN = 2.6
FIELD = (SLABS, ROWS, LANES)
FACE = (3, ROWS, LANES)
EDGE = (ROWS, LANES)
GRAM = (24, LANES)
PLACES = 32
FLOW = (27, ROWS, LANES)
COEF = (9, 4, ROWS, LANES)
f32 = jnp.float32


def gram_row(i, j):
    i, j = min(i, j), max(i, j)
    return sum(min(t, S - 1) + 1 for t in range(j)) + i


def lane_ids():
    return lax.broadcasted_iota(jnp.int32, (ROWS, LANES), 1)


def row_ids():
    return lax.broadcasted_iota(jnp.int32, (ROWS, LANES), 0)


def ends_of(halo, i):
    return pltpu.roll(halo, LANES - 1 - 2 * i, 1)


def along_z(w, halo, i, lanes):
    ends = ends_of(halo, i)
    after = jnp.where(lanes == LANES - 1, ends, pltpu.roll(w, LANES - 1, 1))
    before = jnp.where(lanes == 0, ends, pltpu.roll(w, 1, 1))
    return after, before


def flag(place, i):
    return jnp.full((ROWS, LANES), place[i], jnp.int32) == 1


def faces_of(place, near, far):
    odd, inner = flag(place, 0), flag(place, 1)
    far = jnp.where(inner, far, 0.0)
    return jnp.where(odd, near, far), jnp.where(odd, far, near)


def merge_edges(place, near, far):
    far = jnp.where(flag(place, 3), far, 0.0)
    odd = flag(place, 2)
    low, high = jnp.where(odd, near, far), jnp.where(odd, far, near)
    return jnp.where(lane_ids() % 2 == 1, pltpu.roll(low, 1, 1), pltpu.roll(high, LANES - 1, 1))


def edge_of(get, count, lanes):
    edge = jnp.zeros((ROWS, LANES), f32)
    for i in range(count):
        moved = pltpu.roll(get(i), 2 * i + 1, 1)
        edge = jnp.where((lanes == 2 * i) | (lanes == 2 * i + 1), moved, edge)
    return edge


def store_coefs(coef, vis, low, high, halo):
    lanes, rows = lane_ids(), row_ids()
    for x in range(4):
        v = vis(x)
        up = vis(x + 1) if x < 3 else high
        down = vis(x - 1) if x else low
        yp = jnp.where(rows == ROWS - 1, 0.0, pltpu.roll(v, ROWS - 1, 0))
        ym = jnp.where(rows == 0, 0.0, pltpu.roll(v, 1, 0))
        zp, zm = along_z(v, halo, x, lanes)
        faces = [0.5 * (v + n) for n in (up, down, yp, ym, zp, zm)]
        diagonal = 1.0 + faces[0] + faces[1] + faces[2] + faces[3] + faces[4] + faces[5]
        faces[2] = jnp.where(rows == ROWS - 1, 0.0, faces[2])
        faces[3] = jnp.where(rows == 0, 0.0, faces[3])
        first, last = lanes == 0, lanes == LANES - 1
        coef[8, x] = jnp.where(first, faces[5], jnp.where(last, faces[4], 0.0))
        faces[4] = jnp.where(last, 0.0, faces[4])
        faces[5] = jnp.where(first, 0.0, faces[5])
        coef[0, x] = diagonal
        for f in range(6):
            coef[1 + f, x] = faces[f]
        coef[7, x] = 1.0 / diagonal


def stencil_inside(coef, field, write):
    for x in range(4):
        for c in range(3):
            w = field[4 * c + x]
            beside = coef[3, x] * pltpu.roll(w, ROWS - 1, 0) + coef[4, x] * pltpu.roll(w, 1, 0)
            beside = beside + coef[5, x] * pltpu.roll(w, LANES - 1, 1)
            beside = beside + coef[6, x] * pltpu.roll(w, 1, 1)
            if x < 3:
                beside = beside + coef[1, x] * field[4 * c + x + 1]
            if x:
                beside = beside + coef[2, x] * field[4 * c + x - 1]
            write(c, x, coef[0, x] * w - beside)


def stencil_beyond(coef, sides, halo, write):
    for c in range(3):
        low, high = sides(c)
        for x in range(4):
            beside = coef[8, x] * ends_of(halo, 4 * c + x)
            if x == 0:
                beside = beside + coef[2, x] * low
            if x == 3:
                beside = beside + coef[1, x] * high
            write(c, x, beside)


def dot_rows(a, b):
    total = jnp.zeros((8, LANES), f32)
    for s in range(SLABS):
        total = total + jnp.sum((a[s] * b[s]).reshape(8, 8, LANES), axis=0)
    return jnp.sum(total, axis=0, keepdims=True)


def merge(u, gt, prof, mb):
    for c in range(3):
        total = u[4 * c] + u[4 * c + 1] + u[4 * c + 2] + u[4 * c + 3]
        prof[8 * c : 8 * c + 8] = jnp.sum(total.reshape(8, 8, LANES), axis=1) * (1.0 / 32.0)

    @pl.loop(0, KB // 32, unroll=8)
    def _(step):
        at = pl.multiple_of(step * 32, 32)
        totals = [jnp.zeros((32, LANES), f32)] * 3
        for g in range(GROUPS):
            b = gt[g, pl.ds(at, 32), :]
            for c in range(3):
                totals[c] = totals[c] + b * prof[8 * c + g : 8 * c + g + 1, :]
        for c in range(3):
            total = jnp.sum(totals[c], axis=1, keepdims=True)
            mb[pl.ds(c * KB + at, 32), :] = jnp.broadcast_to(total, (32, LANES))


def solve(factor, mb, sb):
    def rows_of(step, totals):
        totals = list(totals)
        for part in range(16):
            at = pl.multiple_of(step * 128 + part * 8, 8)
            m = mb[pl.ds(at, 8), :]
            for q in range(KC // LANES):
                totals[q] = totals[q] + factor[pl.ds(at, 8), LANES * q : LANES * (q + 1)] * m
        return tuple(totals)

    zero = jnp.zeros((8, LANES), f32)
    totals = lax.fori_loop(0, KC // 128, rows_of, (zero,) * (KC // LANES))
    for q in range(KC // LANES):
        row = jnp.sum(totals[q], axis=0, keepdims=True)
        sb[LANES * q : LANES * (q + 1), :] = jnp.broadcast_to(row, (LANES, LANES)).T


def solve_own(own, mb, pay):
    def rows_of(step, totals):
        totals = list(totals)
        for part in range(32):
            at = pl.multiple_of(step * 256 + part * 8, 8)
            m = mb[pl.ds(at, 8), :]
            for q in range(2):
                r = 2 * (part % 4) + q
                totals[r] = totals[r] + own[pl.ds(at, 8), LANES * q : LANES * (q + 1)] * m
        return tuple(totals)

    zero = jnp.zeros((8, LANES), f32)
    t = lax.fori_loop(0, KC // 256, rows_of, (zero,) * 8)
    pay[0] = zero
    for q in range(2):
        total = (t[q] + t[2 + q]) + (t[4 + q] + t[6 + q])
        pay[0, q : q + 1, :] = jnp.sum(total, axis=0, keepdims=True)


def unpack(pays, sb):
    for g in range(GROUPS):
        at = g * (KC // GROUPS)
        left = jnp.broadcast_to(pays[g, 0, 0:1, :], (LANES, LANES)).T
        right = jnp.broadcast_to(pays[g, 0, 1:2, :], (LANES, LANES)).T
        sb[at : at + LANES, :] = left
        sb[at + LANES : at + KC // GROUPS, :] = right[: KC // GROUPS - LANES]


def spread_over(gt, sb, spread):
    def spread_of(step, totals):
        totals = list(totals)
        for part in range(8):
            at = pl.multiple_of(step * 64 + part * 8, 8)
            solved = [sb[pl.ds(c * KB + at, 8), :] for c in range(3)]
            for g in range(GROUPS):
                b = gt[g, pl.ds(at, 8), :]
                for c in range(3):
                    totals[8 * c + g] = totals[8 * c + g] + b * solved[c]
        return tuple(totals)

    zero = jnp.zeros((8, LANES), f32)
    totals = lax.fori_loop(0, KB // 64, spread_of, (zero,) * 24)
    for r in range(24):
        spread[r : r + 1, :] = jnp.sum(totals[r], axis=0, keepdims=True)


def coarse(u, gt, factor, prof, mb, sb, spread):
    merge(u, gt, prof, mb)
    solve(factor, mb, sb)
    spread_over(gt, sb, spread)


def finish_direction(place, u, coef, spread, v, near, far, edge):
    for x in range(4):
        for c in range(3):
            s = 4 * c + x
            wide = jnp.broadcast_to(spread[8 * c : 8 * c + 8, :][:, None, :], (8, 8, LANES))
            v[s] = u[s] * coef[7, x] + wide.reshape(ROWS, LANES)
    if near is not None:
        hand_over(place, v, near, far, edge)


def hand_over(place, v, near, far, edge):
    for c in range(3):
        near[c] = v[4 * c + 3 - 3 * place[0]]
        far[c] = v[4 * c + 3 * place[0]]
    edge[...] = edge_of(lambda i: v[i], SLABS, lane_ids())


def basis_coefs(span, k):
    half = 0.5 * span
    if k == 0:
        return half, None, 1.0 / half
    return half, 0.5 * half, 2.0 / half


def local_kernel(place, force, viscosity, basis, copies, near, far, edge):
    shares = []
    for c in range(3):
        total = force[4 * c] + force[4 * c + 1] + force[4 * c + 2] + force[4 * c + 3]
        row = jnp.sum(total, axis=0, keepdims=True) * (1.0 / 32.0)
        column = jnp.broadcast_to(row, (LANES, LANES)).T
        for q in range(KB // LANES):
            part = basis[:, LANES * q : LANES * (q + 1)] * column
            shares.append(jnp.sum(part, axis=0, keepdims=True))
    rows = lax.broadcasted_iota(jnp.int32, (8, LANES), 0)
    lanes = lax.broadcasted_iota(jnp.int32, (8, LANES), 1)
    for q in range(2):
        tile = jnp.zeros((8, LANES), f32)
        for r in range(8):
            if 8 * q + r < len(shares):
                tile = jnp.where(rows == r, shares[8 * q + r], tile)
        for g in range(GROUPS):
            copies[g, q] = tile
    near[...] = viscosity[3 - 3 * place[0]]
    far[...] = viscosity[3 * place[0]]
    columns = jnp.zeros((8, LANES), f32)
    for x in range(4):
        moved = pltpu.roll(viscosity[x], 2 * x + 1, 1)
        columns = jnp.where((lanes == 2 * x) | (lanes == 2 * x + 1), moved, columns)
    edge[...] = columns


def begin_kernel(place, pays, own, vnear, vfar, enear, efar, copies, mb, pay):
    for q in range(2):
        total = tree([pays[g, q] for g in range(GROUPS)])
        for r in range(8):
            at = LANES * (8 * q + r)
            if at < KC:
                row = jnp.broadcast_to(total[r : r + 1, :], (LANES, LANES))
                mb[at : at + LANES, :] = row.T
    solve_own(own, mb, pay)
    for g in range(GROUPS):
        copies[g, 0] = pay[0]
        for i, tile in enumerate((vnear, vfar, enear, efar)):
            copies[g, 1 + i] = tile[...]


def start_kernel(place, pays, whole,
                 coef, v, near, far, edge, gram, vh, fields, gt, sb, spread, arrived):
    copy = pltpu.make_async_copy(whole.at[:, pl.ds(0, KB)], gt, arrived)
    copy.start()
    unpack(pays, sb)
    for g in range(GROUPS):
        for s in range(SLABS + 4):
            fields[s, 8 * g : 8 * g + 8, :] = whole[g, KB + 8 * s : KB + 8 * s + 8, :]
        for i in range(4):
            vh[i, 8 * g : 8 * g + 8, :] = pays[g, 1 + i]
    low, high = faces_of(place, vh[0], vh[1])
    halo = merge_edges(place, vh[2], vh[3])
    store_coefs(coef, lambda x: fields[SLABS + x], low, high, halo)
    copy.wait()
    spread_over(gt, sb, spread)
    finish_direction(place, fields, coef, spread, v, near, far, edge)
    gram[...] = jnp.zeros(GRAM, f32)
    gram[0:1, :] = dot_rows(v, fields)


def inside_kernel(place, v, coef, image):
    def write(c, x, value):
        image[4 * c + x] = value

    stencil_inside(coef, v, write)


def image_kernel(place, v, near, far, edge_near, edge_far, coef, gram, inside, image, copies):
    halo = merge_edges(place, edge_near[...], edge_far[...])

    def write(c, x, value):
        image[4 * c + x] = inside[4 * c + x] - value

    stencil_beyond(coef, lambda c: faces_of(place, near[c], far[c]), halo, write)
    rows = lax.broadcasted_iota(jnp.int32, (8, LANES), 0)
    tile = jnp.where(rows == 0, gram[0:1, :], jnp.where(rows == 1, dot_rows(v, image), 0.0))
    for i in range(PLACES):
        copies[i] = tile


def merge_kernel(place, image, gt, own, pay, prof, mb):
    merge(image, gt, prof, mb)
    solve_own(own, mb, pay)


def first_kernel(place, tiles, pays, image, u0, v0, coef, gt,
                 span, u, v, near, far, edge, sb, spread):
    sums = jnp.sum(tree([tiles[i] for i in range(PLACES)]), axis=1, keepdims=True)
    width = SPAN * sums[1:2, :] / sums[0:1, :]
    span[...] = jnp.broadcast_to(width, (8, LANES))
    shift, _, scale = basis_coefs(width, 0)
    unpack(pays, sb)
    spread_over(gt, sb, spread)
    finish_direction(place, image, coef, spread, v, None, None, None)
    for s in range(SLABS):
        u[s] = (image[s] - shift * u0[s]) * scale
        v[s] = (v[s] - shift * v0[s]) * scale
    hand_over(place, v, near, far, edge)


def residual_kernel(place, span, hnear, hfar, enear, efar, coef, inside, gt, own,
                    u, pay, prof, mb):
    next_residual(place, False, span, hnear, hfar, enear, efar, coef, inside, u)
    merge(u, gt, prof, mb)
    solve_own(own, mb, pay)


def direction_kernel(place, pays, coef, gt, u, v, near, far, edge, sb, spread):
    unpack(pays, sb)
    spread_over(gt, sb, spread)
    finish_direction(place, u, coef, spread, v, near, far, edge)


def beside_kernel(k, place, span, gram_in, coef, *refs):
    refs, (gram, inside) = refs[:-2], refs[-2:]
    vs, us = refs[: k + 1], refs[k + 1 :]
    uk = us[0]
    if k:
        store_dots(gram, gram_in, vs[:-1], uk, vs[-1])
    else:
        gram[...] = gram_in[...]
    shift, back, scale = basis_coefs(span[0:1, 0:1], k)

    def write(c, x, value):
        s = 4 * c + x
        value = value - shift * uk[s]
        if k:
            value = value - back * us[1][s]
        inside[s] = value * scale

    stencil_inside(coef, vs[-1], write)


def tree(parts):
    while len(parts) > 1:
        parts = [parts[i] + parts[i + 1] for i in range(0, len(parts), 2)]
    return parts[0]


def pack_sums(gram, copies):
    sums = jnp.sum(gram[...], axis=1, keepdims=True)
    lanes = lax.broadcasted_iota(jnp.int32, (8, LANES), 1)
    tile = jnp.zeros((8, LANES), f32)
    for q in range(GRAM[0] // 8):
        tile = jnp.where(lanes == q, sums[8 * q : 8 * q + 8], tile)
    for i in range(PLACES):
        copies[i] = tile


def store_dots(gram, gram_in, vs, u, v=None):
    gram[...] = gram_in[...]
    vs = list(vs) + ([] if v is None else [v])
    totals = [jnp.zeros((8, LANES), f32)] * len(vs)
    for s in range(SLABS):
        us = u[s]
        for i, vi in enumerate(vs):
            totals[i] = totals[i] + jnp.sum((vi[s] * us).reshape(8, 8, LANES), axis=0)
    level = len(vs) - (0 if v is None else 1)
    for i, total in enumerate(totals):
        r = gram_row(i, level)
        gram[r : r + 1, :] = jnp.sum(total, axis=0, keepdims=True)


def next_residual(place, first, span, near, far, edge_near, edge_far, coef, inside, u):
    halo = merge_edges(place, edge_near[...], edge_far[...])
    scale = basis_coefs(span[0:1, 0:1], 0 if first else 1)[2]

    def write(c, x, value):
        u[4 * c + x] = inside[4 * c + x] - value * scale

    stencil_beyond(coef, lambda c: faces_of(place, near[c], far[c]), halo, write)


def step_kernel(first, place, span, hnear, hfar, enear, efar, coef, inside, gt, factor,
                u, v, near, far, edge, prof, mb, sb, spread):
    next_residual(place, first, span, hnear, hfar, enear, efar, coef, inside, u)
    coarse(u, gt, factor, prof, mb, sb, spread)
    finish_direction(place, u, coef, spread, v, near, far, edge)


def last_kernel(place, span, hnear, hfar, enear, efar, coef, inside, gram_in,
                v0, v1, v2, v3, v4, copies, u, gram):
    vs = (v0, v1, v2, v3, v4)
    next_residual(place, False, span, hnear, hfar, enear, efar, coef, inside, u)
    store_dots(gram, gram_in, vs, u)
    pack_sums(gram, copies)


def well_posed(n):
    rows = []
    good = None
    for j in range(S):
        row = []
        pivot = n[j][j]
        for i in range(j):
            value = n[i][j]
            for t in range(i):
                value = value - rows[i][t] * row[t]
            row.append(value)
            pivot = pivot - value * value / rows[i][i]
        row.append(pivot)
        apart = jnp.where(pivot > APART * n[j][j], 1.0, 0.0)
        good = apart if good is None else good * apart
        rows.append([value / rows[i][i] for i, value in enumerate(row[:j])] + [pivot])
    return good


def krylov_weights(span, sums):
    def product(i, j):
        r = gram_row(i, j)
        return sums[r // 8][r % 8 : r % 8 + 1, :]

    n = [[product(i, j) for j in range(S + 1)] for i in range(S)]
    half = 0.5 * span
    quarter = 0.5 * half

    def operate(p):
        out = [None] * (S + 1)

        def put(i, value):
            out[i] = value if out[i] is None else out[i] + value

        for j, w in enumerate(p):
            put(j, half * w)
            put(j + 1, (half if j == 0 else quarter) * w)
            if j:
                put(j - 1, quarter * w)
        return out[: len(p) + 1]

    def pair(a, b):
        total = None
        for i, ai in enumerate(a):
            part = None
            for j, bj in enumerate(b):
                term = n[i][j] * bj
                part = term if part is None else part + term
            total = ai * part if total is None else total + ai * part
        return total

    one = jnp.ones_like(span)
    r, p = [one], [one]
    x = []
    norm = n[0][0]
    for k in range(S):
        image = operate(p)
        alpha = norm / pair(p, image)
        for j, w in enumerate(p):
            if j < len(x):
                x[j] = x[j] + alpha * w
            else:
                x.append(alpha * w)
        r = [(r[j] - alpha * w) if j < len(r) else -(alpha * w) for j, w in enumerate(image)]
        if k + 1 < S:
            fresh = pair(r, r)
            beta = fresh / norm
            p = [r[j] + beta * p[j] if j < len(p) else r[j] for j in range(len(r))]
            norm = fresh
    return x, well_posed(n)


def weights_of(span, tiles):
    total = tree([tiles[i] for i in range(PLACES)])
    columns = [total[:, q : q + 1] for q in range(GRAM[0] // 8)]
    return krylov_weights(span[0:1, 0:1], columns)


def combine(x, parts, before=None):
    total = x[0] * parts[0]
    for j in range(1, S):
        total = total + x[j] * parts[j]
    return total if before is None else before + total


def combine_kernel(place, span, tiles, fields, vh,
                   v0, v1, v2, v3, v4, n0, n1, n2, n3, n4, f0, f1, f2, f3, f4,
                   en0, en1, en2, en3, en4, ef0, ef1, ef2, ef3, ef4,
                   flow):
    x, good = weights_of(span, tiles)
    vs = (v0, v1, v2, v3, v4)
    ns, fs = (n0, n1, n2, n3, n4), (f0, f1, f2, f3, f4)
    ens, efs = (en0, en1, en2, en3, en4), (ef0, ef1, ef2, ef3, ef4)
    for s in range(SLABS):
        flow[s] = combine(x, [t[s] for t in vs])
    for c in range(3):
        flow[12 + c], flow[15 + c] = faces_of(
            place, combine(x, [t[c] for t in ns]), combine(x, [t[c] for t in fs]))
    halo = merge_edges(
        place, combine(x, [t[...] for t in ens]), combine(x, [t[...] for t in efs]))

    def thinned(viscosity, a, b, c):
        return viscosity / (1.0 + 25.0 * (a * a + b * b + c * c))

    for i in range(4):
        flow[18 + i] = thinned(fields[SLABS + i], flow[i], flow[4 + i], flow[8 + i])
    vis_low, vis_high = faces_of(place, vh[0], vh[1])
    flow[22] = thinned(vis_low, flow[12], flow[13], flow[14])
    flow[23] = thinned(vis_high, flow[15], flow[16], flow[17])
    second = pltpu.roll(halo, LANES - 8, 1)
    third = pltpu.roll(halo, LANES - 16, 1)
    flow[24] = thinned(merge_edges(place, vh[2], vh[3]), halo, second, third)
    flow[25] = halo
    flow[26] = jnp.broadcast_to(good, EDGE)


def restart_kernel(place, flow, fields, gt, factor_in,
                   coef, u, v, near, far, edge, gram, factor, prof, mb, sb, spread, arrived):
    fetch = pltpu.make_async_copy(factor_in, factor, arrived)
    fetch.start()
    store_coefs(coef, lambda i: flow[18 + i], flow[22], flow[23], flow[24])

    def write(c, i, value):
        u[4 * c + i] = fields[4 * c + i] - value

    stencil_inside(coef, flow, write)

    def write_beyond(c, i, value):
        u[4 * c + i] = u[4 * c + i] + value

    stencil_beyond(coef, lambda c: (flow[12 + c], flow[15 + c]), flow[25], write_beyond)
    merge(u, gt, prof, mb)
    fetch.wait()
    solve(factor, mb, sb)
    spread_over(gt, sb, spread)
    finish_direction(place, u, coef, spread, v, near, far, edge)
    gram[...] = jnp.zeros(GRAM, f32)
    gram[0:1, :] = dot_rows(v, u)


def end_kernel(place, span, tiles, flow,
               v0, v1, v2, v3, v4, n0, n1, n2, n3, n4, f0, f1, f2, f3, f4,
               en0, en1, en2, en3, en4, ef0, ef1, ef2, ef3, ef4,
               velocity, pressure, good, cross):
    lanes = lax.broadcasted_iota(jnp.int32, (8, LANES), 1)
    rows = row_ids()
    x, good_now = weights_of(span, tiles)
    good[0, 0] = jnp.min(good_now * flow[26][0:1, 0:1])
    vs = (v0, v1, v2, v3, v4)
    ns, fs = (n0, n1, n2, n3, n4), (f0, f1, f2, f3, f4)
    ens, efs = (en0, en1, en2, en3, en4), (ef0, ef1, ef2, ef3, ef4)
    own = pl.ds(pl.multiple_of(place[4] * 8, 8), 8)
    for s in range(SLABS):
        velocity[s] = combine(x, [t[s, own, :] for t in vs], flow[s, own, :])
    near = combine(x, [t[0, own, :] for t in ns])
    far = combine(x, [t[0, own, :] for t in fs])
    odd = jnp.full((8, LANES), place[0], jnp.int32) == 1
    far = jnp.where(jnp.full((8, LANES), place[1], jnp.int32) == 1, far, 0.0)
    low = flow[12, own, :] + jnp.where(odd, near, far)
    high = flow[15, own, :] + jnp.where(odd, far, near)
    cross[0] = flow[25] + merge_edges(
        place, combine(x, [t[...] for t in ens]), combine(x, [t[...] for t in efs]))
    halo = cross[0, own, :]
    for i in range(4):
        vis = flow[18 + i, own, :]
        up = velocity[i + 1] if i < 3 else high
        down = velocity[i - 1] if i else low
        w = combine(x, [t[4 + i] for t in vs], flow[4 + i])
        yp = jnp.where(rows == ROWS - 1, 0.0, pltpu.roll(w, ROWS - 1, 0))
        ym = jnp.where(rows == 0, 0.0, pltpu.roll(w, 1, 0))
        cross[1 + i] = yp - ym
        zp, zm = along_z(velocity[8 + i], halo, 8 + i, lanes)
        divergence = 0.5 * (up - down) + 0.5 * cross[1 + i, own, :] + 0.5 * (zp - zm)
        pressure[i] = -(vis / (1.0 + vis)) * divergence


def call(kernel, outs, scratch, place, *args, far_away=None, beside=False):
    vmem = pl.BlockSpec(memory_space=pltpu.VMEM)
    places = [pl.BlockSpec(memory_space=pltpu.SMEM)] + [vmem] * len(args)
    if far_away is not None:
        places[1 + far_away] = pl.BlockSpec(memory_space=pl.ANY)
    cost = None
    if beside:
        size = sum(a.size for a in args)
        cost = pl.CostEstimate(flops=2 * size, bytes_accessed=4 * size, transcendentals=0)
    return pl.pallas_call(
        kernel,
        out_shape=[jax.ShapeDtypeStruct(o, f32) for o in outs],
        in_specs=places,
        out_specs=[pl.BlockSpec(memory_space=pltpu.SMEM) if o == (1, 1) else vmem for o in outs],
        scratch_shapes=[pltpu.VMEM(s, f32) if isinstance(s, tuple) else s for s in scratch],
        cost_estimate=cost,
        compiler_params=pltpu.CompilerParams(vmem_limit_bytes=20 * 2**20),
    )(place, *args)


MERGE = ((24, LANES), (KC, LANES))
SPREAD = ((KC, LANES), (24, LANES))
DIRECTION = (FIELD, FACE, FACE, EDGE, GRAM)


def swap_near(value, axis):
    return lax.ppermute(value, axis, [(i, i ^ 1) for i in range(lax.axis_size(axis))])


def swap_far(value, axis):
    count = lax.axis_size(axis)
    pairs = [(i, (i + 1) % count) for i in range(1, count, 2)]
    return lax.ppermute(value, axis, pairs + [(b, a) for a, b in pairs])


def swapped(near, far, edge):
    near_face = swap_near(near, "cap")
    far_face = swap_far(far, "cap")
    near_edge = swap_near(edge, "sub")
    far_edge = swap_far(edge, "sub")
    return near_face, far_face, near_edge, far_edge


def shared(copies):
    return lax.all_to_all(copies, ("cap", "sub"), 0, 0)


def exchanged(pay):
    copies = jnp.broadcast_to(pay[None], (GROUPS,) + pay.shape)
    return lax.all_to_all(copies, "grp", 0, 0)


def body(right_side, viscosity, coarse_basis, coarse_factor):
    cap, sub = lax.axis_index("cap"), lax.axis_index("sub")
    caps, subs = lax.axis_size("cap"), lax.axis_size("sub")
    place = jnp.stack([
        cap % 2, (cap != 0) & (cap != caps - 1),
        sub % 2, (sub != 0) & (sub != subs - 1),
        lax.axis_index("grp"),
    ]).astype(jnp.int32)
    basis = coarse_basis[0, 0]
    force = right_side.reshape(SLABS, 8, LANES)
    own_gt = jnp.concatenate(
        [basis.T.reshape(KB // 8, 8, LANES), force, viscosity], axis=0)
    whole = lax.all_gather(own_gt, "grp", axis=0).reshape(GROUPS, -1, LANES)

    copies, near, far, edge = call(
        local_kernel, ((GROUPS, 2, 8, LANES),) + ((8, LANES),) * 3, (),
        place, force, viscosity, basis)
    vhalos = swapped(near, far, edge)
    vhalos, rows, _ = lax.optimization_barrier((vhalos, coarse_factor[0, 0], own_gt))
    factor = gathered = lax.all_gather(rows, "grp", axis=0, tiled=True)
    own = jnp.pad(coarse_factor[0, 0].T, ((0, 0), (0, 2 * LANES - KC // GROUPS)))
    (copies,) = call(
        begin_kernel, ((GROUPS, 5, 8, LANES),), ((KC, LANES), (1, 8, LANES)),
        place, lax.all_to_all(copies, "grp", 0, 0), own, *vhalos)
    coef, v, near, far, edge, gram, vh, fields, gt = call(
        start_kernel,
        (COEF,) + DIRECTION
        + ((4, ROWS, LANES), (SLABS + 4, ROWS, LANES), (GROUPS, KB, LANES)),
        SPREAD + (pltpu.SemaphoreType.DMA(()),),
        place, lax.all_to_all(copies, "grp", 0, 0), whole)
    u = fields
    for picard in range(2):
        us, vs, halos = [u], [v], []
        for k in range(S):
            beyond = swapped(near, far, edge)
            if picard == 0 and k == 0:
                (inside,) = call(inside_kernel, (FIELD,), (), place, v, coef, beside=True)
            else:
                gram, inside = call(
                    functools.partial(beside_kernel, k), (GRAM, FIELD), (),
                    place, span, gram, coef, *vs, *us[::-1][:2], beside=True)
            beyond, gram, inside = lax.optimization_barrier((beyond, gram, inside))
            halos.append(beyond)
            if k + 1 == S:
                (copies,) = call(
                    last_kernel, ((PLACES, 8, LANES),), (FIELD, GRAM),
                    place, span, *beyond, coef, inside, gram, *vs)
                break
            if picard == 0 and k == 0:
                image, copies = call(
                    image_kernel, (FIELD, (PLACES, 8, LANES)), (),
                    place, v, *beyond, coef, gram, inside)
                (pay,) = call(
                    merge_kernel, ((1, 8, LANES),), MERGE, place, image, gt, own, beside=True)
                span, u, v, near, far, edge = call(
                    first_kernel, ((8, LANES), FIELD) + DIRECTION[:4], SPREAD,
                    place, shared(copies), exchanged(pay), image, u, v, coef, gt)
            elif picard == 0:
                u, pay = call(
                    residual_kernel, (FIELD, (1, 8, LANES)), MERGE,
                    place, span, *beyond, coef, inside, gt, own)
                v, near, far, edge = call(
                    direction_kernel, DIRECTION[:4], SPREAD,
                    place, exchanged(pay), coef, gt, u)
            else:
                u, v, near, far, edge = call(
                    functools.partial(step_kernel, k == 0), (FIELD,) + DIRECTION[:4],
                    MERGE + SPREAD, place, span, *beyond, coef, inside, gt, factor)
            us.append(u)
            vs.append(v)
        tiles = shared(copies)
        kept = vs + [h[side] for side in range(4) for h in halos]
        if picard == 0:
            (flow,) = call(combine_kernel, (FLOW,), (), place, span, tiles, fields, vh, *kept)
            coef, u, v, near, far, edge, gram, factor = call(
                restart_kernel, (COEF, FIELD) + DIRECTION + ((KC, KC),),
                MERGE + SPREAD + (pltpu.SemaphoreType.DMA(()),),
                place, flow, fields, gt, factor, far_away=3)
        else:
            result, pressure, good = call(
                end_kernel, ((SLABS, 8, LANES), (4, 8, LANES), (1, 1)),
                ((5, ROWS, LANES),), place, span, tiles, flow, *kept)
    given, good = lax.optimization_barrier(
        ((right_side, viscosity, coarse_basis, gathered), good))
    return lax.cond(
        good[0, 0] > 0.5,
        lambda *_: (result.reshape(3, 4, 8, LANES), pressure),
        stepwise,
        *given)


exact_mode = lax.Precision.HIGHEST


def padded_2(block, sides, width):
    for axis, dim in sides:
        count = lax.axis_size(axis)
        forward = [(i, i + 1) for i in range(count - 1)]
        backward = [(target, source) for source, target in forward]
        low = lax.ppermute(
            lax.slice_in_dim(block, block.shape[dim] - width, None, axis=dim), axis, forward
        )
        high = lax.ppermute(lax.slice_in_dim(block, 0, width, axis=dim), axis, backward)
        block = jnp.concatenate([low, block, high], axis=dim)
    return block


def stencil_faces(padded):
    centre = padded[1:-1, 1:-1, 1:-1]
    faces = (
        0.5 * (centre + padded[2:, 1:-1, 1:-1]),
        0.5 * (centre + padded[:-2, 1:-1, 1:-1]),
        0.5 * (centre + padded[1:-1, 2:, 1:-1]),
        0.5 * (centre + padded[1:-1, :-2, 1:-1]),
        0.5 * (centre + padded[1:-1, 1:-1, 2:]),
        0.5 * (centre + padded[1:-1, 1:-1, :-2]),
    )
    diagonal = 1.0 + faces[0] + faces[1] + faces[2] + faces[3] + faces[4] + faces[5]
    return (faces, diagonal)


def apply_stencil(padded_field, field, faces, diagonal):
    beside = (
        faces[0] * padded_field[:, 2:, 1:-1, 1:-1] + faces[1] * padded_field[:, :-2, 1:-1, 1:-1]
    )
    beside = (
        beside
        + faces[2] * padded_field[:, 1:-1, 2:, 1:-1]
        + faces[3] * padded_field[:, 1:-1, :-2, 1:-1]
    )
    beside = (
        beside
        + faces[4] * padded_field[:, 1:-1, 1:-1, 2:]
        + faces[5] * padded_field[:, 1:-1, 1:-1, :-2]
    )
    return diagonal * field - beside


def divergence_of(padded_field):
    result = 0.5 * (padded_field[0, 2:, 1:-1, 1:-1] - padded_field[0, :-2, 1:-1, 1:-1])
    result = result + 0.5 * (padded_field[1, 1:-1, 2:, 1:-1] - padded_field[1, 1:-1, :-2, 1:-1])
    return result + 0.5 * (padded_field[2, 1:-1, 1:-1, 2:] - padded_field[2, 1:-1, 1:-1, :-2])


def velocity_padded(field):
    return padded_2(field, (("cap", 1), ("grp", 2), ("sub", 3)), 1)


def curvature_sum(direction, image):
    return lax.psum(jnp.sum(direction * image), ("cap", "grp", "sub"))


def norm_sum(residual, precond):
    return lax.psum(jnp.sum(residual * precond), ("cap", "grp", "sub"))


def stepwise(right_side, viscosity, coarse_basis, whole_factor):
    basis_local = coarse_basis[0, 0]

    def precondition(residual, diagonal):
        profile = jnp.mean(residual, axis=(1, 2))
        local = jnp.dot(profile, basis_local, precision=exact_mode)
        merged = lax.psum(local, "grp").reshape(-1)
        solved = jnp.dot(whole_factor, merged, precision=exact_mode)
        spread = jnp.dot(solved.reshape(3, -1), basis_local.T, precision=exact_mode)
        return residual / diagonal + spread[:, None, None, :]

    velocity = jnp.zeros_like(right_side)
    viscous = viscosity
    for picard in range(2):
        if picard > 0:
            viscous = viscosity / (1.0 + 25.0 * jnp.sum(velocity * velocity, axis=0))
        padded_viscous = padded_2(viscous, (("cap", 0), ("grp", 1), ("sub", 2)), 1)
        faces, diagonal = stencil_faces(padded_viscous)

        def operate(field):
            return apply_stencil(velocity_padded(field), field, faces, diagonal)

        residual = right_side - operate(velocity)
        precond = precondition(residual, diagonal)
        norm_now = norm_sum(residual, precond)
        direction = precond
        for krylov_step in range(S):
            image = operate(direction)
            alpha = norm_now / curvature_sum(direction, image)
            velocity = velocity + alpha * direction
            residual = residual - alpha * image
            if krylov_step + 1 < S:
                precond = precondition(residual, diagonal)
                fresh = norm_sum(residual, precond)
                direction = precond + fresh / norm_now * direction
                norm_now = fresh
    pressure = -(viscous / (1.0 + viscous)) * divergence_of(velocity_padded(velocity))
    return (velocity, pressure)


def solution(mesh):
    placed = (
        P(None, "cap", "grp", "sub"),
        P("cap", "grp", "sub"),
        P("cap", "grp", "sub", None),
        P("cap", "sub", "grp", None),
    )
    return jax.shard_map(
        body,
        mesh=mesh,
        in_specs=placed,
        out_specs=(P(None, "cap", "grp", "sub"), P("cap", "grp", "sub")),
        check_vma=False,
    )
```

```python
import functools

import jax
import jax.numpy as jnp
from jax import lax
from jax.experimental import pallas as pl
from jax.experimental.pallas import tpu as pltpu
from jax.sharding import PartitionSpec as P

S = 5
SLABS = 12
ROWS = 64
LANES = 128
GROUPS = 8
KB = 512
KC = 1536
APART = 1e-3
SPAN = 2.6
FIELD = (SLABS, ROWS, LANES)
FACE = (3, ROWS, LANES)
EDGE = (ROWS, LANES)
GRAM = (24, LANES)
PLACES = 32
FLOW = (27, ROWS, LANES)
COEF = (9, 4, ROWS, LANES)
f32 = jnp.float32


def gram_row(i, j):
    i, j = min(i, j), max(i, j)
    return sum(min(t, S - 1) + 1 for t in range(j)) + i


def lane_ids():
    return lax.broadcasted_iota(jnp.int32, (ROWS, LANES), 1)


def row_ids():
    return lax.broadcasted_iota(jnp.int32, (ROWS, LANES), 0)


def ends_of(halo, i):
    return pltpu.roll(halo, LANES - 1 - 2 * i, 1)


def along_z(w, halo, i, lanes):
    ends = ends_of(halo, i)
    after = jnp.where(lanes == LANES - 1, ends, pltpu.roll(w, LANES - 1, 1))
    before = jnp.where(lanes == 0, ends, pltpu.roll(w, 1, 1))
    return after, before


def flag(place, i):
    return jnp.full((ROWS, LANES), place[i], jnp.int32) == 1


def faces_of(place, near, far):
    odd, inner = flag(place, 0), flag(place, 1)
    far = jnp.where(inner, far, 0.0)
    return jnp.where(odd, near, far), jnp.where(odd, far, near)


def merge_edges(place, near, far):
    far = jnp.where(flag(place, 3), far, 0.0)
    odd = flag(place, 2)
    low, high = jnp.where(odd, near, far), jnp.where(odd, far, near)
    return jnp.where(lane_ids() % 2 == 1, pltpu.roll(low, 1, 1), pltpu.roll(high, LANES - 1, 1))


def edge_of(get, count, lanes):
    edge = jnp.zeros((ROWS, LANES), f32)
    for i in range(count):
        moved = pltpu.roll(get(i), 2 * i + 1, 1)
        edge = jnp.where((lanes == 2 * i) | (lanes == 2 * i + 1), moved, edge)
    return edge


def store_coefs(coef, vis, low, high, halo):
    lanes, rows = lane_ids(), row_ids()
    for x in range(4):
        v = vis(x)
        up = vis(x + 1) if x < 3 else high
        down = vis(x - 1) if x else low
        yp = jnp.where(rows == ROWS - 1, 0.0, pltpu.roll(v, ROWS - 1, 0))
        ym = jnp.where(rows == 0, 0.0, pltpu.roll(v, 1, 0))
        zp, zm = along_z(v, halo, x, lanes)
        faces = [0.5 * (v + n) for n in (up, down, yp, ym, zp, zm)]
        diagonal = 1.0 + faces[0] + faces[1] + faces[2] + faces[3] + faces[4] + faces[5]
        faces[2] = jnp.where(rows == ROWS - 1, 0.0, faces[2])
        faces[3] = jnp.where(rows == 0, 0.0, faces[3])
        first, last = lanes == 0, lanes == LANES - 1
        coef[8, x] = jnp.where(first, faces[5], jnp.where(last, faces[4], 0.0))
        faces[4] = jnp.where(last, 0.0, faces[4])
        faces[5] = jnp.where(first, 0.0, faces[5])
        coef[0, x] = diagonal
        for f in range(6):
            coef[1 + f, x] = faces[f]
        coef[7, x] = 1.0 / diagonal


def stencil_inside(coef, field, write):
    for x in range(4):
        for c in range(3):
            w = field[4 * c + x]
            beside = coef[3, x] * pltpu.roll(w, ROWS - 1, 0) + coef[4, x] * pltpu.roll(w, 1, 0)
            beside = beside + coef[5, x] * pltpu.roll(w, LANES - 1, 1)
            beside = beside + coef[6, x] * pltpu.roll(w, 1, 1)
            if x < 3:
                beside = beside + coef[1, x] * field[4 * c + x + 1]
            if x:
                beside = beside + coef[2, x] * field[4 * c + x - 1]
            write(c, x, coef[0, x] * w - beside)


def stencil_beyond(coef, sides, halo, write):
    for c in range(3):
        low, high = sides(c)
        for x in range(4):
            beside = coef[8, x] * ends_of(halo, 4 * c + x)
            if x == 0:
                beside = beside + coef[2, x] * low
            if x == 3:
                beside = beside + coef[1, x] * high
            write(c, x, beside)


def dot_rows(a, b):
    total = jnp.zeros((8, LANES), f32)
    for s in range(SLABS):
        total = total + jnp.sum((a[s] * b[s]).reshape(8, 8, LANES), axis=0)
    return jnp.sum(total, axis=0, keepdims=True)


def merge(u, gt, prof, mb):
    for c in range(3):
        total = u[4 * c] + u[4 * c + 1] + u[4 * c + 2] + u[4 * c + 3]
        prof[8 * c : 8 * c + 8] = jnp.sum(total.reshape(8, 8, LANES), axis=1) * (1.0 / 32.0)

    @pl.loop(0, KB // 32, unroll=8)
    def _(step):
        at = pl.multiple_of(step * 32, 32)
        totals = [jnp.zeros((32, LANES), f32)] * 3
        for g in range(GROUPS):
            b = gt[g, pl.ds(at, 32), :]
            for c in range(3):
                totals[c] = totals[c] + b * prof[8 * c + g : 8 * c + g + 1, :]
        for c in range(3):
            total = jnp.sum(totals[c], axis=1, keepdims=True)
            mb[pl.ds(c * KB + at, 32), :] = jnp.broadcast_to(total, (32, LANES))


def solve(factor, mb, sb):
    def rows_of(step, totals):
        totals = list(totals)
        for part in range(16):
            at = pl.multiple_of(step * 128 + part * 8, 8)
            m = mb[pl.ds(at, 8), :]
            for q in range(KC // LANES):
                totals[q] = totals[q] + factor[pl.ds(at, 8), LANES * q : LANES * (q + 1)] * m
        return tuple(totals)

    zero = jnp.zeros((8, LANES), f32)
    totals = lax.fori_loop(0, KC // 128, rows_of, (zero,) * (KC // LANES))
    for q in range(KC // LANES):
        row = jnp.sum(totals[q], axis=0, keepdims=True)
        sb[LANES * q : LANES * (q + 1), :] = jnp.broadcast_to(row, (LANES, LANES)).T


def solve_own(own, mb, pay):
    def rows_of(step, totals):
        totals = list(totals)
        for part in range(32):
            at = pl.multiple_of(step * 256 + part * 8, 8)
            m = mb[pl.ds(at, 8), :]
            for q in range(2):
                r = 2 * (part % 4) + q
                totals[r] = totals[r] + own[pl.ds(at, 8), LANES * q : LANES * (q + 1)] * m
        return tuple(totals)

    zero = jnp.zeros((8, LANES), f32)
    t = lax.fori_loop(0, KC // 256, rows_of, (zero,) * 8)
    pay[0] = zero
    for q in range(2):
        total = (t[q] + t[2 + q]) + (t[4 + q] + t[6 + q])
        pay[0, q : q + 1, :] = jnp.sum(total, axis=0, keepdims=True)


def unpack(tile_of, sb):
    for g in range(GROUPS):
        at = g * (KC // GROUPS)
        tile = tile_of(g)
        left = jnp.broadcast_to(tile[0:1, :], (LANES, LANES)).T
        right = jnp.broadcast_to(tile[1:2, :], (LANES, LANES)).T
        sb[at : at + LANES, :] = left
        sb[at + LANES : at + KC // GROUPS, :] = right[: KC // GROUPS - LANES]


def spread_over(gt, sb, spread):
    def spread_of(step, totals):
        totals = list(totals)
        for part in range(8):
            at = pl.multiple_of(step * 64 + part * 8, 8)
            solved = [sb[pl.ds(c * KB + at, 8), :] for c in range(3)]
            for g in range(GROUPS):
                b = gt[g, pl.ds(at, 8), :]
                for c in range(3):
                    totals[8 * c + g] = totals[8 * c + g] + b * solved[c]
        return tuple(totals)

    zero = jnp.zeros((8, LANES), f32)
    totals = lax.fori_loop(0, KB // 64, spread_of, (zero,) * 24)
    for r in range(24):
        spread[r : r + 1, :] = jnp.sum(totals[r], axis=0, keepdims=True)


def coarse(u, gt, factor, prof, mb, sb, spread):
    merge(u, gt, prof, mb)
    solve(factor, mb, sb)
    spread_over(gt, sb, spread)


def finish_direction(place, u, coef, spread, v, near, far, edge):
    for x in range(4):
        for c in range(3):
            s = 4 * c + x
            wide = jnp.broadcast_to(spread[8 * c : 8 * c + 8, :][:, None, :], (8, 8, LANES))
            v[s] = u[s] * coef[7, x] + wide.reshape(ROWS, LANES)
    if near is not None:
        hand_over(place, v, near, far, edge)


def hand_over(place, v, near, far, edge):
    for c in range(3):
        near[c] = v[4 * c + 3 - 3 * place[0]]
        far[c] = v[4 * c + 3 * place[0]]
    edge[...] = edge_of(lambda i: v[i], SLABS, lane_ids())


def basis_coefs(span, k):
    half = 0.5 * span
    if k == 0:
        return half, None, 1.0 / half
    return half, 0.5 * half, 2.0 / half


def local_kernel(place, force, viscosity, basis, copies, near, far, edge):
    shares = []
    for c in range(3):
        total = force[4 * c] + force[4 * c + 1] + force[4 * c + 2] + force[4 * c + 3]
        row = jnp.sum(total, axis=0, keepdims=True) * (1.0 / 32.0)
        column = jnp.broadcast_to(row, (LANES, LANES)).T
        for q in range(KB // LANES):
            part = basis[:, LANES * q : LANES * (q + 1)] * column
            shares.append(jnp.sum(part, axis=0, keepdims=True))
    rows = lax.broadcasted_iota(jnp.int32, (8, LANES), 0)
    lanes = lax.broadcasted_iota(jnp.int32, (8, LANES), 1)
    for q in range(2):
        tile = jnp.zeros((8, LANES), f32)
        for r in range(8):
            if 8 * q + r < len(shares):
                tile = jnp.where(rows == r, shares[8 * q + r], tile)
        for g in range(GROUPS):
            copies[g, q] = tile
    near[...] = viscosity[3 - 3 * place[0]]
    far[...] = viscosity[3 * place[0]]
    columns = jnp.zeros((8, LANES), f32)
    for x in range(4):
        moved = pltpu.roll(viscosity[x], 2 * x + 1, 1)
        columns = jnp.where((lanes == 2 * x) | (lanes == 2 * x + 1), moved, columns)
    edge[...] = columns


def begin_kernel(place, pays, own, vnear, vfar, enear, efar, copies, mb, pay):
    for q in range(2):
        total = tree([pays[g, q] for g in range(GROUPS)])
        for r in range(8):
            at = LANES * (8 * q + r)
            if at < KC:
                row = jnp.broadcast_to(total[r : r + 1, :], (LANES, LANES))
                mb[at : at + LANES, :] = row.T
    solve_own(own, mb, pay)
    for g in range(GROUPS):
        copies[g, 0] = pay[0]
        for i, tile in enumerate((vnear, vfar, enear, efar)):
            copies[g, 1 + i] = tile[...]


def start_kernel(place, pays, whole,
                 coef, v, near, far, edge, gram, vh, fields, gt, sb, spread, arrived):
    copy = pltpu.make_async_copy(whole.at[:, pl.ds(0, KB)], gt, arrived)
    copy.start()
    unpack(lambda g: pays[g, 0], sb)
    for g in range(GROUPS):
        for s in range(SLABS + 4):
            fields[s, 8 * g : 8 * g + 8, :] = whole[g, KB + 8 * s : KB + 8 * s + 8, :]
        for i in range(4):
            vh[i, 8 * g : 8 * g + 8, :] = pays[g, 1 + i]
    low, high = faces_of(place, vh[0], vh[1])
    halo = merge_edges(place, vh[2], vh[3])
    store_coefs(coef, lambda x: fields[SLABS + x], low, high, halo)
    copy.wait()
    spread_over(gt, sb, spread)
    finish_direction(place, fields, coef, spread, v, near, far, edge)
    gram[...] = jnp.zeros(GRAM, f32)
    gram[0:1, :] = dot_rows(v, fields)


def inside_kernel(place, v, coef, image):
    def write(c, x, value):
        image[4 * c + x] = value

    stencil_inside(coef, v, write)


def image_kernel(place, v, near, far, edge_near, edge_far, coef, gram, inside, image, sums):
    halo = merge_edges(place, edge_near[...], edge_far[...])

    def write(c, x, value):
        image[4 * c + x] = inside[4 * c + x] - value

    stencil_beyond(coef, lambda c: faces_of(place, near[c], far[c]), halo, write)
    rows = lax.broadcasted_iota(jnp.int32, (8, LANES), 0)
    sums[...] = jnp.where(rows == 0, gram[0:1, :], jnp.where(rows == 1, dot_rows(v, image), 0.0))


def merge_kernel(place, image, gt, own, pay, prof, mb):
    merge(image, gt, prof, mb)
    solve_own(own, mb, pay)


def carry_kernel(place, pay, crossed, copies):
    for i in range(PLACES):
        copies[i, 0] = pay[0]
        copies[i, 1] = crossed[...]


def first_kernel(place, both, image, u0, v0, coef, gt,
                 span, u, v, near, far, edge, sb, spread):
    sums = jnp.sum(tree([both[i, 1] for i in range(PLACES)]), axis=1, keepdims=True)
    width = SPAN * sums[1:2, :] / sums[0:1, :]
    span[...] = jnp.broadcast_to(width, (8, LANES))
    shift, _, scale = basis_coefs(width, 0)
    unpack(lambda g: both[4 * g + place[5], 0], sb)
    spread_over(gt, sb, spread)
    finish_direction(place, image, coef, spread, v, None, None, None)
    for s in range(SLABS):
        u[s] = (image[s] - shift * u0[s]) * scale
        v[s] = (v[s] - shift * v0[s]) * scale
    hand_over(place, v, near, far, edge)


def residual_kernel(place, span, hnear, hfar, enear, efar, coef, inside, gt, own,
                    u, pay, prof, mb):
    next_residual(place, False, span, hnear, hfar, enear, efar, coef, inside, u)
    merge(u, gt, prof, mb)
    solve_own(own, mb, pay)


def direction_kernel(place, pays, coef, gt, u, v, near, far, edge, sb, spread):
    unpack(lambda g: pays[g, 0], sb)
    spread_over(gt, sb, spread)
    finish_direction(place, u, coef, spread, v, near, far, edge)


def beside_kernel(k, place, span, gram_in, coef, *refs):
    refs, (gram, inside) = refs[:-2], refs[-2:]
    vs, us = refs[: k + 1], refs[k + 1 :]
    uk = us[0]
    if k:
        store_dots(gram, gram_in, vs[:-1], uk, vs[-1])
    else:
        gram[...] = gram_in[...]
    shift, back, scale = basis_coefs(span[0:1, 0:1], k)

    def write(c, x, value):
        s = 4 * c + x
        value = value - shift * uk[s]
        if k:
            value = value - back * us[1][s]
        inside[s] = value * scale

    stencil_inside(coef, vs[-1], write)


def tree(parts):
    while len(parts) > 1:
        parts = [parts[i] + parts[i + 1] for i in range(0, len(parts), 2)]
    return parts[0]


def pack_sums(gram, copies):
    sums = jnp.sum(gram[...], axis=1, keepdims=True)
    lanes = lax.broadcasted_iota(jnp.int32, (8, LANES), 1)
    tile = jnp.zeros((8, LANES), f32)
    for q in range(GRAM[0] // 8):
        tile = jnp.where(lanes == q, sums[8 * q : 8 * q + 8], tile)
    for i in range(PLACES):
        copies[i] = tile


def store_dots(gram, gram_in, vs, u, v=None):
    gram[...] = gram_in[...]
    vs = list(vs) + ([] if v is None else [v])
    totals = [jnp.zeros((8, LANES), f32)] * len(vs)
    for s in range(SLABS):
        us = u[s]
        for i, vi in enumerate(vs):
            totals[i] = totals[i] + jnp.sum((vi[s] * us).reshape(8, 8, LANES), axis=0)
    level = len(vs) - (0 if v is None else 1)
    for i, total in enumerate(totals):
        r = gram_row(i, level)
        gram[r : r + 1, :] = jnp.sum(total, axis=0, keepdims=True)


def next_residual(place, first, span, near, far, edge_near, edge_far, coef, inside, u):
    halo = merge_edges(place, edge_near[...], edge_far[...])
    scale = basis_coefs(span[0:1, 0:1], 0 if first else 1)[2]

    def write(c, x, value):
        u[4 * c + x] = inside[4 * c + x] - value * scale

    stencil_beyond(coef, lambda c: faces_of(place, near[c], far[c]), halo, write)


def step_kernel(first, place, span, hnear, hfar, enear, efar, coef, inside, gt, factor,
                u, v, near, far, edge, prof, mb, sb, spread):
    next_residual(place, first, span, hnear, hfar, enear, efar, coef, inside, u)
    coarse(u, gt, factor, prof, mb, sb, spread)
    finish_direction(place, u, coef, spread, v, near, far, edge)


def last_kernel(place, span, hnear, hfar, enear, efar, coef, inside, gram_in,
                v0, v1, v2, v3, v4, copies, u, gram):
    vs = (v0, v1, v2, v3, v4)
    next_residual(place, False, span, hnear, hfar, enear, efar, coef, inside, u)
    store_dots(gram, gram_in, vs, u)
    pack_sums(gram, copies)


def well_posed(n):
    rows = []
    good = None
    for j in range(S):
        row = []
        pivot = n[j][j]
        for i in range(j):
            value = n[i][j]
            for t in range(i):
                value = value - rows[i][t] * row[t]
            row.append(value)
            pivot = pivot - value * value / rows[i][i]
        row.append(pivot)
        apart = jnp.where(pivot > APART * n[j][j], 1.0, 0.0)
        good = apart if good is None else good * apart
        rows.append([value / rows[i][i] for i, value in enumerate(row[:j])] + [pivot])
    return good


def krylov_weights(span, sums):
    def product(i, j):
        r = gram_row(i, j)
        return sums[r // 8][r % 8 : r % 8 + 1, :]

    n = [[product(i, j) for j in range(S + 1)] for i in range(S)]
    half = 0.5 * span
    quarter = 0.5 * half

    def operate(p):
        out = [None] * (S + 1)

        def put(i, value):
            out[i] = value if out[i] is None else out[i] + value

        for j, w in enumerate(p):
            put(j, half * w)
            put(j + 1, (half if j == 0 else quarter) * w)
            if j:
                put(j - 1, quarter * w)
        return out[: len(p) + 1]

    def pair(a, b):
        total = None
        for i, ai in enumerate(a):
            part = None
            for j, bj in enumerate(b):
                term = n[i][j] * bj
                part = term if part is None else part + term
            total = ai * part if total is None else total + ai * part
        return total

    one = jnp.ones_like(span)
    r, p = [one], [one]
    x = []
    norm = n[0][0]
    for k in range(S):
        image = operate(p)
        alpha = norm / pair(p, image)
        for j, w in enumerate(p):
            if j < len(x):
                x[j] = x[j] + alpha * w
            else:
                x.append(alpha * w)
        r = [(r[j] - alpha * w) if j < len(r) else -(alpha * w) for j, w in enumerate(image)]
        if k + 1 < S:
            fresh = pair(r, r)
            beta = fresh / norm
            p = [r[j] + beta * p[j] if j < len(p) else r[j] for j in range(len(r))]
            norm = fresh
    return x, well_posed(n)


def weights_of(span, tiles):
    total = tree([tiles[i] for i in range(PLACES)])
    columns = [total[:, q : q + 1] for q in range(GRAM[0] // 8)]
    return krylov_weights(span[0:1, 0:1], columns)


def combine(x, parts, before=None):
    total = x[0] * parts[0]
    for j in range(1, S):
        total = total + x[j] * parts[j]
    return total if before is None else before + total


def combine_kernel(place, span, tiles, fields, vh,
                   v0, v1, v2, v3, v4, n0, n1, n2, n3, n4, f0, f1, f2, f3, f4,
                   en0, en1, en2, en3, en4, ef0, ef1, ef2, ef3, ef4,
                   flow):
    x, good = weights_of(span, tiles)
    vs = (v0, v1, v2, v3, v4)
    ns, fs = (n0, n1, n2, n3, n4), (f0, f1, f2, f3, f4)
    ens, efs = (en0, en1, en2, en3, en4), (ef0, ef1, ef2, ef3, ef4)
    for s in range(SLABS):
        flow[s] = combine(x, [t[s] for t in vs])
    for c in range(3):
        flow[12 + c], flow[15 + c] = faces_of(
            place, combine(x, [t[c] for t in ns]), combine(x, [t[c] for t in fs]))
    halo = merge_edges(
        place, combine(x, [t[...] for t in ens]), combine(x, [t[...] for t in efs]))

    def thinned(viscosity, a, b, c):
        return viscosity / (1.0 + 25.0 * (a * a + b * b + c * c))

    for i in range(4):
        flow[18 + i] = thinned(fields[SLABS + i], flow[i], flow[4 + i], flow[8 + i])
    vis_low, vis_high = faces_of(place, vh[0], vh[1])
    flow[22] = thinned(vis_low, flow[12], flow[13], flow[14])
    flow[23] = thinned(vis_high, flow[15], flow[16], flow[17])
    second = pltpu.roll(halo, LANES - 8, 1)
    third = pltpu.roll(halo, LANES - 16, 1)
    flow[24] = thinned(merge_edges(place, vh[2], vh[3]), halo, second, third)
    flow[25] = halo
    flow[26] = jnp.broadcast_to(good, EDGE)


def restart_kernel(place, flow, fields, gt, factor_in,
                   coef, u, v, near, far, edge, gram, factor, prof, mb, sb, spread, arrived):
    fetch = pltpu.make_async_copy(factor_in, factor, arrived)
    fetch.start()
    store_coefs(coef, lambda i: flow[18 + i], flow[22], flow[23], flow[24])

    def write(c, i, value):
        u[4 * c + i] = fields[4 * c + i] - value

    stencil_inside(coef, flow, write)

    def write_beyond(c, i, value):
        u[4 * c + i] = u[4 * c + i] + value

    stencil_beyond(coef, lambda c: (flow[12 + c], flow[15 + c]), flow[25], write_beyond)
    merge(u, gt, prof, mb)
    fetch.wait()
    solve(factor, mb, sb)
    spread_over(gt, sb, spread)
    finish_direction(place, u, coef, spread, v, near, far, edge)
    gram[...] = jnp.zeros(GRAM, f32)
    gram[0:1, :] = dot_rows(v, u)


def end_kernel(place, span, tiles, flow,
               v0, v1, v2, v3, v4, n0, n1, n2, n3, n4, f0, f1, f2, f3, f4,
               en0, en1, en2, en3, en4, ef0, ef1, ef2, ef3, ef4,
               velocity, pressure, good, cross):
    lanes = lax.broadcasted_iota(jnp.int32, (8, LANES), 1)
    rows = row_ids()
    x, good_now = weights_of(span, tiles)
    good[0, 0] = jnp.min(good_now * flow[26][0:1, 0:1])
    vs = (v0, v1, v2, v3, v4)
    ns, fs = (n0, n1, n2, n3, n4), (f0, f1, f2, f3, f4)
    ens, efs = (en0, en1, en2, en3, en4), (ef0, ef1, ef2, ef3, ef4)
    own = pl.ds(pl.multiple_of(place[4] * 8, 8), 8)
    for s in range(SLABS):
        velocity[s] = combine(x, [t[s, own, :] for t in vs], flow[s, own, :])
    near = combine(x, [t[0, own, :] for t in ns])
    far = combine(x, [t[0, own, :] for t in fs])
    odd = jnp.full((8, LANES), place[0], jnp.int32) == 1
    far = jnp.where(jnp.full((8, LANES), place[1], jnp.int32) == 1, far, 0.0)
    low = flow[12, own, :] + jnp.where(odd, near, far)
    high = flow[15, own, :] + jnp.where(odd, far, near)
    cross[0] = flow[25] + merge_edges(
        place, combine(x, [t[...] for t in ens]), combine(x, [t[...] for t in efs]))
    halo = cross[0, own, :]
    for i in range(4):
        vis = flow[18 + i, own, :]
        up = velocity[i + 1] if i < 3 else high
        down = velocity[i - 1] if i else low
        w = combine(x, [t[4 + i] for t in vs], flow[4 + i])
        yp = jnp.where(rows == ROWS - 1, 0.0, pltpu.roll(w, ROWS - 1, 0))
        ym = jnp.where(rows == 0, 0.0, pltpu.roll(w, 1, 0))
        cross[1 + i] = yp - ym
        zp, zm = along_z(velocity[8 + i], halo, 8 + i, lanes)
        divergence = 0.5 * (up - down) + 0.5 * cross[1 + i, own, :] + 0.5 * (zp - zm)
        pressure[i] = -(vis / (1.0 + vis)) * divergence


def call(kernel, outs, scratch, place, *args, far_away=None, beside=False):
    vmem = pl.BlockSpec(memory_space=pltpu.VMEM)
    places = [pl.BlockSpec(memory_space=pltpu.SMEM)] + [vmem] * len(args)
    if far_away is not None:
        places[1 + far_away] = pl.BlockSpec(memory_space=pl.ANY)
    cost = None
    if beside:
        size = sum(a.size for a in args)
        cost = pl.CostEstimate(flops=2 * size, bytes_accessed=4 * size, transcendentals=0)
    return pl.pallas_call(
        kernel,
        out_shape=[jax.ShapeDtypeStruct(o, f32) for o in outs],
        in_specs=places,
        out_specs=[pl.BlockSpec(memory_space=pltpu.SMEM) if o == (1, 1) else vmem for o in outs],
        scratch_shapes=[pltpu.VMEM(s, f32) if isinstance(s, tuple) else s for s in scratch],
        cost_estimate=cost,
        compiler_params=pltpu.CompilerParams(vmem_limit_bytes=20 * 2**20),
    )(place, *args)


MERGE = ((24, LANES), (KC, LANES))
SPREAD = ((KC, LANES), (24, LANES))
DIRECTION = (FIELD, FACE, FACE, EDGE, GRAM)


def swap_near(value, axis):
    return lax.ppermute(value, axis, [(i, i ^ 1) for i in range(lax.axis_size(axis))])


def swap_far(value, axis):
    count = lax.axis_size(axis)
    pairs = [(i, (i + 1) % count) for i in range(1, count, 2)]
    return lax.ppermute(value, axis, pairs + [(b, a) for a, b in pairs])


def swapped(near, far, edge):
    near_face = swap_near(near, "cap")
    far_face = swap_far(far, "cap")
    near_edge = swap_near(edge, "sub")
    far_edge = swap_far(edge, "sub")
    return near_face, far_face, near_edge, far_edge


def shared(copies):
    return lax.all_to_all(copies, ("cap", "sub"), 0, 0)


def crossed(value):
    caps, groups, subs = (lax.axis_size(axis) for axis in ("cap", "grp", "sub"))

    def at(cap, grp, sub):
        return (cap * groups + grp) * subs + sub

    pairs = [
        (at(c ^ g, g, b), at(c, g, b))
        for c in range(caps) for g in range(groups) for b in range(subs)
    ]
    return lax.ppermute(value, ("cap", "grp", "sub"), pairs)


def exchanged(pay):
    copies = jnp.broadcast_to(pay[None], (GROUPS,) + pay.shape)
    return lax.all_to_all(copies, "grp", 0, 0)


def body(right_side, viscosity, coarse_basis, coarse_factor):
    cap, sub = lax.axis_index("cap"), lax.axis_index("sub")
    caps, subs = lax.axis_size("cap"), lax.axis_size("sub")
    place = jnp.stack([
        cap % 2, (cap != 0) & (cap != caps - 1),
        sub % 2, (sub != 0) & (sub != subs - 1),
        lax.axis_index("grp"), sub,
    ]).astype(jnp.int32)
    basis = coarse_basis[0, 0]
    force = right_side.reshape(SLABS, 8, LANES)
    own_gt = jnp.concatenate(
        [basis.T.reshape(KB // 8, 8, LANES), force, viscosity], axis=0)
    whole = lax.all_gather(own_gt, "grp", axis=0).reshape(GROUPS, -1, LANES)

    copies, near, far, edge = call(
        local_kernel, ((GROUPS, 2, 8, LANES),) + ((8, LANES),) * 3, (),
        place, force, viscosity, basis)
    vhalos = swapped(near, far, edge)
    vhalos, rows, _ = lax.optimization_barrier((vhalos, coarse_factor[0, 0], own_gt))
    factor = gathered = lax.all_gather(rows, "grp", axis=0, tiled=True)
    own = jnp.pad(coarse_factor[0, 0].T, ((0, 0), (0, 2 * LANES - KC // GROUPS)))
    (copies,) = call(
        begin_kernel, ((GROUPS, 5, 8, LANES),), ((KC, LANES), (1, 8, LANES)),
        place, lax.all_to_all(copies, "grp", 0, 0), own, *vhalos)
    coef, v, near, far, edge, gram, vh, fields, gt = call(
        start_kernel,
        (COEF,) + DIRECTION
        + ((4, ROWS, LANES), (SLABS + 4, ROWS, LANES), (GROUPS, KB, LANES)),
        SPREAD + (pltpu.SemaphoreType.DMA(()),),
        place, lax.all_to_all(copies, "grp", 0, 0), whole)
    u = fields
    for picard in range(2):
        us, vs, halos = [u], [v], []
        for k in range(S):
            beyond = swapped(near, far, edge)
            if picard == 0 and k == 0:
                (inside,) = call(inside_kernel, (FIELD,), (), place, v, coef, beside=True)
            else:
                gram, inside = call(
                    functools.partial(beside_kernel, k), (GRAM, FIELD), (),
                    place, span, gram, coef, *vs, *us[::-1][:2], beside=True)
            beyond, gram, inside = lax.optimization_barrier((beyond, gram, inside))
            halos.append(beyond)
            if k + 1 == S:
                (copies,) = call(
                    last_kernel, ((PLACES, 8, LANES),), (FIELD, GRAM),
                    place, span, *beyond, coef, inside, gram, *vs)
                break
            if picard == 0 and k == 0:
                image, sums = call(
                    image_kernel, (FIELD, (8, LANES)), (),
                    place, v, *beyond, coef, gram, inside)
                other = crossed(sums)
                (pay,) = call(
                    merge_kernel, ((1, 8, LANES),), MERGE, place, image, gt, own, beside=True)
                (copies,) = call(carry_kernel, ((PLACES, 2, 8, LANES),), (), place, pay, other)
                span, u, v, near, far, edge = call(
                    first_kernel, ((8, LANES), FIELD) + DIRECTION[:4], SPREAD,
                    place, lax.all_to_all(copies, ("grp", "sub"), 0, 0), image, u, v, coef, gt)
            elif picard == 0:
                u, pay = call(
                    residual_kernel, (FIELD, (1, 8, LANES)), MERGE,
                    place, span, *beyond, coef, inside, gt, own)
                v, near, far, edge = call(
                    direction_kernel, DIRECTION[:4], SPREAD,
                    place, exchanged(pay), coef, gt, u)
            else:
                u, v, near, far, edge = call(
                    functools.partial(step_kernel, k == 0), (FIELD,) + DIRECTION[:4],
                    MERGE + SPREAD, place, span, *beyond, coef, inside, gt, factor)
            us.append(u)
            vs.append(v)
        tiles = shared(copies)
        kept = vs + [h[side] for side in range(4) for h in halos]
        if picard == 0:
            (flow,) = call(combine_kernel, (FLOW,), (), place, span, tiles, fields, vh, *kept)
            coef, u, v, near, far, edge, gram, factor = call(
                restart_kernel, (COEF, FIELD) + DIRECTION + ((KC, KC),),
                MERGE + SPREAD + (pltpu.SemaphoreType.DMA(()),),
                place, flow, fields, gt, factor, far_away=3)
        else:
            result, pressure, good = call(
                end_kernel, ((SLABS, 8, LANES), (4, 8, LANES), (1, 1)),
                ((5, ROWS, LANES),), place, span, tiles, flow, *kept)
    given, good = lax.optimization_barrier(
        ((right_side, viscosity, coarse_basis, gathered), good))
    return lax.cond(
        good[0, 0] > 0.5,
        lambda *_: (result.reshape(3, 4, 8, LANES), pressure),
        stepwise,
        *given)


exact_mode = lax.Precision.HIGHEST


def padded_2(block, sides, width):
    for axis, dim in sides:
        count = lax.axis_size(axis)
        forward = [(i, i + 1) for i in range(count - 1)]
        backward = [(target, source) for source, target in forward]
        low = lax.ppermute(
            lax.slice_in_dim(block, block.shape[dim] - width, None, axis=dim), axis, forward
        )
        high = lax.ppermute(lax.slice_in_dim(block, 0, width, axis=dim), axis, backward)
        block = jnp.concatenate([low, block, high], axis=dim)
    return block


def stencil_faces(padded):
    centre = padded[1:-1, 1:-1, 1:-1]
    faces = (
        0.5 * (centre + padded[2:, 1:-1, 1:-1]),
        0.5 * (centre + padded[:-2, 1:-1, 1:-1]),
        0.5 * (centre + padded[1:-1, 2:, 1:-1]),
        0.5 * (centre + padded[1:-1, :-2, 1:-1]),
        0.5 * (centre + padded[1:-1, 1:-1, 2:]),
        0.5 * (centre + padded[1:-1, 1:-1, :-2]),
    )
    diagonal = 1.0 + faces[0] + faces[1] + faces[2] + faces[3] + faces[4] + faces[5]
    return (faces, diagonal)


def apply_stencil(padded_field, field, faces, diagonal):
    beside = (
        faces[0] * padded_field[:, 2:, 1:-1, 1:-1] + faces[1] * padded_field[:, :-2, 1:-1, 1:-1]
    )
    beside = (
        beside
        + faces[2] * padded_field[:, 1:-1, 2:, 1:-1]
        + faces[3] * padded_field[:, 1:-1, :-2, 1:-1]
    )
    beside = (
        beside
        + faces[4] * padded_field[:, 1:-1, 1:-1, 2:]
        + faces[5] * padded_field[:, 1:-1, 1:-1, :-2]
    )
    return diagonal * field - beside


def divergence_of(padded_field):
    result = 0.5 * (padded_field[0, 2:, 1:-1, 1:-1] - padded_field[0, :-2, 1:-1, 1:-1])
    result = result + 0.5 * (padded_field[1, 1:-1, 2:, 1:-1] - padded_field[1, 1:-1, :-2, 1:-1])
    return result + 0.5 * (padded_field[2, 1:-1, 1:-1, 2:] - padded_field[2, 1:-1, 1:-1, :-2])


def velocity_padded(field):
    return padded_2(field, (("cap", 1), ("grp", 2), ("sub", 3)), 1)


def curvature_sum(direction, image):
    return lax.psum(jnp.sum(direction * image), ("cap", "grp", "sub"))


def norm_sum(residual, precond):
    return lax.psum(jnp.sum(residual * precond), ("cap", "grp", "sub"))


def stepwise(right_side, viscosity, coarse_basis, whole_factor):
    basis_local = coarse_basis[0, 0]

    def precondition(residual, diagonal):
        profile = jnp.mean(residual, axis=(1, 2))
        local = jnp.dot(profile, basis_local, precision=exact_mode)
        merged = lax.psum(local, "grp").reshape(-1)
        solved = jnp.dot(whole_factor, merged, precision=exact_mode)
        spread = jnp.dot(solved.reshape(3, -1), basis_local.T, precision=exact_mode)
        return residual / diagonal + spread[:, None, None, :]

    velocity = jnp.zeros_like(right_side)
    viscous = viscosity
    for picard in range(2):
        if picard > 0:
            viscous = viscosity / (1.0 + 25.0 * jnp.sum(velocity * velocity, axis=0))
        padded_viscous = padded_2(viscous, (("cap", 0), ("grp", 1), ("sub", 2)), 1)
        faces, diagonal = stencil_faces(padded_viscous)

        def operate(field):
            return apply_stencil(velocity_padded(field), field, faces, diagonal)

        residual = right_side - operate(velocity)
        precond = precondition(residual, diagonal)
        norm_now = norm_sum(residual, precond)
        direction = precond
        for krylov_step in range(S):
            image = operate(direction)
            alpha = norm_now / curvature_sum(direction, image)
            velocity = velocity + alpha * direction
            residual = residual - alpha * image
            if krylov_step + 1 < S:
                precond = precondition(residual, diagonal)
                fresh = norm_sum(residual, precond)
                direction = precond + fresh / norm_now * direction
                norm_now = fresh
    pressure = -(viscous / (1.0 + viscous)) * divergence_of(velocity_padded(velocity))
    return (velocity, pressure)


def solution(mesh):
    placed = (
        P(None, "cap", "grp", "sub"),
        P("cap", "grp", "sub"),
        P("cap", "grp", "sub", None),
        P("cap", "sub", "grp", None),
    )
    return jax.shard_map(
        body,
        mesh=mesh,
        in_specs=placed,
        out_specs=(P(None, "cap", "grp", "sub"), P("cap", "grp", "sub")),
        check_vma=False,
    )
```

```python
import functools

import jax
import jax.numpy as jnp
from jax import lax
from jax.experimental import pallas as pl
from jax.experimental.pallas import tpu as pltpu
from jax.sharding import PartitionSpec as P

S = 5
SLABS = 12
ROWS = 64
LANES = 128
GROUPS = 8
KB = 512
KC = 1536
APART = 1e-3
SPAN = 2.6
FIELD = (SLABS, ROWS, LANES)
FACE = (3, ROWS, LANES)
EDGE = (ROWS, LANES)
PACKED = (ROWS // 4, LANES)
GRAM = (24, LANES)
PLACES = 32
FLOW = (27, ROWS, LANES)
COEF = (9, 4, ROWS, LANES)
f32 = jnp.float32


def gram_row(i, j):
    i, j = min(i, j), max(i, j)
    return sum(min(t, S - 1) + 1 for t in range(j)) + i


def lane_ids():
    return lax.broadcasted_iota(jnp.int32, (ROWS, LANES), 1)


def row_ids():
    return lax.broadcasted_iota(jnp.int32, (ROWS, LANES), 0)


def ends_of(halo, i):
    return pltpu.roll(halo, LANES - 1 - 2 * i, 1)


def along_z(w, halo, i, lanes):
    ends = ends_of(halo, i)
    after = jnp.where(lanes == LANES - 1, ends, pltpu.roll(w, LANES - 1, 1))
    before = jnp.where(lanes == 0, ends, pltpu.roll(w, 1, 1))
    return after, before


def flag(place, i):
    return jnp.full((ROWS, LANES), place[i], jnp.int32) == 1


def faces_of(place, near, far):
    odd, inner = flag(place, 0), flag(place, 1)
    far = jnp.where(inner, far, 0.0)
    return jnp.where(odd, near, far), jnp.where(odd, far, near)


def merge_edges(place, near, far):
    far = jnp.where(flag(place, 3), far, 0.0)
    odd = flag(place, 2)
    low, high = jnp.where(odd, near, far), jnp.where(odd, far, near)
    return jnp.where(lane_ids() % 2 == 1, pltpu.roll(low, 1, 1), pltpu.roll(high, LANES - 1, 1))


def edge_of(get, count, lanes):
    edge = jnp.zeros((ROWS, LANES), f32)
    for i in range(count):
        moved = pltpu.roll(get(i), 2 * i + 1, 1)
        edge = jnp.where((lanes == 2 * i) | (lanes == 2 * i + 1), moved, edge)
    return edge


def pack_edge(edge):
    lanes = lax.broadcasted_iota(jnp.int32, PACKED, 1)
    packed = edge[: PACKED[0]]
    for q in range(1, 4):
        part = pltpu.roll(edge[PACKED[0] * q : PACKED[0] * (q + 1)], 32 * q, 1)
        packed = jnp.where(lanes // 32 == q, part, packed)
    return packed


def unpack_edge(packed):
    parts = [packed] + [pltpu.roll(packed, LANES - 32 * q, 1) for q in range(1, 4)]
    return jnp.concatenate(parts, axis=0)


def store_coefs(coef, vis, low, high, halo):
    lanes, rows = lane_ids(), row_ids()
    for x in range(4):
        v = vis(x)
        up = vis(x + 1) if x < 3 else high
        down = vis(x - 1) if x else low
        yp = jnp.where(rows == ROWS - 1, 0.0, pltpu.roll(v, ROWS - 1, 0))
        ym = jnp.where(rows == 0, 0.0, pltpu.roll(v, 1, 0))
        zp, zm = along_z(v, halo, x, lanes)
        faces = [0.5 * (v + n) for n in (up, down, yp, ym, zp, zm)]
        diagonal = 1.0 + faces[0] + faces[1] + faces[2] + faces[3] + faces[4] + faces[5]
        faces[2] = jnp.where(rows == ROWS - 1, 0.0, faces[2])
        faces[3] = jnp.where(rows == 0, 0.0, faces[3])
        first, last = lanes == 0, lanes == LANES - 1
        coef[8, x] = jnp.where(first, faces[5], jnp.where(last, faces[4], 0.0))
        faces[4] = jnp.where(last, 0.0, faces[4])
        faces[5] = jnp.where(first, 0.0, faces[5])
        coef[0, x] = diagonal
        for f in range(6):
            coef[1 + f, x] = faces[f]
        coef[7, x] = 1.0 / diagonal


def stencil_inside(coef, field, write):
    for x in range(4):
        for c in range(3):
            w = field[4 * c + x]
            beside = coef[3, x] * pltpu.roll(w, ROWS - 1, 0) + coef[4, x] * pltpu.roll(w, 1, 0)
            beside = beside + coef[5, x] * pltpu.roll(w, LANES - 1, 1)
            beside = beside + coef[6, x] * pltpu.roll(w, 1, 1)
            if x < 3:
                beside = beside + coef[1, x] * field[4 * c + x + 1]
            if x:
                beside = beside + coef[2, x] * field[4 * c + x - 1]
            write(c, x, coef[0, x] * w - beside)


def stencil_beyond(coef, sides, halo, write):
    for c in range(3):
        low, high = sides(c)
        for x in range(4):
            beside = coef[8, x] * ends_of(halo, 4 * c + x)
            if x == 0:
                beside = beside + coef[2, x] * low
            if x == 3:
                beside = beside + coef[1, x] * high
            write(c, x, beside)


def dot_rows(a, b):
    total = jnp.zeros((8, LANES), f32)
    for s in range(SLABS):
        total = total + jnp.sum((a[s] * b[s]).reshape(8, 8, LANES), axis=0)
    return jnp.sum(total, axis=0, keepdims=True)


def merge(u, gt, prof, mb):
    for c in range(3):
        total = u[4 * c] + u[4 * c + 1] + u[4 * c + 2] + u[4 * c + 3]
        prof[8 * c : 8 * c + 8] = jnp.sum(total.reshape(8, 8, LANES), axis=1) * (1.0 / 32.0)

    @pl.loop(0, KB // 32, unroll=8)
    def _(step):
        at = pl.multiple_of(step * 32, 32)
        totals = [jnp.zeros((32, LANES), f32)] * 3
        for g in range(GROUPS):
            b = gt[g, pl.ds(at, 32), :]
            for c in range(3):
                totals[c] = totals[c] + b * prof[8 * c + g : 8 * c + g + 1, :]
        for c in range(3):
            total = jnp.sum(totals[c], axis=1, keepdims=True)
            mb[pl.ds(c * KB + at, 32), :] = jnp.broadcast_to(total, (32, LANES))


def solve(factor, mb, sb):
    def rows_of(step, totals):
        totals = list(totals)
        for part in range(16):
            at = pl.multiple_of(step * 128 + part * 8, 8)
            m = mb[pl.ds(at, 8), :]
            for q in range(KC // LANES):
                totals[q] = totals[q] + factor[pl.ds(at, 8), LANES * q : LANES * (q + 1)] * m
        return tuple(totals)

    zero = jnp.zeros((8, LANES), f32)
    totals = lax.fori_loop(0, KC // 128, rows_of, (zero,) * (KC // LANES))
    for q in range(KC // LANES):
        row = jnp.sum(totals[q], axis=0, keepdims=True)
        sb[LANES * q : LANES * (q + 1), :] = jnp.broadcast_to(row, (LANES, LANES)).T


def solve_own(own, mb, pay):
    def rows_of(step, totals):
        totals = list(totals)
        for part in range(32):
            at = pl.multiple_of(step * 256 + part * 8, 8)
            m = mb[pl.ds(at, 8), :]
            for q in range(2):
                r = 2 * (part % 4) + q
                totals[r] = totals[r] + own[pl.ds(at, 8), LANES * q : LANES * (q + 1)] * m
        return tuple(totals)

    zero = jnp.zeros((8, LANES), f32)
    t = lax.fori_loop(0, KC // 256, rows_of, (zero,) * 8)
    pay[0] = zero
    for q in range(2):
        total = (t[q] + t[2 + q]) + (t[4 + q] + t[6 + q])
        pay[0, q : q + 1, :] = jnp.sum(total, axis=0, keepdims=True)


def unpack(pays, sb):
    for g in range(GROUPS):
        at = g * (KC // GROUPS)
        left = jnp.broadcast_to(pays[g, 0, 0:1, :], (LANES, LANES)).T
        right = jnp.broadcast_to(pays[g, 0, 1:2, :], (LANES, LANES)).T
        sb[at : at + LANES, :] = left
        sb[at + LANES : at + KC // GROUPS, :] = right[: KC // GROUPS - LANES]


def spread_over(gt, sb, spread):
    def spread_of(step, totals):
        totals = list(totals)
        for part in range(8):
            at = pl.multiple_of(step * 64 + part * 8, 8)
            solved = [sb[pl.ds(c * KB + at, 8), :] for c in range(3)]
            for g in range(GROUPS):
                b = gt[g, pl.ds(at, 8), :]
                for c in range(3):
                    totals[8 * c + g] = totals[8 * c + g] + b * solved[c]
        return tuple(totals)

    zero = jnp.zeros((8, LANES), f32)
    totals = lax.fori_loop(0, KB // 64, spread_of, (zero,) * 24)
    for r in range(24):
        spread[r : r + 1, :] = jnp.sum(totals[r], axis=0, keepdims=True)


def coarse(u, gt, factor, prof, mb, sb, spread):
    merge(u, gt, prof, mb)
    solve(factor, mb, sb)
    spread_over(gt, sb, spread)


def finish_direction(place, u, coef, spread, v, near, far, edge):
    for x in range(4):
        for c in range(3):
            s = 4 * c + x
            wide = jnp.broadcast_to(spread[8 * c : 8 * c + 8, :][:, None, :], (8, 8, LANES))
            v[s] = u[s] * coef[7, x] + wide.reshape(ROWS, LANES)
    if near is not None:
        hand_over(place, v, near, far, edge)


def hand_over(place, v, near, far, edge):
    for c in range(3):
        near[c] = v[4 * c + 3 - 3 * place[0]]
        far[c] = v[4 * c + 3 * place[0]]
    edge[...] = pack_edge(edge_of(lambda i: v[i], SLABS, lane_ids()))


def basis_coefs(span, k):
    half = 0.5 * span
    if k == 0:
        return half, None, 1.0 / half
    return half, 0.5 * half, 2.0 / half


def local_kernel(place, force, viscosity, basis, copies, near, far, edge):
    shares = []
    for c in range(3):
        total = force[4 * c] + force[4 * c + 1] + force[4 * c + 2] + force[4 * c + 3]
        row = jnp.sum(total, axis=0, keepdims=True) * (1.0 / 32.0)
        column = jnp.broadcast_to(row, (LANES, LANES)).T
        for q in range(KB // LANES):
            part = basis[:, LANES * q : LANES * (q + 1)] * column
            shares.append(jnp.sum(part, axis=0, keepdims=True))
    rows = lax.broadcasted_iota(jnp.int32, (8, LANES), 0)
    lanes = lax.broadcasted_iota(jnp.int32, (8, LANES), 1)
    for q in range(2):
        tile = jnp.zeros((8, LANES), f32)
        for r in range(8):
            if 8 * q + r < len(shares):
                tile = jnp.where(rows == r, shares[8 * q + r], tile)
        for g in range(GROUPS):
            copies[g, q] = tile
    near[...] = viscosity[3 - 3 * place[0]]
    far[...] = viscosity[3 * place[0]]
    columns = jnp.zeros((8, LANES), f32)
    for x in range(4):
        moved = pltpu.roll(viscosity[x], 2 * x + 1, 1)
        columns = jnp.where((lanes == 2 * x) | (lanes == 2 * x + 1), moved, columns)
    edge[...] = columns


def begin_kernel(place, pays, own, vnear, vfar, enear, efar, copies, mb, pay):
    for q in range(2):
        total = tree([pays[g, q] for g in range(GROUPS)])
        for r in range(8):
            at = LANES * (8 * q + r)
            if at < KC:
                row = jnp.broadcast_to(total[r : r + 1, :], (LANES, LANES))
                mb[at : at + LANES, :] = row.T
    solve_own(own, mb, pay)
    for g in range(GROUPS):
        copies[g, 0] = pay[0]
        for i, tile in enumerate((vnear, vfar, enear, efar)):
            copies[g, 1 + i] = tile[...]


def start_kernel(place, pays, whole,
                 coef, v, near, far, edge, gram, vh, fields, gt, sb, spread, arrived):
    copy = pltpu.make_async_copy(whole.at[:, pl.ds(0, KB)], gt, arrived)
    copy.start()
    unpack(pays, sb)
    for g in range(GROUPS):
        for s in range(SLABS + 4):
            fields[s, 8 * g : 8 * g + 8, :] = whole[g, KB + 8 * s : KB + 8 * s + 8, :]
        for i in range(4):
            vh[i, 8 * g : 8 * g + 8, :] = pays[g, 1 + i]
    low, high = faces_of(place, vh[0], vh[1])
    halo = merge_edges(place, vh[2], vh[3])
    store_coefs(coef, lambda x: fields[SLABS + x], low, high, halo)
    copy.wait()
    spread_over(gt, sb, spread)
    finish_direction(place, fields, coef, spread, v, near, far, edge)
    gram[...] = jnp.zeros(GRAM, f32)
    gram[0:1, :] = dot_rows(v, fields)


def inside_kernel(place, v, coef, image):
    def write(c, x, value):
        image[4 * c + x] = value

    stencil_inside(coef, v, write)


def image_kernel(place, v, near, far, edge_near, edge_far, coef, gram, inside, image, copies):
    halo = merge_edges(place, unpack_edge(edge_near[...]), unpack_edge(edge_far[...]))

    def write(c, x, value):
        image[4 * c + x] = inside[4 * c + x] - value

    stencil_beyond(coef, lambda c: faces_of(place, near[c], far[c]), halo, write)
    rows = lax.broadcasted_iota(jnp.int32, (8, LANES), 0)
    tile = jnp.where(rows == 0, gram[0:1, :], jnp.where(rows == 1, dot_rows(v, image), 0.0))
    for i in range(PLACES):
        copies[i] = tile


def merge_kernel(place, image, gt, own, pay, prof, mb):
    merge(image, gt, prof, mb)
    solve_own(own, mb, pay)


def first_kernel(place, tiles, pays, image, u0, v0, coef, gt,
                 span, u, v, near, far, edge, sb, spread):
    sums = jnp.sum(tree([tiles[i] for i in range(PLACES)]), axis=1, keepdims=True)
    width = SPAN * sums[1:2, :] / sums[0:1, :]
    span[...] = jnp.broadcast_to(width, (8, LANES))
    shift, _, scale = basis_coefs(width, 0)
    unpack(pays, sb)
    spread_over(gt, sb, spread)
    finish_direction(place, image, coef, spread, v, None, None, None)
    for s in range(SLABS):
        u[s] = (image[s] - shift * u0[s]) * scale
        v[s] = (v[s] - shift * v0[s]) * scale
    hand_over(place, v, near, far, edge)


def residual_kernel(place, span, hnear, hfar, enear, efar, coef, inside, gt, own,
                    u, pay, prof, mb):
    next_residual(place, False, span, hnear, hfar, enear, efar, coef, inside, u)
    merge(u, gt, prof, mb)
    solve_own(own, mb, pay)


def direction_kernel(place, pays, coef, gt, u, v, near, far, edge, sb, spread):
    unpack(pays, sb)
    spread_over(gt, sb, spread)
    finish_direction(place, u, coef, spread, v, near, far, edge)


def beside_kernel(k, place, span, gram_in, coef, *refs):
    refs, (gram, inside) = refs[:-2], refs[-2:]
    vs, us = refs[: k + 1], refs[k + 1 :]
    uk = us[0]
    if k:
        store_dots(gram, gram_in, vs[:-1], uk, vs[-1])
    else:
        gram[...] = gram_in[...]
    shift, back, scale = basis_coefs(span[0:1, 0:1], k)

    def write(c, x, value):
        s = 4 * c + x
        value = value - shift * uk[s]
        if k:
            value = value - back * us[1][s]
        inside[s] = value * scale

    stencil_inside(coef, vs[-1], write)


def tree(parts):
    while len(parts) > 1:
        parts = [parts[i] + parts[i + 1] for i in range(0, len(parts), 2)]
    return parts[0]


def pack_sums(gram, copies):
    sums = jnp.sum(gram[...], axis=1, keepdims=True)
    lanes = lax.broadcasted_iota(jnp.int32, (8, LANES), 1)
    tile = jnp.zeros((8, LANES), f32)
    for q in range(GRAM[0] // 8):
        tile = jnp.where(lanes == q, sums[8 * q : 8 * q + 8], tile)
    for i in range(PLACES):
        copies[i] = tile


def store_dots(gram, gram_in, vs, u, v=None):
    gram[...] = gram_in[...]
    vs = list(vs) + ([] if v is None else [v])
    totals = [jnp.zeros((8, LANES), f32)] * len(vs)
    for s in range(SLABS):
        us = u[s]
        for i, vi in enumerate(vs):
            totals[i] = totals[i] + jnp.sum((vi[s] * us).reshape(8, 8, LANES), axis=0)
    level = len(vs) - (0 if v is None else 1)
    for i, total in enumerate(totals):
        r = gram_row(i, level)
        gram[r : r + 1, :] = jnp.sum(total, axis=0, keepdims=True)


def next_residual(place, first, span, near, far, edge_near, edge_far, coef, inside, u):
    halo = merge_edges(place, unpack_edge(edge_near[...]), unpack_edge(edge_far[...]))
    scale = basis_coefs(span[0:1, 0:1], 0 if first else 1)[2]

    def write(c, x, value):
        u[4 * c + x] = inside[4 * c + x] - value * scale

    stencil_beyond(coef, lambda c: faces_of(place, near[c], far[c]), halo, write)


def step_kernel(first, place, span, hnear, hfar, enear, efar, coef, inside, gt, factor,
                u, v, near, far, edge, prof, mb, sb, spread):
    next_residual(place, first, span, hnear, hfar, enear, efar, coef, inside, u)
    coarse(u, gt, factor, prof, mb, sb, spread)
    finish_direction(place, u, coef, spread, v, near, far, edge)


def last_kernel(place, span, hnear, hfar, enear, efar, coef, inside, gram_in,
                v0, v1, v2, v3, v4, copies, u, gram):
    vs = (v0, v1, v2, v3, v4)
    next_residual(place, False, span, hnear, hfar, enear, efar, coef, inside, u)
    store_dots(gram, gram_in, vs, u)
    pack_sums(gram, copies)


def well_posed(n):
    rows = []
    good = None
    for j in range(S):
        row = []
        pivot = n[j][j]
        for i in range(j):
            value = n[i][j]
            for t in range(i):
                value = value - rows[i][t] * row[t]
            row.append(value)
            pivot = pivot - value * value / rows[i][i]
        row.append(pivot)
        apart = jnp.where(pivot > APART * n[j][j], 1.0, 0.0)
        good = apart if good is None else good * apart
        rows.append([value / rows[i][i] for i, value in enumerate(row[:j])] + [pivot])
    return good


def krylov_weights(span, sums):
    def product(i, j):
        r = gram_row(i, j)
        return sums[r // 8][r % 8 : r % 8 + 1, :]

    n = [[product(i, j) for j in range(S + 1)] for i in range(S)]
    half = 0.5 * span
    quarter = 0.5 * half

    def operate(p):
        out = [None] * (S + 1)

        def put(i, value):
            out[i] = value if out[i] is None else out[i] + value

        for j, w in enumerate(p):
            put(j, half * w)
            put(j + 1, (half if j == 0 else quarter) * w)
            if j:
                put(j - 1, quarter * w)
        return out[: len(p) + 1]

    def pair(a, b):
        total = None
        for i, ai in enumerate(a):
            part = None
            for j, bj in enumerate(b):
                term = n[i][j] * bj
                part = term if part is None else part + term
            total = ai * part if total is None else total + ai * part
        return total

    one = jnp.ones_like(span)
    r, p = [one], [one]
    x = []
    norm = n[0][0]
    for k in range(S):
        image = operate(p)
        alpha = norm / pair(p, image)
        for j, w in enumerate(p):
            if j < len(x):
                x[j] = x[j] + alpha * w
            else:
                x.append(alpha * w)
        r = [(r[j] - alpha * w) if j < len(r) else -(alpha * w) for j, w in enumerate(image)]
        if k + 1 < S:
            fresh = pair(r, r)
            beta = fresh / norm
            p = [r[j] + beta * p[j] if j < len(p) else r[j] for j in range(len(r))]
            norm = fresh
    return x, well_posed(n)


def weights_of(span, tiles):
    total = tree([tiles[i] for i in range(PLACES)])
    columns = [total[:, q : q + 1] for q in range(GRAM[0] // 8)]
    return krylov_weights(span[0:1, 0:1], columns)


def combine(x, parts, before=None):
    total = x[0] * parts[0]
    for j in range(1, S):
        total = total + x[j] * parts[j]
    return total if before is None else before + total


def combine_kernel(place, span, tiles, fields, vh,
                   v0, v1, v2, v3, v4, n0, n1, n2, n3, n4, f0, f1, f2, f3, f4,
                   en0, en1, en2, en3, en4, ef0, ef1, ef2, ef3, ef4,
                   flow):
    x, good = weights_of(span, tiles)
    vs = (v0, v1, v2, v3, v4)
    ns, fs = (n0, n1, n2, n3, n4), (f0, f1, f2, f3, f4)
    ens, efs = (en0, en1, en2, en3, en4), (ef0, ef1, ef2, ef3, ef4)
    for s in range(SLABS):
        flow[s] = combine(x, [t[s] for t in vs])
    for c in range(3):
        flow[12 + c], flow[15 + c] = faces_of(
            place, combine(x, [t[c] for t in ns]), combine(x, [t[c] for t in fs]))
    halo = merge_edges(
        place, unpack_edge(combine(x, [t[...] for t in ens])),
        unpack_edge(combine(x, [t[...] for t in efs])))

    def thinned(viscosity, a, b, c):
        return viscosity / (1.0 + 25.0 * (a * a + b * b + c * c))

    for i in range(4):
        flow[18 + i] = thinned(fields[SLABS + i], flow[i], flow[4 + i], flow[8 + i])
    vis_low, vis_high = faces_of(place, vh[0], vh[1])
    flow[22] = thinned(vis_low, flow[12], flow[13], flow[14])
    flow[23] = thinned(vis_high, flow[15], flow[16], flow[17])
    second = pltpu.roll(halo, LANES - 8, 1)
    third = pltpu.roll(halo, LANES - 16, 1)
    flow[24] = thinned(merge_edges(place, vh[2], vh[3]), halo, second, third)
    flow[25] = halo
    flow[26] = jnp.broadcast_to(good, EDGE)


def restart_kernel(place, flow, fields, gt, factor_in,
                   coef, u, v, near, far, edge, gram, factor, prof, mb, sb, spread, arrived):
    fetch = pltpu.make_async_copy(factor_in, factor, arrived)
    fetch.start()
    store_coefs(coef, lambda i: flow[18 + i], flow[22], flow[23], flow[24])

    def write(c, i, value):
        u[4 * c + i] = fields[4 * c + i] - value

    stencil_inside(coef, flow, write)

    def write_beyond(c, i, value):
        u[4 * c + i] = u[4 * c + i] + value

    stencil_beyond(coef, lambda c: (flow[12 + c], flow[15 + c]), flow[25], write_beyond)
    merge(u, gt, prof, mb)
    fetch.wait()
    solve(factor, mb, sb)
    spread_over(gt, sb, spread)
    finish_direction(place, u, coef, spread, v, near, far, edge)
    gram[...] = jnp.zeros(GRAM, f32)
    gram[0:1, :] = dot_rows(v, u)


def end_kernel(place, span, tiles, flow,
               v0, v1, v2, v3, v4, n0, n1, n2, n3, n4, f0, f1, f2, f3, f4,
               en0, en1, en2, en3, en4, ef0, ef1, ef2, ef3, ef4,
               velocity, pressure, good, cross):
    lanes = lax.broadcasted_iota(jnp.int32, (8, LANES), 1)
    rows = row_ids()
    x, good_now = weights_of(span, tiles)
    good[0, 0] = jnp.min(good_now * flow[26][0:1, 0:1])
    vs = (v0, v1, v2, v3, v4)
    ns, fs = (n0, n1, n2, n3, n4), (f0, f1, f2, f3, f4)
    ens, efs = (en0, en1, en2, en3, en4), (ef0, ef1, ef2, ef3, ef4)
    own = pl.ds(pl.multiple_of(place[4] * 8, 8), 8)
    for s in range(SLABS):
        velocity[s] = combine(x, [t[s, own, :] for t in vs], flow[s, own, :])
    near = combine(x, [t[0, own, :] for t in ns])
    far = combine(x, [t[0, own, :] for t in fs])
    odd = jnp.full((8, LANES), place[0], jnp.int32) == 1
    far = jnp.where(jnp.full((8, LANES), place[1], jnp.int32) == 1, far, 0.0)
    low = flow[12, own, :] + jnp.where(odd, near, far)
    high = flow[15, own, :] + jnp.where(odd, far, near)
    cross[0] = flow[25] + merge_edges(
        place, unpack_edge(combine(x, [t[...] for t in ens])),
        unpack_edge(combine(x, [t[...] for t in efs])))
    halo = cross[0, own, :]
    for i in range(4):
        vis = flow[18 + i, own, :]
        up = velocity[i + 1] if i < 3 else high
        down = velocity[i - 1] if i else low
        w = combine(x, [t[4 + i] for t in vs], flow[4 + i])
        yp = jnp.where(rows == ROWS - 1, 0.0, pltpu.roll(w, ROWS - 1, 0))
        ym = jnp.where(rows == 0, 0.0, pltpu.roll(w, 1, 0))
        cross[1 + i] = yp - ym
        zp, zm = along_z(velocity[8 + i], halo, 8 + i, lanes)
        divergence = 0.5 * (up - down) + 0.5 * cross[1 + i, own, :] + 0.5 * (zp - zm)
        pressure[i] = -(vis / (1.0 + vis)) * divergence


def call(kernel, outs, scratch, place, *args, far_away=None, beside=False):
    vmem = pl.BlockSpec(memory_space=pltpu.VMEM)
    places = [pl.BlockSpec(memory_space=pltpu.SMEM)] + [vmem] * len(args)
    if far_away is not None:
        places[1 + far_away] = pl.BlockSpec(memory_space=pl.ANY)
    cost = None
    if beside:
        size = sum(a.size for a in args)
        cost = pl.CostEstimate(flops=2 * size, bytes_accessed=4 * size, transcendentals=0)
    return pl.pallas_call(
        kernel,
        out_shape=[jax.ShapeDtypeStruct(o, f32) for o in outs],
        in_specs=places,
        out_specs=[pl.BlockSpec(memory_space=pltpu.SMEM) if o == (1, 1) else vmem for o in outs],
        scratch_shapes=[pltpu.VMEM(s, f32) if isinstance(s, tuple) else s for s in scratch],
        cost_estimate=cost,
        compiler_params=pltpu.CompilerParams(vmem_limit_bytes=20 * 2**20),
    )(place, *args)


MERGE = ((24, LANES), (KC, LANES))
SPREAD = ((KC, LANES), (24, LANES))
DIRECTION = (FIELD, FACE, FACE, PACKED, GRAM)


def swap_near(value, axis):
    return lax.ppermute(value, axis, [(i, i ^ 1) for i in range(lax.axis_size(axis))])


def swap_far(value, axis):
    count = lax.axis_size(axis)
    pairs = [(i, (i + 1) % count) for i in range(1, count, 2)]
    return lax.ppermute(value, axis, pairs + [(b, a) for a, b in pairs])


def swapped(near, far, edge):
    near_face = swap_near(near, "cap")
    far_face = swap_far(far, "cap")
    near_edge = swap_near(edge, "sub")
    far_edge = swap_far(edge, "sub")
    return near_face, far_face, near_edge, far_edge


def shared(copies):
    return lax.all_to_all(copies, ("cap", "sub"), 0, 0)


def exchanged(pay):
    copies = jnp.broadcast_to(pay[None], (GROUPS,) + pay.shape)
    return lax.all_to_all(copies, "grp", 0, 0)


def body(right_side, viscosity, coarse_basis, coarse_factor):
    cap, sub = lax.axis_index("cap"), lax.axis_index("sub")
    caps, subs = lax.axis_size("cap"), lax.axis_size("sub")
    place = jnp.stack([
        cap % 2, (cap != 0) & (cap != caps - 1),
        sub % 2, (sub != 0) & (sub != subs - 1),
        lax.axis_index("grp"),
    ]).astype(jnp.int32)
    basis = coarse_basis[0, 0]
    force = right_side.reshape(SLABS, 8, LANES)
    own_gt = jnp.concatenate(
        [basis.T.reshape(KB // 8, 8, LANES), force, viscosity], axis=0)
    whole = lax.all_gather(own_gt, "grp", axis=0).reshape(GROUPS, -1, LANES)

    copies, near, far, edge = call(
        local_kernel, ((GROUPS, 2, 8, LANES),) + ((8, LANES),) * 3, (),
        place, force, viscosity, basis)
    vhalos = swapped(near, far, edge)
    vhalos, rows, _ = lax.optimization_barrier((vhalos, coarse_factor[0, 0], own_gt))
    factor = gathered = lax.all_gather(rows, "grp", axis=0, tiled=True)
    own = jnp.pad(coarse_factor[0, 0].T, ((0, 0), (0, 2 * LANES - KC // GROUPS)))
    (copies,) = call(
        begin_kernel, ((GROUPS, 5, 8, LANES),), ((KC, LANES), (1, 8, LANES)),
        place, lax.all_to_all(copies, "grp", 0, 0), own, *vhalos)
    coef, v, near, far, edge, gram, vh, fields, gt = call(
        start_kernel,
        (COEF,) + DIRECTION
        + ((4, ROWS, LANES), (SLABS + 4, ROWS, LANES), (GROUPS, KB, LANES)),
        SPREAD + (pltpu.SemaphoreType.DMA(()),),
        place, lax.all_to_all(copies, "grp", 0, 0), whole)
    u = fields
    for picard in range(2):
        us, vs, halos = [u], [v], []
        for k in range(S):
            beyond = swapped(near, far, edge)
            if picard == 0 and k == 0:
                (inside,) = call(inside_kernel, (FIELD,), (), place, v, coef, beside=True)
            else:
                gram, inside = call(
                    functools.partial(beside_kernel, k), (GRAM, FIELD), (),
                    place, span, gram, coef, *vs, *us[::-1][:2], beside=True)
            beyond, gram, inside = lax.optimization_barrier((beyond, gram, inside))
            halos.append(beyond)
            if k + 1 == S:
                (copies,) = call(
                    last_kernel, ((PLACES, 8, LANES),), (FIELD, GRAM),
                    place, span, *beyond, coef, inside, gram, *vs)
                break
            if picard == 0 and k == 0:
                image, copies = call(
                    image_kernel, (FIELD, (PLACES, 8, LANES)), (),
                    place, v, *beyond, coef, gram, inside)
                (pay,) = call(
                    merge_kernel, ((1, 8, LANES),), MERGE, place, image, gt, own, beside=True)
                span, u, v, near, far, edge = call(
                    first_kernel, ((8, LANES), FIELD) + DIRECTION[:4], SPREAD,
                    place, shared(copies), exchanged(pay), image, u, v, coef, gt)
            elif picard == 0:
                u, pay = call(
                    residual_kernel, (FIELD, (1, 8, LANES)), MERGE,
                    place, span, *beyond, coef, inside, gt, own)
                v, near, far, edge = call(
                    direction_kernel, DIRECTION[:4], SPREAD,
                    place, exchanged(pay), coef, gt, u)
            else:
                u, v, near, far, edge = call(
                    functools.partial(step_kernel, k == 0), (FIELD,) + DIRECTION[:4],
                    MERGE + SPREAD, place, span, *beyond, coef, inside, gt, factor)
            us.append(u)
            vs.append(v)
        tiles = shared(copies)
        kept = vs + [h[side] for side in range(4) for h in halos]
        if picard == 0:
            (flow,) = call(combine_kernel, (FLOW,), (), place, span, tiles, fields, vh, *kept)
            coef, u, v, near, far, edge, gram, factor = call(
                restart_kernel, (COEF, FIELD) + DIRECTION + ((KC, KC),),
                MERGE + SPREAD + (pltpu.SemaphoreType.DMA(()),),
                place, flow, fields, gt, factor, far_away=3)
        else:
            result, pressure, good = call(
                end_kernel, ((SLABS, 8, LANES), (4, 8, LANES), (1, 1)),
                ((5, ROWS, LANES),), place, span, tiles, flow, *kept)
    given, good = lax.optimization_barrier(
        ((right_side, viscosity, coarse_basis, gathered), good))
    return lax.cond(
        good[0, 0] > 0.5,
        lambda *_: (result.reshape(3, 4, 8, LANES), pressure),
        stepwise,
        *given)


exact_mode = lax.Precision.HIGHEST


def padded_2(block, sides, width):
    for axis, dim in sides:
        count = lax.axis_size(axis)
        forward = [(i, i + 1) for i in range(count - 1)]
        backward = [(target, source) for source, target in forward]
        low = lax.ppermute(
            lax.slice_in_dim(block, block.shape[dim] - width, None, axis=dim), axis, forward
        )
        high = lax.ppermute(lax.slice_in_dim(block, 0, width, axis=dim), axis, backward)
        block = jnp.concatenate([low, block, high], axis=dim)
    return block


def stencil_faces(padded):
    centre = padded[1:-1, 1:-1, 1:-1]
    faces = (
        0.5 * (centre + padded[2:, 1:-1, 1:-1]),
        0.5 * (centre + padded[:-2, 1:-1, 1:-1]),
        0.5 * (centre + padded[1:-1, 2:, 1:-1]),
        0.5 * (centre + padded[1:-1, :-2, 1:-1]),
        0.5 * (centre + padded[1:-1, 1:-1, 2:]),
        0.5 * (centre + padded[1:-1, 1:-1, :-2]),
    )
    diagonal = 1.0 + faces[0] + faces[1] + faces[2] + faces[3] + faces[4] + faces[5]
    return (faces, diagonal)


def apply_stencil(padded_field, field, faces, diagonal):
    beside = (
        faces[0] * padded_field[:, 2:, 1:-1, 1:-1] + faces[1] * padded_field[:, :-2, 1:-1, 1:-1]
    )
    beside = (
        beside
        + faces[2] * padded_field[:, 1:-1, 2:, 1:-1]
        + faces[3] * padded_field[:, 1:-1, :-2, 1:-1]
    )
    beside = (
        beside
        + faces[4] * padded_field[:, 1:-1, 1:-1, 2:]
        + faces[5] * padded_field[:, 1:-1, 1:-1, :-2]
    )
    return diagonal * field - beside


def divergence_of(padded_field):
    result = 0.5 * (padded_field[0, 2:, 1:-1, 1:-1] - padded_field[0, :-2, 1:-1, 1:-1])
    result = result + 0.5 * (padded_field[1, 1:-1, 2:, 1:-1] - padded_field[1, 1:-1, :-2, 1:-1])
    return result + 0.5 * (padded_field[2, 1:-1, 1:-1, 2:] - padded_field[2, 1:-1, 1:-1, :-2])


def velocity_padded(field):
    return padded_2(field, (("cap", 1), ("grp", 2), ("sub", 3)), 1)


def curvature_sum(direction, image):
    return lax.psum(jnp.sum(direction * image), ("cap", "grp", "sub"))


def norm_sum(residual, precond):
    return lax.psum(jnp.sum(residual * precond), ("cap", "grp", "sub"))


def stepwise(right_side, viscosity, coarse_basis, whole_factor):
    basis_local = coarse_basis[0, 0]

    def precondition(residual, diagonal):
        profile = jnp.mean(residual, axis=(1, 2))
        local = jnp.dot(profile, basis_local, precision=exact_mode)
        merged = lax.psum(local, "grp").reshape(-1)
        solved = jnp.dot(whole_factor, merged, precision=exact_mode)
        spread = jnp.dot(solved.reshape(3, -1), basis_local.T, precision=exact_mode)
        return residual / diagonal + spread[:, None, None, :]

    velocity = jnp.zeros_like(right_side)
    viscous = viscosity
    for picard in range(2):
        if picard > 0:
            viscous = viscosity / (1.0 + 25.0 * jnp.sum(velocity * velocity, axis=0))
        padded_viscous = padded_2(viscous, (("cap", 0), ("grp", 1), ("sub", 2)), 1)
        faces, diagonal = stencil_faces(padded_viscous)

        def operate(field):
            return apply_stencil(velocity_padded(field), field, faces, diagonal)

        residual = right_side - operate(velocity)
        precond = precondition(residual, diagonal)
        norm_now = norm_sum(residual, precond)
        direction = precond
        for krylov_step in range(S):
            image = operate(direction)
            alpha = norm_now / curvature_sum(direction, image)
            velocity = velocity + alpha * direction
            residual = residual - alpha * image
            if krylov_step + 1 < S:
                precond = precondition(residual, diagonal)
                fresh = norm_sum(residual, precond)
                direction = precond + fresh / norm_now * direction
                norm_now = fresh
    pressure = -(viscous / (1.0 + viscous)) * divergence_of(velocity_padded(velocity))
    return (velocity, pressure)


def solution(mesh):
    placed = (
        P(None, "cap", "grp", "sub"),
        P("cap", "grp", "sub"),
        P("cap", "grp", "sub", None),
        P("cap", "sub", "grp", None),
    )
    return jax.shard_map(
        body,
        mesh=mesh,
        in_specs=placed,
        out_specs=(P(None, "cap", "grp", "sub"), P("cap", "grp", "sub")),
        check_vma=False,
    )
```

```python
import functools

import jax
import jax.numpy as jnp
from jax import lax
from jax.experimental import pallas as pl
from jax.experimental.pallas import tpu as pltpu
from jax.sharding import PartitionSpec as P

S = 5
SLABS = 12
ROWS = 64
LANES = 128
GROUPS = 8
KB = 512
KC = 1536
APART = 1e-3
SPAN = 2.6
FIELD = (SLABS, ROWS, LANES)
FACE = (3, ROWS, LANES)
EDGE = (ROWS, LANES)
PACKED = (ROWS // 4, LANES)
GRAM = (24, LANES)
PLACES = 32
FLOW = (27, ROWS, LANES)
COEF = (9, 4, ROWS, LANES)
f32 = jnp.float32


def gram_row(i, j):
    i, j = min(i, j), max(i, j)
    return sum(min(t, S - 1) + 1 for t in range(j)) + i


def lane_ids():
    return lax.broadcasted_iota(jnp.int32, (ROWS, LANES), 1)


def row_ids():
    return lax.broadcasted_iota(jnp.int32, (ROWS, LANES), 0)


def ends_of(halo, i):
    return pltpu.roll(halo, LANES - 1 - 2 * i, 1)


def along_z(w, halo, i, lanes):
    ends = ends_of(halo, i)
    after = jnp.where(lanes == LANES - 1, ends, pltpu.roll(w, LANES - 1, 1))
    before = jnp.where(lanes == 0, ends, pltpu.roll(w, 1, 1))
    return after, before


def flag(place, i):
    return jnp.full((ROWS, LANES), place[i], jnp.int32) == 1


def faces_of(place, near, far):
    odd, inner = flag(place, 0), flag(place, 1)
    far = jnp.where(inner, far, 0.0)
    return jnp.where(odd, near, far), jnp.where(odd, far, near)


def merge_edges(place, near, far):
    far = jnp.where(flag(place, 3), far, 0.0)
    odd = flag(place, 2)
    low, high = jnp.where(odd, near, far), jnp.where(odd, far, near)
    return jnp.where(lane_ids() % 2 == 1, pltpu.roll(low, 1, 1), pltpu.roll(high, LANES - 1, 1))


def edge_of(get, count, lanes):
    edge = jnp.zeros((ROWS, LANES), f32)
    for i in range(count):
        moved = pltpu.roll(get(i), 2 * i + 1, 1)
        edge = jnp.where((lanes == 2 * i) | (lanes == 2 * i + 1), moved, edge)
    return edge


def pack_edge(edge):
    lanes = lax.broadcasted_iota(jnp.int32, PACKED, 1)
    packed = edge[: PACKED[0]]
    for q in range(1, 4):
        part = pltpu.roll(edge[PACKED[0] * q : PACKED[0] * (q + 1)], 32 * q, 1)
        packed = jnp.where(lanes // 32 == q, part, packed)
    return packed


def unpack_edge(packed):
    parts = [packed] + [pltpu.roll(packed, LANES - 32 * q, 1) for q in range(1, 4)]
    return jnp.concatenate(parts, axis=0)


def store_coefs(coef, vis, low, high, halo):
    lanes, rows = lane_ids(), row_ids()
    for x in range(4):
        v = vis(x)
        up = vis(x + 1) if x < 3 else high
        down = vis(x - 1) if x else low
        yp = jnp.where(rows == ROWS - 1, 0.0, pltpu.roll(v, ROWS - 1, 0))
        ym = jnp.where(rows == 0, 0.0, pltpu.roll(v, 1, 0))
        zp, zm = along_z(v, halo, x, lanes)
        faces = [0.5 * (v + n) for n in (up, down, yp, ym, zp, zm)]
        diagonal = 1.0 + faces[0] + faces[1] + faces[2] + faces[3] + faces[4] + faces[5]
        faces[2] = jnp.where(rows == ROWS - 1, 0.0, faces[2])
        faces[3] = jnp.where(rows == 0, 0.0, faces[3])
        first, last = lanes == 0, lanes == LANES - 1
        coef[8, x] = jnp.where(first, faces[5], jnp.where(last, faces[4], 0.0))
        faces[4] = jnp.where(last, 0.0, faces[4])
        faces[5] = jnp.where(first, 0.0, faces[5])
        coef[0, x] = diagonal
        for f in range(6):
            coef[1 + f, x] = faces[f]
        coef[7, x] = 1.0 / diagonal


def stencil_inside(coef, field, write):
    for x in range(4):
        for c in range(3):
            w = field[4 * c + x]
            beside = coef[3, x] * pltpu.roll(w, ROWS - 1, 0) + coef[4, x] * pltpu.roll(w, 1, 0)
            beside = beside + coef[5, x] * pltpu.roll(w, LANES - 1, 1)
            beside = beside + coef[6, x] * pltpu.roll(w, 1, 1)
            if x < 3:
                beside = beside + coef[1, x] * field[4 * c + x + 1]
            if x:
                beside = beside + coef[2, x] * field[4 * c + x - 1]
            write(c, x, coef[0, x] * w - beside)


def stencil_beyond(coef, sides, halo, write):
    for c in range(3):
        low, high = sides(c)
        for x in range(4):
            beside = coef[8, x] * ends_of(halo, 4 * c + x)
            if x == 0:
                beside = beside + coef[2, x] * low
            if x == 3:
                beside = beside + coef[1, x] * high
            write(c, x, beside)


def dot_rows(a, b):
    total = jnp.zeros((8, LANES), f32)
    for s in range(SLABS):
        total = total + jnp.sum((a[s] * b[s]).reshape(8, 8, LANES), axis=0)
    return jnp.sum(total, axis=0, keepdims=True)


def merge(u, gt, prof, mb):
    for c in range(3):
        total = u[4 * c] + u[4 * c + 1] + u[4 * c + 2] + u[4 * c + 3]
        prof[8 * c : 8 * c + 8] = jnp.sum(total.reshape(8, 8, LANES), axis=1) * (1.0 / 32.0)

    @pl.loop(0, KB // 32, unroll=16)
    def _(step):
        at = pl.multiple_of(step * 32, 32)
        totals = [jnp.zeros((32, LANES), f32)] * 3
        for g in range(GROUPS):
            b = gt[g, pl.ds(at, 32), :]
            for c in range(3):
                totals[c] = totals[c] + b * prof[8 * c + g : 8 * c + g + 1, :]
        for c in range(3):
            total = jnp.sum(totals[c], axis=1, keepdims=True)
            mb[pl.ds(c * KB + at, 32), :] = jnp.broadcast_to(total, (32, LANES))


def solve(factor, mb, sb):
    def rows_of(step, totals):
        totals = list(totals)
        for part in range(32):
            at = pl.multiple_of(step * 256 + part * 8, 8)
            m = mb[pl.ds(at, 8), :]
            for q in range(KC // LANES):
                totals[q] = totals[q] + factor[pl.ds(at, 8), LANES * q : LANES * (q + 1)] * m
        return tuple(totals)

    zero = jnp.zeros((8, LANES), f32)
    totals = lax.fori_loop(0, KC // 256, rows_of, (zero,) * (KC // LANES))
    for q in range(KC // LANES):
        row = jnp.sum(totals[q], axis=0, keepdims=True)
        sb[LANES * q : LANES * (q + 1), :] = jnp.broadcast_to(row, (LANES, LANES)).T


def solve_own(own, mb, pay):
    def rows_of(step, totals):
        totals = list(totals)
        for part in range(32):
            at = pl.multiple_of(step * 256 + part * 8, 8)
            m = mb[pl.ds(at, 8), :]
            for q in range(2):
                r = 2 * (part % 4) + q
                totals[r] = totals[r] + own[pl.ds(at, 8), LANES * q : LANES * (q + 1)] * m
        return tuple(totals)

    zero = jnp.zeros((8, LANES), f32)
    t = lax.fori_loop(0, KC // 256, rows_of, (zero,) * 8)
    pay[0] = zero
    for q in range(2):
        total = (t[q] + t[2 + q]) + (t[4 + q] + t[6 + q])
        pay[0, q : q + 1, :] = jnp.sum(total, axis=0, keepdims=True)


def unpack(pays, sb):
    for g in range(GROUPS):
        at = g * (KC // GROUPS)
        left = jnp.broadcast_to(pays[g, 0, 0:1, :], (LANES, LANES)).T
        right = jnp.broadcast_to(pays[g, 0, 1:2, :], (LANES, LANES)).T
        sb[at : at + LANES, :] = left
        sb[at + LANES : at + KC // GROUPS, :] = right[: KC // GROUPS - LANES]


def spread_over(gt, sb, spread):
    def spread_of(step, totals):
        totals = list(totals)
        for part in range(16):
            at = pl.multiple_of(step * 128 + part * 8, 8)
            solved = [sb[pl.ds(c * KB + at, 8), :] for c in range(3)]
            for g in range(GROUPS):
                b = gt[g, pl.ds(at, 8), :]
                for c in range(3):
                    totals[8 * c + g] = totals[8 * c + g] + b * solved[c]
        return tuple(totals)

    zero = jnp.zeros((8, LANES), f32)
    totals = lax.fori_loop(0, KB // 128, spread_of, (zero,) * 24)
    for r in range(24):
        spread[r : r + 1, :] = jnp.sum(totals[r], axis=0, keepdims=True)


def coarse(u, gt, factor, prof, mb, sb, spread):
    merge(u, gt, prof, mb)
    solve(factor, mb, sb)
    spread_over(gt, sb, spread)


def finish_direction(place, u, coef, spread, v, near, far, edge):
    for x in range(4):
        for c in range(3):
            s = 4 * c + x
            wide = jnp.broadcast_to(spread[8 * c : 8 * c + 8, :][:, None, :], (8, 8, LANES))
            v[s] = u[s] * coef[7, x] + wide.reshape(ROWS, LANES)
    if near is not None:
        hand_over(place, v, near, far, edge)


def hand_over(place, v, near, far, edge):
    for c in range(3):
        near[c] = v[4 * c + 3 - 3 * place[0]]
        far[c] = v[4 * c + 3 * place[0]]
    edge[...] = pack_edge(edge_of(lambda i: v[i], SLABS, lane_ids()))


def basis_coefs(span, k):
    half = 0.5 * span
    if k == 0:
        return half, None, 1.0 / half
    return half, 0.5 * half, 2.0 / half


def local_kernel(place, force, viscosity, basis, copies, near, far, edge):
    shares = []
    for c in range(3):
        total = force[4 * c] + force[4 * c + 1] + force[4 * c + 2] + force[4 * c + 3]
        row = jnp.sum(total, axis=0, keepdims=True) * (1.0 / 32.0)
        column = jnp.broadcast_to(row, (LANES, LANES)).T
        for q in range(KB // LANES):
            part = basis[:, LANES * q : LANES * (q + 1)] * column
            shares.append(jnp.sum(part, axis=0, keepdims=True))
    rows = lax.broadcasted_iota(jnp.int32, (8, LANES), 0)
    lanes = lax.broadcasted_iota(jnp.int32, (8, LANES), 1)
    for q in range(2):
        tile = jnp.zeros((8, LANES), f32)
        for r in range(8):
            if 8 * q + r < len(shares):
                tile = jnp.where(rows == r, shares[8 * q + r], tile)
        for g in range(GROUPS):
            copies[g, q] = tile
    near[...] = viscosity[3 - 3 * place[0]]
    far[...] = viscosity[3 * place[0]]
    columns = jnp.zeros((8, LANES), f32)
    for x in range(4):
        moved = pltpu.roll(viscosity[x], 2 * x + 1, 1)
        columns = jnp.where((lanes == 2 * x) | (lanes == 2 * x + 1), moved, columns)
    edge[...] = columns


def begin_kernel(place, pays, own, vnear, vfar, enear, efar, copies, mb, pay):
    for q in range(2):
        total = tree([pays[g, q] for g in range(GROUPS)])
        for r in range(8):
            at = LANES * (8 * q + r)
            if at < KC:
                row = jnp.broadcast_to(total[r : r + 1, :], (LANES, LANES))
                mb[at : at + LANES, :] = row.T
    solve_own(own, mb, pay)
    for g in range(GROUPS):
        copies[g, 0] = pay[0]
        for i, tile in enumerate((vnear, vfar, enear, efar)):
            copies[g, 1 + i] = tile[...]


def start_kernel(place, pays, whole,
                 coef, v, near, far, edge, gram, vh, fields, gt, sb, spread, arrived):
    copy = pltpu.make_async_copy(whole.at[:, pl.ds(0, KB)], gt, arrived)
    copy.start()
    unpack(pays, sb)
    for g in range(GROUPS):
        for s in range(SLABS + 4):
            fields[s, 8 * g : 8 * g + 8, :] = whole[g, KB + 8 * s : KB + 8 * s + 8, :]
        for i in range(4):
            vh[i, 8 * g : 8 * g + 8, :] = pays[g, 1 + i]
    low, high = faces_of(place, vh[0], vh[1])
    halo = merge_edges(place, vh[2], vh[3])
    store_coefs(coef, lambda x: fields[SLABS + x], low, high, halo)
    copy.wait()
    spread_over(gt, sb, spread)
    finish_direction(place, fields, coef, spread, v, near, far, edge)
    gram[...] = jnp.zeros(GRAM, f32)
    gram[0:1, :] = dot_rows(v, fields)


def inside_kernel(place, v, coef, image):
    def write(c, x, value):
        image[4 * c + x] = value

    stencil_inside(coef, v, write)


def image_kernel(place, v, near, far, edge_near, edge_far, coef, gram, inside, image, copies):
    halo = merge_edges(place, unpack_edge(edge_near[...]), unpack_edge(edge_far[...]))

    def write(c, x, value):
        image[4 * c + x] = inside[4 * c + x] - value

    stencil_beyond(coef, lambda c: faces_of(place, near[c], far[c]), halo, write)
    rows = lax.broadcasted_iota(jnp.int32, (8, LANES), 0)
    tile = jnp.where(rows == 0, gram[0:1, :], jnp.where(rows == 1, dot_rows(v, image), 0.0))
    for i in range(PLACES):
        copies[i] = tile


def merge_kernel(place, image, gt, own, pay, prof, mb):
    merge(image, gt, prof, mb)
    solve_own(own, mb, pay)


def first_kernel(place, tiles, pays, image, u0, v0, coef, gt,
                 span, u, v, near, far, edge, sb, spread):
    sums = jnp.sum(tree([tiles[i] for i in range(PLACES)]), axis=1, keepdims=True)
    width = SPAN * sums[1:2, :] / sums[0:1, :]
    span[...] = jnp.broadcast_to(width, (8, LANES))
    shift, _, scale = basis_coefs(width, 0)
    unpack(pays, sb)
    spread_over(gt, sb, spread)
    finish_direction(place, image, coef, spread, v, None, None, None)
    for s in range(SLABS):
        u[s] = (image[s] - shift * u0[s]) * scale
        v[s] = (v[s] - shift * v0[s]) * scale
    hand_over(place, v, near, far, edge)


def residual_kernel(place, span, hnear, hfar, enear, efar, coef, inside, gt, own,
                    u, pay, prof, mb):
    next_residual(place, False, span, hnear, hfar, enear, efar, coef, inside, u)
    merge(u, gt, prof, mb)
    solve_own(own, mb, pay)


def direction_kernel(place, pays, coef, gt, u, v, near, far, edge, sb, spread):
    unpack(pays, sb)
    spread_over(gt, sb, spread)
    finish_direction(place, u, coef, spread, v, near, far, edge)


def beside_kernel(k, place, span, gram_in, coef, *refs):
    refs, (gram, inside) = refs[:-2], refs[-2:]
    vs, us = refs[: k + 1], refs[k + 1 :]
    uk = us[0]
    if k:
        store_dots(gram, gram_in, vs[:-1], uk, vs[-1])
    else:
        gram[...] = gram_in[...]
    shift, back, scale = basis_coefs(span[0:1, 0:1], k)

    def write(c, x, value):
        s = 4 * c + x
        value = value - shift * uk[s]
        if k:
            value = value - back * us[1][s]
        inside[s] = value * scale

    stencil_inside(coef, vs[-1], write)


def tree(parts):
    while len(parts) > 1:
        parts = [parts[i] + parts[i + 1] for i in range(0, len(parts), 2)]
    return parts[0]


def pack_sums(gram, copies):
    sums = jnp.sum(gram[...], axis=1, keepdims=True)
    lanes = lax.broadcasted_iota(jnp.int32, (8, LANES), 1)
    tile = jnp.zeros((8, LANES), f32)
    for q in range(GRAM[0] // 8):
        tile = jnp.where(lanes == q, sums[8 * q : 8 * q + 8], tile)
    for i in range(PLACES):
        copies[i] = tile


def store_dots(gram, gram_in, vs, u, v=None):
    gram[...] = gram_in[...]
    vs = list(vs) + ([] if v is None else [v])
    totals = [jnp.zeros((8, LANES), f32)] * len(vs)
    for s in range(SLABS):
        us = u[s]
        for i, vi in enumerate(vs):
            totals[i] = totals[i] + jnp.sum((vi[s] * us).reshape(8, 8, LANES), axis=0)
    level = len(vs) - (0 if v is None else 1)
    for i, total in enumerate(totals):
        r = gram_row(i, level)
        gram[r : r + 1, :] = jnp.sum(total, axis=0, keepdims=True)


def next_residual(place, first, span, near, far, edge_near, edge_far, coef, inside, u):
    halo = merge_edges(place, unpack_edge(edge_near[...]), unpack_edge(edge_far[...]))
    scale = basis_coefs(span[0:1, 0:1], 0 if first else 1)[2]

    def write(c, x, value):
        u[4 * c + x] = inside[4 * c + x] - value * scale

    stencil_beyond(coef, lambda c: faces_of(place, near[c], far[c]), halo, write)


def step_kernel(first, place, span, hnear, hfar, enear, efar, coef, inside, gt, factor,
                u, v, near, far, edge, prof, mb, sb, spread):
    next_residual(place, first, span, hnear, hfar, enear, efar, coef, inside, u)
    coarse(u, gt, factor, prof, mb, sb, spread)
    finish_direction(place, u, coef, spread, v, near, far, edge)


def last_kernel(place, span, hnear, hfar, enear, efar, coef, inside, gram_in,
                v0, v1, v2, v3, v4, copies, u, gram):
    vs = (v0, v1, v2, v3, v4)
    next_residual(place, False, span, hnear, hfar, enear, efar, coef, inside, u)
    store_dots(gram, gram_in, vs, u)
    pack_sums(gram, copies)


def well_posed(n):
    rows = []
    good = None
    for j in range(S):
        row = []
        pivot = n[j][j]
        for i in range(j):
            value = n[i][j]
            for t in range(i):
                value = value - rows[i][t] * row[t]
            row.append(value)
            pivot = pivot - value * value / rows[i][i]
        row.append(pivot)
        apart = jnp.where(pivot > APART * n[j][j], 1.0, 0.0)
        good = apart if good is None else good * apart
        rows.append([value / rows[i][i] for i, value in enumerate(row[:j])] + [pivot])
    return good


def krylov_weights(span, sums):
    def product(i, j):
        r = gram_row(i, j)
        return sums[r // 8][r % 8 : r % 8 + 1, :]

    n = [[product(i, j) for j in range(S + 1)] for i in range(S)]
    half = 0.5 * span
    quarter = 0.5 * half

    def operate(p):
        out = [None] * (S + 1)

        def put(i, value):
            out[i] = value if out[i] is None else out[i] + value

        for j, w in enumerate(p):
            put(j, half * w)
            put(j + 1, (half if j == 0 else quarter) * w)
            if j:
                put(j - 1, quarter * w)
        return out[: len(p) + 1]

    def pair(a, b):
        total = None
        for i, ai in enumerate(a):
            part = None
            for j, bj in enumerate(b):
                term = n[i][j] * bj
                part = term if part is None else part + term
            total = ai * part if total is None else total + ai * part
        return total

    one = jnp.ones_like(span)
    r, p = [one], [one]
    x = []
    norm = n[0][0]
    for k in range(S):
        image = operate(p)
        alpha = norm / pair(p, image)
        for j, w in enumerate(p):
            if j < len(x):
                x[j] = x[j] + alpha * w
            else:
                x.append(alpha * w)
        r = [(r[j] - alpha * w) if j < len(r) else -(alpha * w) for j, w in enumerate(image)]
        if k + 1 < S:
            fresh = pair(r, r)
            beta = fresh / norm
            p = [r[j] + beta * p[j] if j < len(p) else r[j] for j in range(len(r))]
            norm = fresh
    return x, well_posed(n)


def weights_of(span, tiles):
    total = tree([tiles[i] for i in range(PLACES)])
    columns = [total[:, q : q + 1] for q in range(GRAM[0] // 8)]
    return krylov_weights(span[0:1, 0:1], columns)


def combine(x, parts, before=None):
    total = x[0] * parts[0]
    for j in range(1, S):
        total = total + x[j] * parts[j]
    return total if before is None else before + total


def combine_kernel(place, span, tiles, fields, vh,
                   v0, v1, v2, v3, v4, n0, n1, n2, n3, n4, f0, f1, f2, f3, f4,
                   en0, en1, en2, en3, en4, ef0, ef1, ef2, ef3, ef4,
                   flow):
    x, good = weights_of(span, tiles)
    vs = (v0, v1, v2, v3, v4)
    ns, fs = (n0, n1, n2, n3, n4), (f0, f1, f2, f3, f4)
    ens, efs = (en0, en1, en2, en3, en4), (ef0, ef1, ef2, ef3, ef4)
    for s in range(SLABS):
        flow[s] = combine(x, [t[s] for t in vs])
    for c in range(3):
        flow[12 + c], flow[15 + c] = faces_of(
            place, combine(x, [t[c] for t in ns]), combine(x, [t[c] for t in fs]))
    halo = merge_edges(
        place, unpack_edge(combine(x, [t[...] for t in ens])),
        unpack_edge(combine(x, [t[...] for t in efs])))

    def thinned(viscosity, a, b, c):
        return viscosity / (1.0 + 25.0 * (a * a + b * b + c * c))

    for i in range(4):
        flow[18 + i] = thinned(fields[SLABS + i], flow[i], flow[4 + i], flow[8 + i])
    vis_low, vis_high = faces_of(place, vh[0], vh[1])
    flow[22] = thinned(vis_low, flow[12], flow[13], flow[14])
    flow[23] = thinned(vis_high, flow[15], flow[16], flow[17])
    second = pltpu.roll(halo, LANES - 8, 1)
    third = pltpu.roll(halo, LANES - 16, 1)
    flow[24] = thinned(merge_edges(place, vh[2], vh[3]), halo, second, third)
    flow[25] = halo
    flow[26] = jnp.broadcast_to(good, EDGE)


def restart_kernel(place, flow, fields, gt, factor_in,
                   coef, u, v, near, far, edge, gram, factor, prof, mb, sb, spread, arrived):
    fetch = pltpu.make_async_copy(factor_in, factor, arrived)
    fetch.start()
    store_coefs(coef, lambda i: flow[18 + i], flow[22], flow[23], flow[24])

    def write(c, i, value):
        u[4 * c + i] = fields[4 * c + i] - value

    stencil_inside(coef, flow, write)

    def write_beyond(c, i, value):
        u[4 * c + i] = u[4 * c + i] + value

    stencil_beyond(coef, lambda c: (flow[12 + c], flow[15 + c]), flow[25], write_beyond)
    merge(u, gt, prof, mb)
    fetch.wait()
    solve(factor, mb, sb)
    spread_over(gt, sb, spread)
    finish_direction(place, u, coef, spread, v, near, far, edge)
    gram[...] = jnp.zeros(GRAM, f32)
    gram[0:1, :] = dot_rows(v, u)


def end_kernel(place, span, tiles, flow,
               v0, v1, v2, v3, v4, n0, n1, n2, n3, n4, f0, f1, f2, f3, f4,
               en0, en1, en2, en3, en4, ef0, ef1, ef2, ef3, ef4,
               velocity, pressure, good, cross):
    lanes = lax.broadcasted_iota(jnp.int32, (8, LANES), 1)
    rows = row_ids()
    x, good_now = weights_of(span, tiles)
    good[0, 0] = jnp.min(good_now * flow[26][0:1, 0:1])
    vs = (v0, v1, v2, v3, v4)
    ns, fs = (n0, n1, n2, n3, n4), (f0, f1, f2, f3, f4)
    ens, efs = (en0, en1, en2, en3, en4), (ef0, ef1, ef2, ef3, ef4)
    own = pl.ds(pl.multiple_of(place[4] * 8, 8), 8)
    for s in range(SLABS):
        velocity[s] = combine(x, [t[s, own, :] for t in vs], flow[s, own, :])
    near = combine(x, [t[0, own, :] for t in ns])
    far = combine(x, [t[0, own, :] for t in fs])
    odd = jnp.full((8, LANES), place[0], jnp.int32) == 1
    far = jnp.where(jnp.full((8, LANES), place[1], jnp.int32) == 1, far, 0.0)
    low = flow[12, own, :] + jnp.where(odd, near, far)
    high = flow[15, own, :] + jnp.where(odd, far, near)
    cross[0] = flow[25] + merge_edges(
        place, unpack_edge(combine(x, [t[...] for t in ens])),
        unpack_edge(combine(x, [t[...] for t in efs])))
    halo = cross[0, own, :]
    for i in range(4):
        vis = flow[18 + i, own, :]
        up = velocity[i + 1] if i < 3 else high
        down = velocity[i - 1] if i else low
        w = combine(x, [t[4 + i] for t in vs], flow[4 + i])
        yp = jnp.where(rows == ROWS - 1, 0.0, pltpu.roll(w, ROWS - 1, 0))
        ym = jnp.where(rows == 0, 0.0, pltpu.roll(w, 1, 0))
        cross[1 + i] = yp - ym
        zp, zm = along_z(velocity[8 + i], halo, 8 + i, lanes)
        divergence = 0.5 * (up - down) + 0.5 * cross[1 + i, own, :] + 0.5 * (zp - zm)
        pressure[i] = -(vis / (1.0 + vis)) * divergence


def call(kernel, outs, scratch, place, *args, far_away=None, beside=False):
    vmem = pl.BlockSpec(memory_space=pltpu.VMEM)
    places = [pl.BlockSpec(memory_space=pltpu.SMEM)] + [vmem] * len(args)
    if far_away is not None:
        places[1 + far_away] = pl.BlockSpec(memory_space=pl.ANY)
    cost = None
    if beside:
        size = sum(a.size for a in args)
        cost = pl.CostEstimate(flops=2 * size, bytes_accessed=4 * size, transcendentals=0)
    return pl.pallas_call(
        kernel,
        out_shape=[jax.ShapeDtypeStruct(o, f32) for o in outs],
        in_specs=places,
        out_specs=[pl.BlockSpec(memory_space=pltpu.SMEM) if o == (1, 1) else vmem for o in outs],
        scratch_shapes=[pltpu.VMEM(s, f32) if isinstance(s, tuple) else s for s in scratch],
        cost_estimate=cost,
        compiler_params=pltpu.CompilerParams(vmem_limit_bytes=20 * 2**20),
    )(place, *args)


MERGE = ((24, LANES), (KC, LANES))
SPREAD = ((KC, LANES), (24, LANES))
DIRECTION = (FIELD, FACE, FACE, PACKED, GRAM)


def swap_near(value, axis):
    return lax.ppermute(value, axis, [(i, i ^ 1) for i in range(lax.axis_size(axis))])


def swap_far(value, axis):
    count = lax.axis_size(axis)
    pairs = [(i, (i + 1) % count) for i in range(1, count, 2)]
    return lax.ppermute(value, axis, pairs + [(b, a) for a, b in pairs])


def swapped(near, far, edge):
    near_face = swap_near(near, "cap")
    far_face = swap_far(far, "cap")
    near_edge = swap_near(edge, "sub")
    far_edge = swap_far(edge, "sub")
    return near_face, far_face, near_edge, far_edge


def shared(copies):
    return lax.all_to_all(copies, ("cap", "sub"), 0, 0)


def exchanged(pay):
    copies = jnp.broadcast_to(pay[None], (GROUPS,) + pay.shape)
    return lax.all_to_all(copies, "grp", 0, 0)


def body(right_side, viscosity, coarse_basis, coarse_factor):
    cap, sub = lax.axis_index("cap"), lax.axis_index("sub")
    caps, subs = lax.axis_size("cap"), lax.axis_size("sub")
    place = jnp.stack([
        cap % 2, (cap != 0) & (cap != caps - 1),
        sub % 2, (sub != 0) & (sub != subs - 1),
        lax.axis_index("grp"),
    ]).astype(jnp.int32)
    basis = coarse_basis[0, 0]
    force = right_side.reshape(SLABS, 8, LANES)
    own_gt = jnp.concatenate(
        [basis.T.reshape(KB // 8, 8, LANES), force, viscosity], axis=0)
    whole = lax.all_gather(own_gt, "grp", axis=0).reshape(GROUPS, -1, LANES)

    copies, near, far, edge = call(
        local_kernel, ((GROUPS, 2, 8, LANES),) + ((8, LANES),) * 3, (),
        place, force, viscosity, basis)
    vhalos = swapped(near, far, edge)
    vhalos, rows, _ = lax.optimization_barrier((vhalos, coarse_factor[0, 0], own_gt))
    factor = gathered = lax.all_gather(rows, "grp", axis=0, tiled=True)
    own = jnp.pad(coarse_factor[0, 0].T, ((0, 0), (0, 2 * LANES - KC // GROUPS)))
    (copies,) = call(
        begin_kernel, ((GROUPS, 5, 8, LANES),), ((KC, LANES), (1, 8, LANES)),
        place, lax.all_to_all(copies, "grp", 0, 0), own, *vhalos)
    coef, v, near, far, edge, gram, vh, fields, gt = call(
        start_kernel,
        (COEF,) + DIRECTION
        + ((4, ROWS, LANES), (SLABS + 4, ROWS, LANES), (GROUPS, KB, LANES)),
        SPREAD + (pltpu.SemaphoreType.DMA(()),),
        place, lax.all_to_all(copies, "grp", 0, 0), whole)
    u = fields
    for picard in range(2):
        us, vs, halos = [u], [v], []
        for k in range(S):
            beyond = swapped(near, far, edge)
            if picard == 0 and k == 0:
                (inside,) = call(inside_kernel, (FIELD,), (), place, v, coef, beside=True)
            else:
                gram, inside = call(
                    functools.partial(beside_kernel, k), (GRAM, FIELD), (),
                    place, span, gram, coef, *vs, *us[::-1][:2], beside=True)
            beyond, gram, inside = lax.optimization_barrier((beyond, gram, inside))
            halos.append(beyond)
            if k + 1 == S:
                (copies,) = call(
                    last_kernel, ((PLACES, 8, LANES),), (FIELD, GRAM),
                    place, span, *beyond, coef, inside, gram, *vs)
                break
            if picard == 0 and k == 0:
                image, copies = call(
                    image_kernel, (FIELD, (PLACES, 8, LANES)), (),
                    place, v, *beyond, coef, gram, inside)
                (pay,) = call(
                    merge_kernel, ((1, 8, LANES),), MERGE, place, image, gt, own, beside=True)
                span, u, v, near, far, edge = call(
                    first_kernel, ((8, LANES), FIELD) + DIRECTION[:4], SPREAD,
                    place, shared(copies), exchanged(pay), image, u, v, coef, gt)
            elif picard == 0:
                u, pay = call(
                    residual_kernel, (FIELD, (1, 8, LANES)), MERGE,
                    place, span, *beyond, coef, inside, gt, own)
                v, near, far, edge = call(
                    direction_kernel, DIRECTION[:4], SPREAD,
                    place, exchanged(pay), coef, gt, u)
            else:
                u, v, near, far, edge = call(
                    functools.partial(step_kernel, k == 0), (FIELD,) + DIRECTION[:4],
                    MERGE + SPREAD, place, span, *beyond, coef, inside, gt, factor)
            us.append(u)
            vs.append(v)
        tiles = shared(copies)
        kept = vs + [h[side] for side in range(4) for h in halos]
        if picard == 0:
            (flow,) = call(combine_kernel, (FLOW,), (), place, span, tiles, fields, vh, *kept)
            coef, u, v, near, far, edge, gram, factor = call(
                restart_kernel, (COEF, FIELD) + DIRECTION + ((KC, KC),),
                MERGE + SPREAD + (pltpu.SemaphoreType.DMA(()),),
                place, flow, fields, gt, factor, far_away=3)
        else:
            result, pressure, good = call(
                end_kernel, ((SLABS, 8, LANES), (4, 8, LANES), (1, 1)),
                ((5, ROWS, LANES),), place, span, tiles, flow, *kept)
    given, good = lax.optimization_barrier(
        ((right_side, viscosity, coarse_basis, gathered), good))
    return lax.cond(
        good[0, 0] > 0.5,
        lambda *_: (result.reshape(3, 4, 8, LANES), pressure),
        stepwise,
        *given)


exact_mode = lax.Precision.HIGHEST


def padded_2(block, sides, width):
    for axis, dim in sides:
        count = lax.axis_size(axis)
        forward = [(i, i + 1) for i in range(count - 1)]
        backward = [(target, source) for source, target in forward]
        low = lax.ppermute(
            lax.slice_in_dim(block, block.shape[dim] - width, None, axis=dim), axis, forward
        )
        high = lax.ppermute(lax.slice_in_dim(block, 0, width, axis=dim), axis, backward)
        block = jnp.concatenate([low, block, high], axis=dim)
    return block


def stencil_faces(padded):
    centre = padded[1:-1, 1:-1, 1:-1]
    faces = (
        0.5 * (centre + padded[2:, 1:-1, 1:-1]),
        0.5 * (centre + padded[:-2, 1:-1, 1:-1]),
        0.5 * (centre + padded[1:-1, 2:, 1:-1]),
        0.5 * (centre + padded[1:-1, :-2, 1:-1]),
        0.5 * (centre + padded[1:-1, 1:-1, 2:]),
        0.5 * (centre + padded[1:-1, 1:-1, :-2]),
    )
    diagonal = 1.0 + faces[0] + faces[1] + faces[2] + faces[3] + faces[4] + faces[5]
    return (faces, diagonal)


def apply_stencil(padded_field, field, faces, diagonal):
    beside = (
        faces[0] * padded_field[:, 2:, 1:-1, 1:-1] + faces[1] * padded_field[:, :-2, 1:-1, 1:-1]
    )
    beside = (
        beside
        + faces[2] * padded_field[:, 1:-1, 2:, 1:-1]
        + faces[3] * padded_field[:, 1:-1, :-2, 1:-1]
    )
    beside = (
        beside
        + faces[4] * padded_field[:, 1:-1, 1:-1, 2:]
        + faces[5] * padded_field[:, 1:-1, 1:-1, :-2]
    )
    return diagonal * field - beside


def divergence_of(padded_field):
    result = 0.5 * (padded_field[0, 2:, 1:-1, 1:-1] - padded_field[0, :-2, 1:-1, 1:-1])
    result = result + 0.5 * (padded_field[1, 1:-1, 2:, 1:-1] - padded_field[1, 1:-1, :-2, 1:-1])
    return result + 0.5 * (padded_field[2, 1:-1, 1:-1, 2:] - padded_field[2, 1:-1, 1:-1, :-2])


def velocity_padded(field):
    return padded_2(field, (("cap", 1), ("grp", 2), ("sub", 3)), 1)


def curvature_sum(direction, image):
    return lax.psum(jnp.sum(direction * image), ("cap", "grp", "sub"))


def norm_sum(residual, precond):
    return lax.psum(jnp.sum(residual * precond), ("cap", "grp", "sub"))


def stepwise(right_side, viscosity, coarse_basis, whole_factor):
    basis_local = coarse_basis[0, 0]

    def precondition(residual, diagonal):
        profile = jnp.mean(residual, axis=(1, 2))
        local = jnp.dot(profile, basis_local, precision=exact_mode)
        merged = lax.psum(local, "grp").reshape(-1)
        solved = jnp.dot(whole_factor, merged, precision=exact_mode)
        spread = jnp.dot(solved.reshape(3, -1), basis_local.T, precision=exact_mode)
        return residual / diagonal + spread[:, None, None, :]

    velocity = jnp.zeros_like(right_side)
    viscous = viscosity
    for picard in range(2):
        if picard > 0:
            viscous = viscosity / (1.0 + 25.0 * jnp.sum(velocity * velocity, axis=0))
        padded_viscous = padded_2(viscous, (("cap", 0), ("grp", 1), ("sub", 2)), 1)
        faces, diagonal = stencil_faces(padded_viscous)

        def operate(field):
            return apply_stencil(velocity_padded(field), field, faces, diagonal)

        residual = right_side - operate(velocity)
        precond = precondition(residual, diagonal)
        norm_now = norm_sum(residual, precond)
        direction = precond
        for krylov_step in range(S):
            image = operate(direction)
            alpha = norm_now / curvature_sum(direction, image)
            velocity = velocity + alpha * direction
            residual = residual - alpha * image
            if krylov_step + 1 < S:
                precond = precondition(residual, diagonal)
                fresh = norm_sum(residual, precond)
                direction = precond + fresh / norm_now * direction
                norm_now = fresh
    pressure = -(viscous / (1.0 + viscous)) * divergence_of(velocity_padded(velocity))
    return (velocity, pressure)


def solution(mesh):
    placed = (
        P(None, "cap", "grp", "sub"),
        P("cap", "grp", "sub"),
        P("cap", "grp", "sub", None),
        P("cap", "sub", "grp", None),
    )
    return jax.shard_map(
        body,
        mesh=mesh,
        in_specs=placed,
        out_specs=(P(None, "cap", "grp", "sub"), P("cap", "grp", "sub")),
        check_vma=False,
    )
```
